32 devices in a mesh: batch: 2 (over x), wide: 16 (over z, y, core).
Axes of the slice: x: 2, y: 2, z: 4, core: 2. Of those that a mesh axis runs over, the one named last changes fastest.
Arguments:
- prefix_in: bfloat16 [32, 1024, 2048], P(('batch', 'wide')), may hold values from -6 to 6
- action_in: bfloat16 [32, 256, 1024], P(('batch', 'wide')), may hold values from -6 to 6
- target: float32 [32, 256, 32], P(('batch', 'wide')), may hold values from -20 to 20
- valid_mask: int32 [32, 256, 32], P(('batch', 'wide')), may hold values from 0 to 1, as said below
- prefix_ids: int32 [32, 1024], P(('batch', 'wide')), may hold values from 0 to 1, never falling along the last dimension, each value on 1 to 1023 neighbouring positions
- action_ids: int32 [32, 256], P(('batch', 'wide')), may hold values from 0 to 1, never falling along the last dimension, each value on 1 to 255 neighbouring positions
- action_blocks: int32 [32, 256], P(('batch', 'wide')), may hold values 0 or 1
- learning_rate: float32 [1], replicated, may hold values from 1.4481547 to 2.8963094
- prefix_weight: float32 [2048, 512], P('wide'), may hold values from -0.125 to 0.125
- attention_weight: float32 [1024, 4608], P('wide'), may hold values from -0.1875 to 0.1875
- feedforward_weight: float32 [4096, 3, 1024], P('wide'), may hold values from -0.1875 to 0.1875
- prefix_gains: float32 [1, 2048], replicated, may hold values from -0.0625 to 0.0625
- action_gains: float32 [3, 1024], replicated, may hold values from -0.0625 to 0.0625
- readout_weight: float32 [1024, 32], replicated, may hold values from -0.1875 to 0.1875
- prefix_weight_moment: float32 [2048, 512], P('wide'), may hold values from -0.00390625 to 0.00390625
- attention_weight_moment: float32 [1024, 4608], P('wide'), may hold values from -0.00390625 to 0.00390625
- feedforward_weight_moment: float32 [4096, 3, 1024], P('wide'), may hold values from -0.00390625 to 0.00390625
- prefix_gains_moment: float32 [1, 2048], replicated, may hold values from -0.00390625 to 0.00390625
- action_gains_moment: float32 [3, 1024], replicated, may hold values from -0.00390625 to 0.00390625
- readout_weight_moment: float32 [1024, 32], replicated, may hold values from -0.00390625 to 0.00390625
- prefix_weight_average: float32 [2048, 512], P('wide'), may hold values from -0.125 to 0.125
- attention_weight_average: float32 [1024, 4608], P('wide'), may hold values from -0.1875 to 0.1875
- feedforward_weight_average: float32 [4096, 3, 1024], P('wide'), may hold values from -0.1875 to 0.1875
- prefix_gains_average: float32 [1, 2048], replicated, may hold values from -0.0625 to 0.0625
- action_gains_average: float32 [3, 1024], replicated, may hold values from -0.0625 to 0.0625
- readout_weight_average: float32 [1024, 32], replicated, may hold values from -0.1875 to 0.1875
Outputs:
- loss: float32 [], replicated
- prefix_weight_next: float32 [2048, 512], P('wide')
- attention_weight_next: float32 [1024, 4608], P('wide')
- feedforward_weight_next: float32 [4096, 3, 1024], P('wide')
- prefix_gains_next: float32 [1, 2048], replicated
- action_gains_next: float32 [3, 1024], replicated
- readout_weight_next: float32 [1024, 32], replicated
- prefix_weight_moment_next: float32 [2048, 512], P('wide')
- attention_weight_moment_next: float32 [1024, 4608], P('wide')
- feedforward_weight_moment_next: float32 [4096, 3, 1024], P('wide')
- prefix_gains_moment_next: float32 [1, 2048], replicated
- action_gains_moment_next: float32 [3, 1024], replicated
- readout_weight_moment_next: float32 [1024, 32], replicated
- prefix_weight_average_next: float32 [2048, 512], P('wide')
- attention_weight_average_next: float32 [1024, 4608], P('wide')
- feedforward_weight_average_next: float32 [4096, 3, 1024], P('wide')
- prefix_gains_average_next: float32 [1, 2048], replicated
- action_gains_average_next: float32 [3, 1024], replicated
- readout_weight_average_next: float32 [1024, 32], replicated
The draws below stay inside these ranges and needn't reach their ends.
Inputs may be any that keep to these rules, and one draw needn't show every extreme that they name: prefix_ids: non-decreasing along each row; every episode number appears in both prefix_ids and action_ids of a row. action_ids: non-decreasing along each row; every episode number appears in both prefix_ids and action_ids of a row. valid_mask: 1 at every row's first action token.
All inputs are finite; a program needn't handle non-finite values. No bound on the sum of `action_blocks` on one device may be relied on, other than what follows from the above.
Results may differ from the reference program's by a relative error of at most 0.0058.
Values may be sent and summed in bfloat16 or wider, within the bound.
No kernel may reach another device: no remote copies, remote signals or barrier semaphores. Data moves between devices by JAX's collectives and lax.ppermute only.
A program may use at most 192 MiB of HBM per device.

```python
import math
import jax
import jax.numpy as jnp
import numpy as np
from jax import lax

D_P = 2048
D_A = 1024
HEADS = 8
HEAD_DIM = 256
FF_A = 4096
ACT = 32
TP_DEV = 1024
TA_DEV = 256
EPIS = 2
ROWS = 32


def draw_target(key, part):
    shape = (ROWS, TA_DEV, ACT)
    rows_index = lax.broadcasted_iota(jnp.int32, shape, 0).astype(jnp.float32)
    rising = jnp.exp(jnp.log(3.0) * rows_index / max(ROWS - 1, 1))
    values = jax.random.normal(key, shape, jnp.float32)
    return values * rising


def draw_valid_mask(key, part):
    shape = (ROWS, TA_DEV, ACT)
    rows_index = lax.broadcasted_iota(jnp.int32, shape, 0)
    limits = 300 + 600 * rows_index // max(ROWS - 1, 1)
    picks = jax.random.randint(key, shape, 0, 1000)
    leading = lax.broadcasted_iota(jnp.int32, shape, 1) == 0
    return jnp.where(leading | (picks < limits), 1, 0).astype(jnp.int32)


def touch_ends(entries, own_key, low, largest):
    extent = entries.shape
    place = [jax.random.randint(jax.random.fold_in(own_key, axis), (), 0, extent[axis]) for axis in range(len(extent))]
    entries = entries.at[tuple(place)].set(low)
    longest = extent.index(max(extent))
    place[longest] = (place[longest] + 1) % extent[longest]
    return entries.at[tuple(place)].set(largest)


def steps_of(stream_key, shape, pieces, low, largest):
    level, own = 1.0, jax.random.fold_in(stream_key, 6)
    for dim, shards_of in pieces:
        steps = jnp.exp(jax.random.uniform(jax.random.fold_in(own, dim), (shards_of,), jnp.float32, low / len(pieces), largest / len(pieces)))
        level = level * jnp.repeat(steps, shape[dim] // shards_of).reshape([-1 if axis == dim else 1 for axis in range(len(shape))])
    return level


def split_up(amount, total, bound, lean):
    loads = [(1 << 20) // math.isqrt(rank ** lean) + 1 for rank in range(2, amount + 1)]
    rest, holding = total - bound - (amount - 1), [1] * (amount - 1)
    while rest > 0:
        free = [i for i in range(amount - 1) if holding[i] < bound]
        mass, remaining = sum([loads[i] for i in free]), rest
        for i in free:
            extra = min(bound - holding[i], max(1, remaining * loads[i] // mass), rest)
            holding[i] = holding[i] + extra
            rest = rest - extra
    return np.array([bound] + holding)


def uneven(key, number_of, total, most, slope):
    if number_of == 2:
        one = jax.random.randint(key, (), max(1, total - most), min(most, total - 1) + 1)
        return jnp.stack([one, total - one])
    tallies = jnp.asarray(split_up(number_of, total, most, slope), jnp.int32)
    pairs = (number_of - 1) // 2
    giver, receiver = tallies[1:1 + 2 * pairs:2], tallies[2:2 + 2 * pairs:2]
    room = jnp.minimum(giver - 1, most - receiver)
    moved = jax.random.randint(jax.random.fold_in(key, 1), (pairs,), 0, 1 << 20) % (room + 1)
    tallies = tallies.at[1:1 + 2 * pairs:2].set(giver - moved).at[2:2 + 2 * pairs:2].set(receiver + moved)
    return tallies[jax.random.permutation(jax.random.fold_in(key, 2), number_of)]


def gaussian(key, extent, scale, limit, shards=(), held_as=jnp.bfloat16):
    array = scale * jax.random.normal(key, extent, jnp.float32)
    if shards:
        array = array * steps_of(key, extent, shards, -0.22, 0.18)
    return jnp.clip(array, -limit, limit).astype(held_as)


def setup_inputs(seed: int = 0) -> dict:
    splits = jax.random.split(jax.random.key(seed), 27)
    prefix_in = gaussian(splits[0], (ROWS, TP_DEV, D_P), 1.0, 6.0, ((0, 32),))
    action_in = gaussian(splits[1], (ROWS, TA_DEV, D_A), 1.0, 6.0, ((0, 32),))
    target = draw_target(jax.random.fold_in(splits[26], 71), 0)
    valid_mask = draw_valid_mask(jax.random.fold_in(splits[26], 71), 0)
    prefix_ids = jax.vmap(lambda own: jnp.searchsorted(jnp.cumsum(uneven(own, EPIS, TP_DEV, 2 * (TP_DEV // EPIS) - 1, 1)), jnp.arange(TP_DEV), side="right"))(jax.random.split(splits[4], ROWS)).reshape((ROWS, TP_DEV)).astype(jnp.int32)
    action_ids = jax.vmap(lambda own: jnp.searchsorted(jnp.cumsum(uneven(own, EPIS, TA_DEV, 2 * (TA_DEV // EPIS) - 1, 1)), jnp.arange(TA_DEV), side="right"))(jax.random.split(splits[5], ROWS)).reshape((ROWS, TA_DEV)).astype(jnp.int32)
    action_blocks = touch_ends((jax.random.randint(splits[6], (ROWS, TA_DEV), 0, 8) < 1).astype(jnp.int32), jax.random.fold_in(splits[6], 1), 0, 1)
    learning_rate = jnp.clip(jnp.exp(jax.random.uniform(splits[7], (1,), jnp.float32, math.log(1.4481547), math.log(2.8963094))), 1.4481547, 2.8963094)
    prefix_weight = gaussian(splits[8], (D_P, 2 * HEAD_DIM), D_P ** -0.5, 0.125, ((0, 16),), jnp.float32)
    attention_weight = gaussian(splits[9], (D_A, 2 * HEADS * HEAD_DIM + 2 * HEAD_DIM), D_A ** -0.5, 0.1875, ((0, 16),), jnp.float32)
    feedforward_weight = gaussian(splits[10], (FF_A, 3, D_A), D_A ** -0.5, 0.1875, ((0, 16),), jnp.float32)
    prefix_gains = gaussian(splits[11], (1, D_P), 0.01, 0.0625, (), jnp.float32)
    action_gains = gaussian(splits[12], (3, D_A), 0.01, 0.0625, (), jnp.float32)
    readout_weight = gaussian(splits[13], (D_A, ACT), D_A ** -0.5, 0.1875, (), jnp.float32)
    prefix_weight_moment = gaussian(splits[14], (D_P, 2 * HEAD_DIM), (2.0 / (ACT * (TA_DEV * ROWS) ** 0.5)), 0.00390625, ((0, 16),), jnp.float32)
    attention_weight_moment = gaussian(splits[15], (D_A, 2 * HEADS * HEAD_DIM + 2 * HEAD_DIM), (2.0 / (ACT * (TA_DEV * ROWS) ** 0.5)), 0.00390625, ((0, 16),), jnp.float32)
    feedforward_weight_moment = gaussian(splits[16], (FF_A, 3, D_A), (2.0 / (ACT * (TA_DEV * ROWS) ** 0.5)), 0.00390625, ((0, 16),), jnp.float32)
    prefix_gains_moment = gaussian(splits[17], (1, D_P), (2.0 / (ACT * (TA_DEV * ROWS) ** 0.5)), 0.00390625, (), jnp.float32)
    action_gains_moment = gaussian(splits[18], (3, D_A), (2.0 / (ACT * (TA_DEV * ROWS) ** 0.5)), 0.00390625, (), jnp.float32)
    readout_weight_moment = gaussian(splits[19], (D_A, ACT), (2.0 / (ACT * (TA_DEV * ROWS) ** 0.5)), 0.00390625, (), jnp.float32)
    prefix_weight_average = gaussian(splits[20], (D_P, 2 * HEAD_DIM), D_P ** -0.5, 0.125, ((0, 16),), jnp.float32)
    attention_weight_average = gaussian(splits[21], (D_A, 2 * HEADS * HEAD_DIM + 2 * HEAD_DIM), D_A ** -0.5, 0.1875, ((0, 16),), jnp.float32)
    feedforward_weight_average = gaussian(splits[22], (FF_A, 3, D_A), D_A ** -0.5, 0.1875, ((0, 16),), jnp.float32)
    prefix_gains_average = gaussian(splits[23], (1, D_P), 0.01, 0.0625, (), jnp.float32)
    action_gains_average = gaussian(splits[24], (3, D_A), 0.01, 0.0625, (), jnp.float32)
    readout_weight_average = gaussian(splits[25], (D_A, ACT), D_A ** -0.5, 0.1875, (), jnp.float32)
    return dict(prefix_in=prefix_in, action_in=action_in, target=target, valid_mask=valid_mask, prefix_ids=prefix_ids, action_ids=action_ids, action_blocks=action_blocks, learning_rate=learning_rate, prefix_weight=prefix_weight, attention_weight=attention_weight, feedforward_weight=feedforward_weight, prefix_gains=prefix_gains, action_gains=action_gains, readout_weight=readout_weight, prefix_weight_moment=prefix_weight_moment, attention_weight_moment=attention_weight_moment, feedforward_weight_moment=feedforward_weight_moment, prefix_gains_moment=prefix_gains_moment, action_gains_moment=action_gains_moment, readout_weight_moment=readout_weight_moment, prefix_weight_average=prefix_weight_average, attention_weight_average=attention_weight_average, feedforward_weight_average=feedforward_weight_average, prefix_gains_average=prefix_gains_average, action_gains_average=action_gains_average, readout_weight_average=readout_weight_average)


NORM_EPSILON = 1e-06
MOMENTUM = 0.9
AVERAGE_DECAY = 0.8
NEGATIVE = -1e+30
HIGHEST = lax.Precision.HIGHEST

@jax.custom_vjp
def low(v):
    return lax.optimization_barrier(v.astype(jnp.bfloat16)).astype(jnp.float32)

@jax.custom_vjp
def low_back(v):
    return v

def low_keep(v):
    return (low(v), None)

def low_pass(kept, grad):
    return (grad,)

def back_keep(v):
    return (v, None)

def back_low(kept, grad):
    return (low(grad),)
low.defvjp(low_keep, low_pass)
low_back.defvjp(back_keep, back_low)

def rms_norm(stream, gain_row):
    return stream * lax.rsqrt(lax.optimization_barrier(jnp.mean(stream * stream, axis=-1, keepdims=True)) + NORM_EPSILON) * (1.0 + gain_row)

def visible(prefix_ids, action_ids, block_flags):
    levels = jnp.cumsum(block_flags)
    from_prefix = action_ids[:, None] == prefix_ids[None, :]
    from_action = (action_ids[:, None] == action_ids[None, :]) & (levels[None, :] <= levels[:, None])
    return jnp.concatenate([from_prefix, from_action], axis=1).astype(jnp.int32)

def row_loss(weights, row):
    prefix_weight, attention_weight, feedforward_weight, prefix_gains, action_gains, readout_weight = weights
    prefix_rows, action_rows, target_rows, valid_rows, prefix_ids, action_ids, block_flags = row
    query_width = HEADS * HEAD_DIM
    qkv_width = query_width + 2 * HEAD_DIM
    prefix_norm = low(rms_norm(prefix_rows, prefix_gains[0]))
    prefix_kv = low_back(low(jnp.dot(prefix_norm, prefix_weight, precision=HIGHEST)))
    action_norm = low(rms_norm(action_rows, action_gains[0]))
    action_qkv = low_back(low(jnp.dot(action_norm, attention_weight[:, :qkv_width], precision=HIGHEST)))
    queries = action_qkv[:, :query_width].reshape(-1, HEADS, HEAD_DIM)
    key_rows = jnp.concatenate([prefix_kv[:, :HEAD_DIM], action_qkv[:, query_width:query_width + HEAD_DIM]], 0)
    value_rows = jnp.concatenate([prefix_kv[:, HEAD_DIM:], action_qkv[:, query_width + HEAD_DIM:]], 0)
    scores = low_back(jnp.einsum('thd,kd->thk', queries, key_rows, precision=HIGHEST) * HEAD_DIM ** (-0.5))
    allowed = visible(prefix_ids, action_ids, block_flags)
    masked = jnp.where(allowed[:, None, :] != 0, scores, NEGATIVE)
    exp_scores = jnp.exp(masked - lax.optimization_barrier(jnp.max(masked, axis=-1, keepdims=True)))
    soft_weights = exp_scores / lax.optimization_barrier(jnp.sum(exp_scores, axis=-1, keepdims=True))
    mixed_heads = low_back(low(jnp.einsum('thk,kd->thd', low(soft_weights), value_rows, precision=HIGHEST)))
    mixed_heads = mixed_heads.reshape(-1, query_width)
    attention_out = low_back(jnp.einsum('th,dh->td', mixed_heads, attention_weight[:, qkv_width:], precision=HIGHEST))
    residual = action_rows + attention_out
    hidden_norm = low(rms_norm(residual, action_gains[1]))
    gate_value = low_back(jnp.einsum('td,fd->tf', hidden_norm, feedforward_weight[:, 0], precision=HIGHEST))
    linear_value = low_back(jnp.einsum('td,fd->tf', hidden_norm, feedforward_weight[:, 1], precision=HIGHEST))
    hidden = low(jax.nn.gelu(gate_value, approximate=True) * linear_value)
    branch_out = low_back(jnp.einsum('tf,fd->td', hidden, feedforward_weight[:, 2], precision=HIGHEST))
    final_stream = residual + branch_out
    predicted = jnp.dot(rms_norm(final_stream, action_gains[2]), readout_weight, precision=HIGHEST)
    error_term = predicted - target_rows
    return jnp.sum(valid_rows * error_term * error_term)

def advance(weight, moment, average, gradient, step_rate):
    moment_next = MOMENTUM * moment + gradient
    weight_next = weight - step_rate * (gradient + MOMENTUM * moment_next)
    average_next = AVERAGE_DECAY * average + (1.0 - AVERAGE_DECAY) * weight_next
    return (weight_next, moment_next, average_next)

def reference(prefix_in, action_in, target, valid_mask, prefix_ids, action_ids, action_blocks, learning_rate, prefix_weight, attention_weight, feedforward_weight, prefix_gains, action_gains, readout_weight, prefix_weight_moment, attention_weight_moment, feedforward_weight_moment, prefix_gains_moment, action_gains_moment, readout_weight_moment, prefix_weight_average, attention_weight_average, feedforward_weight_average, prefix_gains_average, action_gains_average, readout_weight_average):
    valid_float = valid_mask.astype(jnp.float32)
    valid_count = jnp.sum(valid_float)
    rows = (prefix_in.astype(jnp.float32), action_in.astype(jnp.float32), target, valid_float, prefix_ids, action_ids, action_blocks)
    params = (prefix_weight, attention_weight, feedforward_weight, prefix_gains, action_gains, readout_weight)

    def objective(weights):
        rounded = (low(weights[0]), low(weights[1]), low(weights[2]), weights[3], weights[4], weights[5])
        sums = lax.map(lambda row: jax.checkpoint(row_loss)(rounded, row), rows)
        return jnp.sum(sums) / valid_count
    loss_value, pull = jax.vjp(objective, params)
    grads = pull(jnp.ones_like(loss_value))[0]
    step_rate = learning_rate[0]
    first = advance(prefix_weight, prefix_weight_moment, prefix_weight_average, grads[0], step_rate)
    second = advance(attention_weight, attention_weight_moment, attention_weight_average, grads[1], step_rate)
    third = advance(feedforward_weight, feedforward_weight_moment, feedforward_weight_average, grads[2], step_rate)
    fourth = advance(prefix_gains, prefix_gains_moment, prefix_gains_average, grads[3], step_rate)
    fifth = advance(action_gains, action_gains_moment, action_gains_average, grads[4], step_rate)
    sixth = advance(readout_weight, readout_weight_moment, readout_weight_average, grads[5], step_rate)
    return (loss_value, first[0], second[0], third[0], fourth[0], fifth[0], sixth[0], first[1], second[1], third[1], fourth[1], fifth[1], sixth[1], first[2], second[2], third[2], fourth[2], fifth[2], sixth[2])
```

```python
import functools
import math

import jax
import jax.numpy as jnp
from jax import lax
from jax.experimental import pallas as pl
from jax.experimental.pallas import tpu as pltpu
from jax.sharding import PartitionSpec as P

HEADS = 8
HEAD_DIM = 256
QUERY_WIDTH = HEADS * HEAD_DIM
QKV_WIDTH = QUERY_WIDTH + 2 * HEAD_DIM
SCORE_SCALE = HEAD_DIM ** (-0.5)

NORM_EPSILON = 1e-06
MOMENTUM = 0.9
AVERAGE_DECAY = 0.8
NEGATIVE = -1e30

bf16 = jnp.bfloat16
f32 = jnp.float32
HIGHEST = lax.Precision.HIGHEST
VMEM_LIMIT = 48 * 2**20


def rms_norm(stream, gain_row):
    return (
        stream
        * lax.rsqrt(jnp.mean(stream * stream, axis=-1, keepdims=True) + NORM_EPSILON)
        * (1.0 + gain_row)
    )


def norm_back(stream, gain_row, cotangent):
    _, pull = jax.vjp(rms_norm, stream, gain_row)
    return pull(cotangent)


def gated_unit(gate_value, linear_value):
    return jax.nn.gelu(gate_value, approximate=True) * linear_value


def visible(prefix_ids, action_ids, block_flags):
    length = block_flags.shape[0]
    place = jnp.arange(length)
    upto = place[None, :] <= place[:, None]
    levels = jnp.sum(jnp.where(upto, block_flags[None, :], 0), axis=1)
    from_prefix = prefix_ids[:, None] == action_ids[None, :]
    from_action = (action_ids[:, None] == action_ids[None, :]) & (
        levels[:, None] <= levels[None, :]
    )
    return jnp.concatenate([from_prefix, from_action], axis=0).astype(jnp.int32)


def advance(weight, moment, average, gradient, step_rate):
    moment_next = MOMENTUM * moment + gradient
    weight_next = weight - step_rate * (gradient + MOMENTUM * moment_next)
    average_next = AVERAGE_DECAY * average + (1.0 - AVERAGE_DECAY) * weight_next
    return (weight_next, moment_next, average_next)


def mm(a, b, contract, out=f32):
    return lax.dot_general(
        a, b, (((contract[0],), (contract[1],)), ((), ())), preferred_element_type=f32
    ).astype(out)


class Ring:
    def __init__(self, wide):
        chips = wide // 2
        self.wide, self.chips = wide, chips
        self.cycle = list(range(0, chips, 2)) + list(range(1, chips, 2))[::-1]
        ahead = [(self.cycle[i], self.cycle[(i + 1) % chips]) for i in range(chips)]
        self.right = [(2 * s + c, 2 * t + c) for s, t in ahead for c in (0, 1)]
        self.left = [(t, s) for s, t in self.right]
        self.core = [(w, w ^ 1) for w in range(wide)]
        self.n_right = chips // 2
        self.n_left = chips - 1 - self.n_right

    def to_right(self, v):
        return lax.ppermute(v, "wide", self.right)

    def to_left(self, v):
        return lax.ppermute(v, "wide", self.left)

    def to_core(self, v):
        return lax.ppermute(v, "wide", self.core)

    def to_peer(self, v):
        return lax.ppermute(v, "batch", [(0, 1), (1, 0)])

    def owners(self):
        chip = lax.axis_index("wide") // 2
        place = [self.cycle.index(i) for i in range(self.chips)]
        here = jnp.array(place, jnp.int32)[chip]
        cycle = jnp.array(self.cycle, jnp.int32)
        rights = [cycle[(here - d + self.chips) % self.chips] for d in range(1, self.n_right + 1)]
        lefts = [cycle[(here + d) % self.chips] for d in range(1, self.n_left + 1)]
        return chip, rights, lefts

    def gather(self, shard, axis):
        half = shard.shape[axis] // 2
        me = lax.axis_index("batch")
        right, left = [], []
        if half % 16:
            r = l = shard
            for d in range(self.n_right):
                r = self.to_right(r)
                right.append((r,))
                if d < self.n_left:
                    l = self.to_left(l)
                    left.append(l)
            return right, left
        r = lax.dynamic_slice_in_dim(shard, me * half, half, axis)
        l = shard
        for d in range(self.n_right):
            r = self.to_right(r)
            if d < self.n_left:
                l = self.to_left(l)
                left.append(l)
            right.append((r, self.to_peer(r)))
        return right, left

    def scatter(self, own, right, left, axis):
        def add(u, v):
            return (u.astype(f32) + v.astype(f32)).astype(bf16)

        half = own.shape[axis] // 2
        me = lax.axis_index("batch")
        r = l = None
        split = half % 16 == 0
        for d in range(self.n_right - 1, -1, -1):
            mine = add(right[d][0], self.to_peer(right[d][1])) if split else right[d][0]
            r = self.to_left(mine if r is None else add(mine, r))
            if d < self.n_left:
                l = self.to_right(left[d] if l is None else add(left[d], l))
        whole = add(own, l)
        if not split:
            whole = add(whole, r)
            return whole.astype(f32) + self.to_peer(whole).astype(f32)
        mine = lax.dynamic_slice_in_dim(whole, me * half, half, axis)
        other = lax.dynamic_slice_in_dim(whole, (1 - me) * half, half, axis)
        total = (mine.astype(f32) + r.astype(f32) + self.to_peer(other).astype(f32)).astype(bf16)
        across = self.to_peer(total)
        return jnp.where(
            me == 0,
            jnp.concatenate([total, across], axis),
            jnp.concatenate([across, total], axis),
        ).astype(f32)

    def sum_all(self, v):
        k = 1
        while k < self.wide:
            v = v + lax.ppermute(v, "wide", [(w, w ^ k) for w in range(self.wide)])
            k *= 2
        return v + self.to_peer(v)


def assemble(ring, own, right, left, core_own, core_right, core_left, rows_a, width_a):
    half = rows_a // 2
    chip, rights, lefts = ring.owners()
    me, core = lax.axis_index("batch"), lax.axis_index("wide") % 2
    pieces, starts, sizes = [], [], []
    for which, o, rr, ll in ((core, own, right, left), (1 - core, core_own, core_right, core_left)):
        pieces.append(o)
        starts.append((chip * 2 + which, 0))
        sizes.append(rows_a)
        for d, parts in enumerate(rr):
            pieces += list(parts)
            spots = (me * half, (1 - me) * half) if len(parts) == 2 else (0,)
            starts += [(rights[d] * 2 + which, spot) for spot in spots]
            sizes += [p.shape[0] for p in parts]
        for d, whole in enumerate(ll):
            pieces.append(whole)
            starts.append((lefts[d] * 2 + which, 0))
            sizes.append(rows_a)
    n = len(pieces)
    table = jnp.stack([jnp.stack([jnp.asarray(s, jnp.int32) for s, _ in starts]),
                       jnp.stack([jnp.asarray(t, jnp.int32) for _, t in starts])])
    width_p = pieces[0].shape[1] - width_a
    pw = width_p // 2

    def kernel(table_ref, *refs):
        ins, (qkv, out, pre, sems) = refs[:n], refs[n:]
        copies = []
        for i in range(n):
            shard, inner = table_ref[0, i], table_ref[1, i]
            at = pl.multiple_of(shard * rows_a + inner, sizes[i])
            size = sizes[i]
            copies.append((ins[i].at[:, pl.ds(0, QKV_WIDTH)], qkv.at[pl.ds(at, size), :]))
            copies.append((ins[i].at[:, pl.ds(QKV_WIDTH, width_a - QKV_WIDTH)], out.at[pl.ds(at, size), :]))
            for j in (0, 1):
                to = pl.multiple_of(shard * (2 * rows_a) + j * rows_a + inner, sizes[i])
                copies.append((ins[i].at[:, pl.ds(width_a + j * pw, pw)], pre.at[pl.ds(to, size), :]))
        made = [pltpu.make_async_copy(s, t, sems.at[k]) for k, (s, t) in enumerate(copies)]
        for c in made:
            c.start()
        for c in made:
            c.wait()

    total = rows_a * ring.wide
    shapes = ((total, QKV_WIDTH), (total, width_a - QKV_WIDTH), (2 * total, pw))
    return pl.pallas_call(
        kernel,
        out_shape=[jax.ShapeDtypeStruct(sh, bf16) for sh in shapes],
        grid_spec=pltpu.PrefetchScalarGridSpec(
            num_scalar_prefetch=1,
            grid=(1,),
            in_specs=[pl.BlockSpec(memory_space=pl.ANY)] * n,
            out_specs=[pl.BlockSpec(sh, lambda i, t: (0, 0)) for sh in shapes],
            scratch_shapes=[pltpu.SemaphoreType.DMA((4 * n,))],
        ),
        compiler_params=pltpu.CompilerParams(vmem_limit_bytes=VMEM_LIMIT),
        cost_estimate=pl.CostEstimate(
            flops=0, transcendentals=0, bytes_accessed=2 * 2 * total * (width_a + width_p)
        ),
        name="assemble",
    )(table, *pieces)


def gelu_parts(v):
    c = math.sqrt(2.0 / math.pi)
    square = v * v
    t = jnp.tanh(c * v * (1.0 + 0.044715 * square))
    half = 0.5 * (1.0 + t)
    slope = half + 0.5 * v * (1.0 - t * t) * c * (1.0 + 3.0 * 0.044715 * square)
    return v * half, slope


def load_block(refs, buf, sems, k):
    at, made = 0, []
    for j, r in enumerate(refs):
        size = r.shape[1]
        made.append(pltpu.make_async_copy(r, buf.at[:, pl.ds(at, size), :], sems.at[k, j]))
        at += size
    return made


def ff_forward(norm_two, blocks, before):
    nb = len(blocks)
    flat = [a for blk in blocks for a in blk]
    tokens, dim = norm_two.shape
    units = sum(a.shape[1] for a in blocks[0])
    half = tokens // 2
    has_before = before is not None

    def kernel(norm_ref, *refs):
        refs = list(refs)
        ins = [[refs.pop(0) for _ in blk] for blk in blocks]
        if has_before:
            own_in, oth_in = refs.pop(0), refs.pop(0)
        gate_out, lin_out, hid_out, own_out, oth_out, buf, sems = refs
        i = pl.program_id(0)

        @pl.when(i == 0)
        def _():
            for k in range(nb):
                for c in load_block(ins[k], buf.at[k], sems, k):
                    c.start()
            if has_before:
                own_out[...] = own_in[...]
                oth_out[...] = oth_in[...]
            else:
                own_out[...] = jnp.zeros_like(own_out)
                oth_out[...] = jnp.zeros_like(oth_out)

        for k in range(nb):

            @pl.when(i == k)
            def _(k=k):
                for c in load_block(ins[k], buf.at[k], sems, k):
                    c.wait()

        w = buf.at[i]
        gate = mm(norm_ref[...], w[0], (1, 1))
        linear = mm(norm_ref[...], w[1], (1, 1))
        gate_out[0] = gate
        lin_out[0] = linear
        hidden = (gelu_parts(gate)[0] * linear).astype(bf16)
        hid_out[0] = hidden
        own_out[...] += mm(hidden[:half], w[2], (1, 0))
        oth_out[...] += mm(hidden[half:], w[2], (1, 0))

    once = pl.BlockSpec((tokens, dim), lambda i: (0, 0))
    row = pl.BlockSpec((half, dim), lambda i: (0, 0))
    step = pl.BlockSpec((1, tokens, units), lambda i: (i, 0, 0))
    any_space = pl.BlockSpec(memory_space=pl.ANY)
    return pl.pallas_call(
        kernel,
        out_shape=[
            jax.ShapeDtypeStruct((nb, tokens, units), f32),
            jax.ShapeDtypeStruct((nb, tokens, units), f32),
            jax.ShapeDtypeStruct((nb, tokens, units), bf16),
            jax.ShapeDtypeStruct((half, dim), f32),
            jax.ShapeDtypeStruct((half, dim), f32),
        ],
        grid=(nb,),
        in_specs=[once] + [any_space] * len(flat) + [row, row] * has_before,
        out_specs=[step, step, step, row, row],
        scratch_shapes=[
            pltpu.VMEM((nb, 3, units, dim), bf16),
            pltpu.SemaphoreType.DMA((nb, 2)),
        ],
        compiler_params=pltpu.CompilerParams(vmem_limit_bytes=VMEM_LIMIT),
        cost_estimate=pl.CostEstimate(
            flops=6 * nb * tokens * units * dim,
            transcendentals=nb * tokens * units,
            bytes_accessed=nb * (6 * units * dim + 10 * tokens * units),
        ),
        name="ff_forward",
    )(norm_two, *flat, *(before or ()))


def ff_backward(norm_two, branch_two, blocks, kept, picks, before):
    nb = len(blocks)
    flat = [a for blk in blocks for a in blk]
    gate_all, lin_all, hid_all = kept
    tokens, dim = norm_two.shape
    units = sum(a.shape[1] for a in blocks[0])
    half = tokens // 2
    has_before = before is not None
    first, stride = picks

    def kernel(norm_ref, branch_ref, gate_ref, lin_ref, hid_ref, *refs):
        refs = list(refs)
        ins = [[refs.pop(0) for _ in blk] for blk in blocks]
        if has_before:
            own_in, oth_in = refs.pop(0), refs.pop(0)
        outs = [[refs.pop(0) for _ in blk] for blk in blocks]
        own_out, oth_out, buf, grads, sems, out_sems = refs
        i = pl.program_id(0)

        def stores(k):
            at, made = 0, []
            for j, r in enumerate(outs[k]):
                size = r.shape[1]
                made.append(pltpu.make_async_copy(grads.at[k, :, pl.ds(at, size), :], r, out_sems.at[k, j]))
                at += size
            return made

        @pl.when(i == 0)
        def _():
            for k in range(nb):
                for c in load_block(ins[k], buf.at[k], sems, k):
                    c.start()
            if has_before:
                own_out[...] = own_in[...]
                oth_out[...] = oth_in[...]
            else:
                own_out[...] = jnp.zeros_like(own_out)
                oth_out[...] = jnp.zeros_like(oth_out)

        for k in range(nb):

            @pl.when(i == k)
            def _(k=k):
                for c in load_block(ins[k], buf.at[k], sems, k):
                    c.wait()

        w, g = buf.at[i], grads.at[i]
        back_hidden = mm(branch_ref[...], w[2], (1, 1))
        value, slope = gelu_parts(gate_ref[0])
        back_gate = (back_hidden * lin_ref[0] * slope).astype(bf16)
        back_linear = (back_hidden * value).astype(bf16)
        g[0] = mm(back_gate, norm_ref[...], (0, 0), bf16)
        g[1] = mm(back_linear, norm_ref[...], (0, 0), bf16)
        g[2] = mm(hid_ref[0], branch_ref[...], (0, 0), bf16)
        own_out[...] += mm(back_gate[:half], w[0], (1, 0)) + mm(back_linear[:half], w[1], (1, 0))
        oth_out[...] += mm(back_gate[half:], w[0], (1, 0)) + mm(back_linear[half:], w[1], (1, 0))

        for k in range(nb):

            @pl.when(i == k)
            def _(k=k):
                for c in stores(k):
                    c.start()

        @pl.when(i == nb - 1)
        def _():
            for k in range(nb):
                for c in stores(k):
                    c.wait()

    once = pl.BlockSpec((tokens, dim), lambda i: (0, 0))
    row = pl.BlockSpec((half, dim), lambda i: (0, 0))
    step = pl.BlockSpec((1, tokens, units), lambda i: (first + stride * i, 0, 0))
    any_space = pl.BlockSpec(memory_space=pl.ANY)
    made = pl.pallas_call(
        kernel,
        out_shape=[jax.ShapeDtypeStruct(a.shape, bf16) for a in flat]
        + [jax.ShapeDtypeStruct((half, dim), f32)] * 2,
        grid=(nb,),
        in_specs=[once, once, step, step, step] + [any_space] * len(flat) + [row, row] * has_before,
        out_specs=[any_space] * len(flat) + [row, row],
        scratch_shapes=[
            pltpu.VMEM((nb, 3, units, dim), bf16),
            pltpu.VMEM((nb, 3, units, dim), bf16),
            pltpu.SemaphoreType.DMA((nb, 2)),
            pltpu.SemaphoreType.DMA((nb, 2)),
        ],
        compiler_params=pltpu.CompilerParams(vmem_limit_bytes=VMEM_LIMIT),
        cost_estimate=pl.CostEstimate(
            flops=12 * nb * tokens * units * dim,
            transcendentals=nb * tokens * units,
            bytes_accessed=nb * (12 * units * dim + 10 * tokens * units),
        ),
        name="ff_backward",
    )(norm_two, branch_two, gate_all, lin_all, hid_all, *flat, *(before or ()))
    made = list(made)
    grads = [tuple(made.pop(0) for _ in blk) for blk in blocks]
    return grads, made


def attention(action_qkv, prefix_kv, allowed):
    tokens, keys = action_qkv.shape[0], allowed.shape[0]
    n_pre = prefix_kv.shape[0]

    def kernel(q_ref, kv_ref, pre_ref, allowed_ref, out_ref, k_all, v_turned):
        @pl.when(pl.program_id(0) == 0)
        def _():
            k_all[:n_pre] = pre_ref[:, :HEAD_DIM]
            k_all[n_pre:] = kv_ref[:, :HEAD_DIM]
            v_turned[:, :n_pre] = pre_ref[:, HEAD_DIM:].T
            v_turned[:, n_pre:] = kv_ref[:, HEAD_DIM:].T

        scores = mm(k_all[...], q_ref[...], (1, 1)) * SCORE_SCALE
        scores = jnp.where(allowed_ref[...] != 0, scores, NEGATIVE)
        exp_scores = jnp.exp(scores - jnp.max(scores, axis=0, keepdims=True))
        soft = exp_scores / jnp.sum(exp_scores, axis=0, keepdims=True)
        out_ref[...] = mm(v_turned[...], soft.astype(bf16), (1, 0)).T.astype(bf16)

    return pl.pallas_call(
        kernel,
        out_shape=jax.ShapeDtypeStruct((tokens, QUERY_WIDTH), bf16),
        grid=(HEADS,),
        in_specs=[
            pl.BlockSpec((tokens, HEAD_DIM), lambda h: (0, h)),
            pl.BlockSpec((tokens, 2 * HEAD_DIM), lambda h: (0, HEADS // 2)),
            pl.BlockSpec((n_pre, 2 * HEAD_DIM), lambda h: (0, 0)),
            pl.BlockSpec((keys, tokens), lambda h: (0, 0)),
        ],
        out_specs=pl.BlockSpec((tokens, HEAD_DIM), lambda h: (0, h)),
        scratch_shapes=[pltpu.VMEM((keys, HEAD_DIM), bf16), pltpu.VMEM((HEAD_DIM, keys), bf16)],
        compiler_params=pltpu.CompilerParams(vmem_limit_bytes=VMEM_LIMIT),
        cost_estimate=pl.CostEstimate(
            flops=4 * tokens * keys * QUERY_WIDTH,
            transcendentals=HEADS * tokens * keys,
            bytes_accessed=4 * tokens * QUERY_WIDTH + 4 * keys * HEAD_DIM + 4 * keys * tokens,
        ),
        name="attention",
    )(action_qkv, action_qkv, prefix_kv, allowed)


def attention_back(action_qkv, prefix_kv, allowed, back_mixed):
    tokens, keys = action_qkv.shape[0], allowed.shape[0]
    n_pre = prefix_kv.shape[0]

    def kernel(q_ref, kv_ref, pre_ref, allowed_ref, back_ref, qkv_out, pre_out, k_all, v_all, k_turned, k_sum, v_sum):
        h = pl.program_id(0)

        @pl.when(h == 0)
        def _():
            k_all[:n_pre] = pre_ref[:, :HEAD_DIM]
            k_all[n_pre:] = kv_ref[:, :HEAD_DIM]
            v_all[:n_pre] = pre_ref[:, HEAD_DIM:]
            v_all[n_pre:] = kv_ref[:, HEAD_DIM:]
            k_turned[...] = k_all[...].T
            k_sum[...] = jnp.zeros_like(k_sum)
            v_sum[...] = jnp.zeros_like(v_sum)

        query, back = q_ref[...], back_ref[...]
        scores = mm(k_all[...], query, (1, 1)) * SCORE_SCALE
        scores = jnp.where(allowed_ref[...] != 0, scores, NEGATIVE)
        exp_scores = jnp.exp(scores - jnp.max(scores, axis=0, keepdims=True))
        soft = exp_scores / jnp.sum(exp_scores, axis=0, keepdims=True)
        v_sum[...] += mm(soft.astype(bf16), back, (1, 0))
        back_soft = mm(v_all[...], back, (1, 1))
        mean = jnp.sum(soft * back_soft, axis=0, keepdims=True)
        back_scores = (soft * (back_soft - mean)).astype(bf16)
        k_sum[...] += mm(back_scores, query, (1, 0))
        turned = mm(k_turned[...], back_scores, (1, 0)) * SCORE_SCALE
        qkv_out[:, pl.ds(pl.multiple_of(h * HEAD_DIM, HEAD_DIM), HEAD_DIM)] = turned.T.astype(bf16)

        @pl.when(h == HEADS - 1)
        def _():
            pre_out[:, :HEAD_DIM] = (k_sum[:n_pre] * SCORE_SCALE).astype(bf16)
            pre_out[:, HEAD_DIM:] = v_sum[:n_pre].astype(bf16)
            qkv_out[:, QUERY_WIDTH : QUERY_WIDTH + HEAD_DIM] = (k_sum[n_pre:] * SCORE_SCALE).astype(bf16)
            qkv_out[:, QUERY_WIDTH + HEAD_DIM :] = v_sum[n_pre:].astype(bf16)

    return pl.pallas_call(
        kernel,
        out_shape=[
            jax.ShapeDtypeStruct((tokens, QKV_WIDTH), bf16),
            jax.ShapeDtypeStruct((n_pre, 2 * HEAD_DIM), bf16),
        ],
        grid=(HEADS,),
        in_specs=[
            pl.BlockSpec((tokens, HEAD_DIM), lambda h: (0, h)),
            pl.BlockSpec((tokens, 2 * HEAD_DIM), lambda h: (0, HEADS // 2)),
            pl.BlockSpec((n_pre, 2 * HEAD_DIM), lambda h: (0, 0)),
            pl.BlockSpec((keys, tokens), lambda h: (0, 0)),
            pl.BlockSpec((tokens, HEAD_DIM), lambda h: (0, h)),
        ],
        out_specs=[
            pl.BlockSpec((tokens, QKV_WIDTH), lambda h: (0, 0)),
            pl.BlockSpec((n_pre, 2 * HEAD_DIM), lambda h: (0, 0)),
        ],
        scratch_shapes=[
            pltpu.VMEM((keys, HEAD_DIM), bf16),
            pltpu.VMEM((keys, HEAD_DIM), bf16),
            pltpu.VMEM((HEAD_DIM, keys), bf16),
            pltpu.VMEM((keys, HEAD_DIM), f32),
            pltpu.VMEM((keys, HEAD_DIM), f32),
        ],
        compiler_params=pltpu.CompilerParams(vmem_limit_bytes=VMEM_LIMIT),
        cost_estimate=pl.CostEstimate(
            flops=10 * tokens * keys * QUERY_WIDTH,
            transcendentals=HEADS * tokens * keys,
            bytes_accessed=8 * tokens * QUERY_WIDTH + 8 * keys * HEAD_DIM + 4 * keys * tokens,
        ),
        name="attention_back",
    )(action_qkv, action_qkv, prefix_kv, allowed, back_mixed)


def on_device(
    ring,
    prefix_in,
    action_in,
    target,
    valid_mask,
    prefix_ids,
    action_ids,
    action_blocks,
    learning_rate,
    prefix_weight,
    attention_weight,
    feedforward_weight,
    prefix_gains,
    action_gains,
    readout_weight,
    prefix_weight_moment,
    attention_weight_moment,
    feedforward_weight_moment,
    prefix_gains_moment,
    action_gains_moment,
    readout_weight_moment,
    prefix_weight_average,
    attention_weight_average,
    feedforward_weight_average,
    prefix_gains_average,
    action_gains_average,
    readout_weight_average,
):
    core = lax.axis_index("wide") % 2
    rows_a, width_a = attention_weight.shape
    width_p = prefix_weight.shape[1]
    n_right, n_left = ring.n_right, ring.n_left

    prefix_bf = prefix_weight.astype(bf16)
    packed = jnp.concatenate(
        [attention_weight.astype(bf16), prefix_bf[:rows_a], prefix_bf[rows_a:]], axis=1
    )
    a_right, a_left = ring.gather(packed, 0)
    swap = ring.to_core
    qkv_weight, output_weight, prefix_full = assemble(
        ring,
        packed,
        a_right,
        a_left,
        swap(packed),
        [tuple(swap(u) for u in parts) for parts in a_right],
        [swap(u) for u in a_left],
        rows_a,
        width_a,
    )
    ff_own = jnp.transpose(feedforward_weight, (1, 0, 2)).astype(bf16)
    f_right, f_left = ring.gather(ff_own, 1)
    own = [("own", 0)]
    order = own + [x for d in range(n_right) for x in ([("left", d)] if d < n_left else []) + [("right", d)]]
    weights = {("own", 0): (ff_own,)}
    weights.update({("left", d): (w,) for d, w in enumerate(f_left)})
    weights.update({("right", d): pair for d, pair in enumerate(f_right)})
    groups = [order[: 1 + 2 * (n_left - 1)], order[1 + 2 * (n_left - 1) :]]

    prefix_rows = prefix_in[0].astype(f32)
    action_rows = action_in[0].astype(f32)
    target_rows = target[0]
    valid_rows = valid_mask[0].astype(f32)
    allowed = visible(prefix_ids[0], action_ids[0], action_blocks[0])
    prefix_norm = rms_norm(prefix_rows, prefix_gains[0]).astype(bf16)
    action_norm = rms_norm(action_rows, action_gains[0]).astype(bf16)
    prefix_kv = mm(prefix_norm, prefix_full, (1, 0), bf16)
    action_qkv = mm(action_norm, qkv_weight, (1, 0), bf16)
    mixed_heads = attention(action_qkv, prefix_kv, allowed)
    residual = action_rows + mm(mixed_heads, output_weight, (1, 1))
    tokens = residual.shape[0]
    hidden_norm = rms_norm(residual, action_gains[1]).astype(bf16)
    norm_two = jnp.concatenate([hidden_norm, swap(hidden_norm)], 0)
    kept, branch = [], None
    for group in groups:
        *values, own_rows, other_rows = ff_forward(norm_two, [weights[x] for x in group], branch)
        kept.append(values)
        branch = (own_rows, other_rows)
    final_stream = residual + branch[0] + swap(branch[1])
    final_norm = rms_norm(final_stream, action_gains[2])
    predicted = jnp.dot(final_norm, readout_weight, precision=HIGHEST)
    error_term = predicted - target_rows

    loss_sum = jnp.sum(valid_rows * error_term * error_term)
    own_count = jnp.sum(valid_rows)
    back_predicted = 2.0 * valid_rows * error_term
    grad_readout = lax.dot_general(
        back_predicted, final_norm, (((0,), (0,)), ((), ())), precision=HIGHEST
    )
    back_final, grad_gain_final = norm_back(
        final_stream, action_gains[2], jnp.dot(back_predicted, readout_weight.T, precision=HIGHEST)
    )
    back_branch = back_final.astype(bf16)
    branch_two = jnp.concatenate([back_branch, swap(back_branch)], 0)
    back, grads = None, {}
    for group, values in zip(reversed(groups), reversed(kept)):
        last = len(group) - 1
        made, back = ff_backward(
            norm_two, branch_two, [weights[x] for x in group[::-1]], values, (last, -1), back
        )
        grads.update(zip(group[::-1], made))
    ff_sum = ring.scatter(
        grads["own", 0][0],
        [grads["right", d] for d in range(n_right)],
        [grads["left", d][0] for d in range(n_left)],
        1,
    )
    back_norm_in = back[0] + swap(back[1])
    back_norm_out, grad_gain_hidden = norm_back(residual, action_gains[1], back_norm_in)
    back_residual = back_final + back_norm_out
    back_attention = back_residual.astype(bf16)
    back_mixed = mm(back_attention, output_weight, (1, 0), bf16)
    back_qkv, back_prefix_kv = attention_back(action_qkv, prefix_kv, allowed, back_mixed)

    def by_core(v, size):
        cut = v.reshape(v.shape[0], ring.chips, 2, size)
        cut = jnp.transpose(cut, (2, 0, 1, 3)).reshape(2, v.shape[0], ring.chips * size)
        return (
            lax.dynamic_index_in_dim(cut, core, 0, False),
            lax.dynamic_index_in_dim(cut, 1 - core, 0, False),
        )

    norm_mine, norm_other = by_core(action_norm, rows_a)
    attn_mine, attn_other = by_core(back_attention, rows_a)
    norm_rows = jnp.concatenate([norm_mine, swap(norm_other)], 0)
    attn_rows = jnp.concatenate([attn_mine, swap(attn_other)], 0)
    qkv_rows = jnp.concatenate([back_qkv, swap(back_qkv)], 0)
    mixed_rows = jnp.concatenate([mixed_heads, swap(mixed_heads)], 0)
    grad_qkv = mm(norm_rows, qkv_rows, (0, 0), bf16)
    grad_output = mm(attn_rows, mixed_rows, (0, 0), bf16)
    grad_prefix = mm(prefix_norm, back_prefix_kv, (0, 0), bf16)
    grad_prefix = grad_prefix.reshape(ring.chips, 2, 2, rows_a, width_p).transpose(1, 0, 3, 2, 4)
    grad_prefix = grad_prefix.reshape(2, ring.chips * rows_a, 2 * width_p)
    prefix_mine = lax.dynamic_index_in_dim(grad_prefix, core, 0, False)
    prefix_other = lax.dynamic_index_in_dim(grad_prefix, 1 - core, 0, False)
    prefix_sum = (prefix_mine.astype(f32) + swap(prefix_other).astype(f32)).astype(bf16)
    grad_packed = jnp.concatenate([grad_qkv, grad_output, prefix_sum], 1)
    chip, rights, lefts = ring.owners()
    me, cut = lax.axis_index("batch"), rows_a // 2

    def rows_of(owner, start, size):
        return lax.dynamic_slice_in_dim(grad_packed, owner * rows_a + start, size, 0)

    packed_sum = ring.scatter(
        rows_of(chip, 0, rows_a),
        [
            (rows_of(o, me * cut, cut), rows_of(o, (1 - me) * cut, cut))
            if len(parts) == 2
            else (rows_of(o, 0, rows_a),)
            for o, parts in zip(rights, a_right)
        ],
        [rows_of(o, 0, rows_a) for o in lefts],
        0,
    )

    _, grad_gain_action = norm_back(
        action_rows, action_gains[0], mm(back_qkv, qkv_weight, (1, 1))
    )
    _, grad_gain_prefix = norm_back(
        prefix_rows, prefix_gains[0], mm(back_prefix_kv, prefix_full, (1, 1))
    )
    dim = action_rows.shape[1]
    small = jnp.concatenate(
        [
            grad_readout,
            grad_gain_prefix.reshape(-1, dim),
            grad_gain_action[None],
            grad_gain_hidden[None],
            grad_gain_final[None],
            jnp.full((1, dim), loss_sum),
            jnp.full((1, dim), own_count),
        ],
        0,
    )
    small = ring.sum_all(small)
    act = grad_readout.shape[0]
    n_pre = grad_gain_prefix.shape[0] // dim
    count = small[act + n_pre + 4, 0]
    loss_value = small[act + n_pre + 3, 0] / count
    scale = 1.0 / count
    step_rate = learning_rate[0]
    first = advance(
        prefix_weight,
        prefix_weight_moment,
        prefix_weight_average,
        jnp.concatenate(
            [packed_sum[:, width_a : width_a + width_p], packed_sum[:, width_a + width_p :]], 0
        )
        * scale,
        step_rate,
    )
    second = advance(
        attention_weight,
        attention_weight_moment,
        attention_weight_average,
        packed_sum[:, :width_a] * scale,
        step_rate,
    )
    third = advance(
        feedforward_weight,
        feedforward_weight_moment,
        feedforward_weight_average,
        jnp.transpose(ff_sum, (1, 0, 2)) * scale,
        step_rate,
    )
    fourth = advance(
        prefix_gains,
        prefix_gains_moment,
        prefix_gains_average,
        small[act : act + n_pre].reshape(1, -1) * scale,
        step_rate,
    )
    fifth = advance(
        action_gains,
        action_gains_moment,
        action_gains_average,
        small[act + n_pre : act + n_pre + 3] * scale,
        step_rate,
    )
    sixth = advance(
        readout_weight,
        readout_weight_moment,
        readout_weight_average,
        small[:act].T * scale,
        step_rate,
    )
    return (loss_value,) + tuple(
        group[i]
        for i in range(3)
        for group in (first, second, third, fourth, fifth, sixth)
    )


def solution(mesh):
    rows = P(("batch", "wide"))
    wide = P("wide")
    whole = P()
    weights = (wide, wide, wide, whole, whole, whole)
    return jax.shard_map(
        functools.partial(on_device, Ring(mesh.shape["wide"])),
        mesh=mesh,
        in_specs=(rows,) * 7 + (whole,) + weights * 3,
        out_specs=(whole,) + weights * 3,
        check_vma=False,
    )
```

```python
import functools
import math

import jax
import jax.numpy as jnp
import numpy as np
from jax import lax
from jax.experimental import pallas as pl
from jax.experimental.pallas import tpu as pltpu
from jax.sharding import PartitionSpec as P

HEADS = 8
HEAD_DIM = 256
QUERY_WIDTH = HEADS * HEAD_DIM
QKV_WIDTH = QUERY_WIDTH + 2 * HEAD_DIM
SCORE_SCALE = HEAD_DIM ** (-0.5)

NORM_EPSILON = 1e-06
MOMENTUM = 0.9
AVERAGE_DECAY = 0.8
NEGATIVE = -1e30

bf16 = jnp.bfloat16
f32 = jnp.float32
HIGHEST = lax.Precision.HIGHEST
VMEM_LIMIT = 48 * 2**20
BRIEF = pl.CostEstimate(flops=1, transcendentals=0, bytes_accessed=1)


def rms_norm(stream, gain_row):
    return (
        stream
        * lax.rsqrt(jnp.mean(stream * stream, axis=-1, keepdims=True) + NORM_EPSILON)
        * (1.0 + gain_row)
    )


def norm_back(stream, gain_row, cotangent):
    _, pull = jax.vjp(rms_norm, stream, gain_row)
    return pull(cotangent)


def gated_unit(gate_value, linear_value):
    return jax.nn.gelu(gate_value, approximate=True) * linear_value


def visible(prefix_ids, action_ids, block_flags):
    length = block_flags.shape[0]
    place = jnp.arange(length)
    upto = place[None, :] <= place[:, None]
    levels = jnp.sum(jnp.where(upto, block_flags[None, :], 0), axis=1)
    from_prefix = prefix_ids[:, None] == action_ids[None, :]
    from_action = (action_ids[:, None] == action_ids[None, :]) & (
        levels[:, None] <= levels[None, :]
    )
    return jnp.concatenate([from_prefix, from_action], axis=0).astype(jnp.int32)


def advance(weight, moment, average, gradient, step_rate):
    moment_next = MOMENTUM * moment + gradient
    weight_next = weight - step_rate * (gradient + MOMENTUM * moment_next)
    average_next = AVERAGE_DECAY * average + (1.0 - AVERAGE_DECAY) * weight_next
    return (weight_next, moment_next, average_next)


def mm(a, b, contract, out=f32):
    return lax.dot_general(
        a, b, (((contract[0],), (contract[1],)), ((), ())), preferred_element_type=f32
    ).astype(out)


class Order:
    def __init__(self):
        self.token = jnp.zeros((), jnp.int32)

    def __call__(self, *values):
        *values, self.token = lax.optimization_barrier((*values, self.token))
        return values[0] if len(values) == 1 else values


class Ring:
    def __init__(self, wide):
        chips = wide // 2
        self.wide, self.chips = wide, chips
        self.cycle = list(range(0, chips, 2)) + list(range(1, chips, 2))[::-1]
        ahead = [(self.cycle[i], self.cycle[(i + 1) % chips]) for i in range(chips)]
        self.right = [(2 * s + c, 2 * t + c) for s, t in ahead for c in (0, 1)]
        self.left = [(t, s) for s, t in self.right]
        self.core = [(w, w ^ 1) for w in range(wide)]
        self.n_right = chips // 2
        self.n_left = chips - 1 - self.n_right

    def to_right(self, v):
        return lax.ppermute(v, "wide", self.right)

    def to_left(self, v):
        return lax.ppermute(v, "wide", self.left)

    def to_core(self, v):
        return lax.ppermute(v, "wide", self.core)

    def to_peer(self, v):
        return lax.ppermute(v, "batch", [(0, 1), (1, 0)])

    def owners(self, w):
        here = self.cycle.index(w // 2)
        rights = [self.cycle[(here - d) % self.chips] for d in range(1, self.n_right + 1)]
        lefts = [self.cycle[(here + d) % self.chips] for d in range(1, self.n_left + 1)]
        return [w // 2] + rights + lefts

    def bits(self):
        k, steps = 1, [self.to_peer]
        while k < self.wide:
            pairs = [(w, w ^ k) for w in range(self.wide)]
            steps.append(functools.partial(lax.ppermute, axis_name="wide", perm=pairs))
            k *= 2
        return steps


def add(*terms):
    return sum(t.astype(f32) for t in terms).astype(bf16)


class Gathering:
    def __init__(self, ring, order, axis, split_left):
        self.ring, self.order, self.axis, self.split_left = ring, order, axis, split_left
        self.blocks = {}
        self.flying = {}
        self.count = {"right": ring.n_right, "left": ring.n_left}
        self.d = {"right": 0, "left": 0}

    def halved(self, side, shard):
        half = shard.shape[self.axis] // 2
        return half % 16 == 0 and (side == "right" or self.split_left)

    def start(self, side, shard):
        cut = self.halved(side, shard)
        if cut:
            half = shard.shape[self.axis] // 2
            shard = lax.dynamic_slice_in_dim(shard, lax.axis_index("batch") * half, half, self.axis)
        self.flying[side] = (cut, self.send(side, shard))

    def send(self, side, v):
        return self.ring.to_right(v) if side == "right" else self.ring.to_left(v)

    def step(self, *sides):
        sides = [x for x in sides if self.d[x] < self.count[x]]
        for side in sides:
            cut, v = self.flying[side]
            v = self.order(v)
            d = self.d[side]
            self.blocks[side, d] = (v, self.ring.to_peer(v)) if cut else (v,)
            self.d[side] = d + 1
            if d + 1 < self.count[side]:
                self.flying[side] = (cut, self.send(side, v))

    def settle(self, *keys):
        for key in keys:
            if key in self.blocks:
                self.blocks[key] = tuple(self.order(p) for p in self.blocks[key])


class Summing:
    def __init__(self, ring, order, axis):
        self.ring, self.order, self.axis = ring, order, axis
        self.parts, self.crossed = {}, {}
        self.came = {"right": None, "left": None}
        self.d = {"right": ring.n_right - 1, "left": ring.n_left - 1}

    def put(self, key, parts):
        self.parts[key] = parts
        if len(parts) == 2:
            self.crossed[key] = self.ring.to_peer(parts[1])

    def step(self, *sides):
        for side in sides:
            d = self.d[side]
            if d < 0:
                continue
            terms = [self.parts[side, d][0]]
            terms += [self.crossed[side, d]] if (side, d) in self.crossed else []
            terms += [self.came[side]] if self.came[side] is not None else []
            terms = self.order(*terms)
            total = self.order(add(*terms)) if isinstance(terms, (list, tuple)) else terms
            self.came[side] = self.ring.to_left(total) if side == "right" else self.ring.to_right(total)
            self.d[side] = d - 1

    def ready(self, *keys):
        for key in keys:
            if key in self.crossed:
                self.crossed[key] = self.order(self.crossed[key])

    def land(self, side):
        self.came[side] = self.order(self.came[side])

    def left(self):
        return max(self.d.values()) + 1

    def own(self, shard):
        me = lax.axis_index("batch")
        half = shard.shape[self.axis] // 2
        self.ends = ["right"]
        if len(self.parts["left", 0]) == 1:
            shard = self.order(add(*self.order(shard, self.came["left"])))
        else:
            self.ends.append("left")
        self.split = len(self.parts["right", 0]) == 2
        self.mine = shard
        if self.split:
            self.mine = lax.dynamic_slice_in_dim(shard, me * half, half, self.axis)
            other = lax.dynamic_slice_in_dim(shard, (1 - me) * half, half, self.axis)
            self.mine, other = self.order(self.mine, other)
            self.across = self.ring.to_peer(other)

    def close(self):
        terms = [self.mine] + [self.came[e] for e in self.ends] + ([self.across] if self.split else [])
        self.total = self.order(add(*self.order(*terms)))
        self.across = self.ring.to_peer(self.total)

    def result(self):
        me = lax.axis_index("batch")
        total, across = self.order(self.total, self.across)
        if not self.split:
            return total.astype(f32) + across.astype(f32)
        return jnp.where(
            me == 0,
            jnp.concatenate([total, across], self.axis),
            jnp.concatenate([across, total], self.axis),
        ).astype(f32)


def packing(ring, counts, rows_a, width_a):
    half = rows_a // 2
    table = np.zeros((2, ring.wide, 2, sum(counts)), np.int32)
    for me in (0, 1):
        for w in range(ring.wide):
            where, first = [], []
            for owner, n in zip(ring.owners(w), counts):
                where += [owner] * n
                first += [me * half, (1 - me) * half] if n == 2 else [0]
            table[me, w] = where, first
    table = jnp.array(table)[lax.axis_index("batch"), lax.axis_index("wide")]

    def spots(part, chip, inner, size, width_p):
        at = pl.ds(pl.multiple_of(chip * rows_a + inner, size), size)
        pw = width_p // 2
        yield part.at[:, pl.ds(0, QKV_WIDTH)], 0, at
        yield part.at[:, pl.ds(QKV_WIDTH, width_a - QKV_WIDTH)], 1, at
        for j in (0, 1):
            to = pl.ds(pl.multiple_of(chip * (2 * rows_a) + j * rows_a + inner, size), size)
            yield part.at[:, pl.ds(width_a + j * pw, pw)], 2, to

    return table, spots


def repack(ring, blocks, arrays, rows_a, width_a, width_p):
    gather = arrays is None
    counts = [len(b) for b in blocks] if gather else blocks
    half = rows_a // 2
    table, spots = packing(ring, counts, rows_a, width_a)
    sizes = [size for n in counts for size in ([half] * 2 if n == 2 else [rows_a])]
    n = len(sizes)
    total = rows_a * ring.chips
    shapes = ((total, QKV_WIDTH), (total, width_a - QKV_WIDTH), (2 * total, width_p // 2))
    any_space = pl.BlockSpec(memory_space=pl.ANY)
    whole = [pl.BlockSpec(sh, lambda i, t: (0, 0)) for sh in shapes]

    def kernel(table_ref, *refs):
        sems = refs[-1]
        parts, full = (refs[:n], refs[n:-1]) if gather else (refs[3:-1], refs[:3])
        copies = []
        for i in range(n):
            for cut, which, rows in spots(parts[i], table_ref[0, i], table_ref[1, i], sizes[i], width_p):
                other = full[which].at[rows, :]
                pair = (cut, other) if gather else (other, cut)
                copies.append(pltpu.make_async_copy(*pair, sems.at[len(copies)]))
        for c in copies:
            c.start()
        for c in copies:
            c.wait()

    out_shapes = shapes if gather else [(size, width_a + width_p) for size in sizes]
    out = pl.pallas_call(
        kernel,
        out_shape=[jax.ShapeDtypeStruct(sh, bf16) for sh in out_shapes],
        grid_spec=pltpu.PrefetchScalarGridSpec(
            num_scalar_prefetch=1,
            grid=(1,),
            in_specs=[any_space] * n if gather else whole,
            out_specs=whole if gather else [any_space] * n,
            scratch_shapes=[pltpu.SemaphoreType.DMA((4 * n,))],
        ),
        compiler_params=pltpu.CompilerParams(vmem_limit_bytes=VMEM_LIMIT),
        cost_estimate=BRIEF,
        name="assemble" if gather else "disassemble",
    )(table, *([p for b in blocks for p in b] if gather else arrays))
    if gather:
        return out
    out = list(out)
    return [tuple(out.pop(0) for _ in range(k)) for k in counts]


def interleave(ring, own, other, rows):
    core = (lax.axis_index("wide") % 2).reshape(1)

    def kernel(core_ref, own_ref, other_ref, out_ref, sems):
        copies = []
        for chip in range(ring.chips):
            for j, ref in enumerate((own_ref, other_ref)):
                side = core_ref[0] if j == 0 else 1 - core_ref[0]
                to = pl.ds(pl.multiple_of((2 * chip + side) * rows, rows), rows)
                copies.append(
                    pltpu.make_async_copy(
                        ref.at[pl.ds(chip * rows, rows), :], out_ref.at[to, :], sems.at[chip, j]
                    )
                )
        for c in copies:
            c.start()
        for c in copies:
            c.wait()

    shape = (2 * own.shape[0], own.shape[1])
    return pl.pallas_call(
        kernel,
        out_shape=jax.ShapeDtypeStruct(shape, bf16),
        grid_spec=pltpu.PrefetchScalarGridSpec(
            num_scalar_prefetch=1,
            grid=(1,),
            in_specs=[pl.BlockSpec(memory_space=pl.ANY)] * 2,
            out_specs=pl.BlockSpec(shape, lambda i, t: (0, 0)),
            scratch_shapes=[pltpu.SemaphoreType.DMA((ring.chips, 2))],
        ),
        compiler_params=pltpu.CompilerParams(vmem_limit_bytes=VMEM_LIMIT),
        cost_estimate=BRIEF,
        name="interleave",
    )(core, own, other)


def norm_by_core(ring, rows, gains, size):
    core = (lax.axis_index("wide") % 2).reshape(1)
    tokens, dim = rows.shape
    step = 128

    def kernel(core_ref, rows_ref, gains_ref, mine_ref, other_ref):
        v = rows_ref[...].astype(f32)
        normed = rms_norm(v, gains_ref[0]).astype(bf16)
        for swapped in (0, 1):

            @pl.when(core_ref[0] == swapped)
            def _(swapped=swapped):
                for chip in range(ring.chips):
                    for side, ref in enumerate((mine_ref, other_ref)):
                        at = (2 * chip + (side ^ swapped)) * size
                        ref[:, chip * size : (chip + 1) * size] = normed[:, at : at + size]

    half = pl.BlockSpec((step, dim // 2), lambda i, t: (i, 0))
    return pl.pallas_call(
        kernel,
        out_shape=[jax.ShapeDtypeStruct((tokens, dim // 2), bf16)] * 2,
        grid_spec=pltpu.PrefetchScalarGridSpec(
            num_scalar_prefetch=1,
            grid=(tokens // step,),
            in_specs=[
                pl.BlockSpec((step, dim), lambda i, t: (i, 0)),
                pl.BlockSpec((1, dim), lambda i, t: (0, 0)),
            ],
            out_specs=[half, half],
        ),
        compiler_params=pltpu.CompilerParams(vmem_limit_bytes=VMEM_LIMIT),
        cost_estimate=BRIEF,
        name="norm_by_core",
    )(core, rows, gains)


def gelu_parts(v):
    c = math.sqrt(2.0 / math.pi)
    square = v * v
    t = jnp.tanh(c * v * (1.0 + 0.044715 * square))
    half = 0.5 * (1.0 + t)
    slope = half + 0.5 * v * (1.0 - t * t) * c * (1.0 + 3.0 * 0.044715 * square)
    return v * half, slope


def load_block(refs, buf, sems, k):
    at, made = 0, []
    for j, r in enumerate(refs):
        size = r.shape[1]
        made.append(pltpu.make_async_copy(r, buf.at[:, pl.ds(at, size), :], sems.at[k, j]))
        at += size
    return made


def ff_forward(norm_two, blocks, before):
    nb = len(blocks)
    flat = [a for blk in blocks for a in blk]
    tokens, dim = norm_two.shape
    units = sum(a.shape[1] for a in blocks[0])
    half = tokens // 2
    has_before = before is not None

    def kernel(norm_ref, *refs):
        refs = list(refs)
        ins = [[refs.pop(0) for _ in blk] for blk in blocks]
        if has_before:
            own_in, oth_in = refs.pop(0), refs.pop(0)
        gate_out, lin_out, hid_out, own_out, oth_out, buf, total, sems = refs
        i = pl.program_id(0)

        @pl.when(i == 0)
        def _():
            for k in range(nb):
                for c in load_block(ins[k], buf.at[k], sems, k):
                    c.start()
            if has_before:
                total[:half] = own_in[...]
                total[half:] = oth_in[...]
            else:
                total[...] = jnp.zeros_like(total)

        for k in range(nb):

            @pl.when(i == k)
            def _(k=k):
                for c in load_block(ins[k], buf.at[k], sems, k):
                    c.wait()

        w = buf.at[i]
        if units % 128 == 0:
            both = mm(norm_ref[...], w[:2].reshape(2 * units, dim), (1, 1))
            gate, linear = both[:, :units], both[:, units:]
        else:
            gate, linear = (mm(norm_ref[...], w[j], (1, 1)) for j in (0, 1))
        gate_out[0] = gate
        lin_out[0] = linear
        hidden = (gelu_parts(gate)[0] * linear).astype(bf16)
        hid_out[0] = hidden
        total[...] += mm(hidden, w[2], (1, 0))

        @pl.when(i == nb - 1)
        def _():
            own_out[...] = total[:half]
            oth_out[...] = total[half:]

    once = pl.BlockSpec((tokens, dim), lambda i: (0, 0))
    row = pl.BlockSpec((half, dim), lambda i: (0, 0))
    step = pl.BlockSpec((1, tokens, units), lambda i: (i, 0, 0))
    any_space = pl.BlockSpec(memory_space=pl.ANY)
    return pl.pallas_call(
        kernel,
        out_shape=[
            jax.ShapeDtypeStruct((nb, tokens, units), f32),
            jax.ShapeDtypeStruct((nb, tokens, units), f32),
            jax.ShapeDtypeStruct((nb, tokens, units), bf16),
            jax.ShapeDtypeStruct((half, dim), f32),
            jax.ShapeDtypeStruct((half, dim), f32),
        ],
        grid=(nb,),
        in_specs=[once] + [any_space] * len(flat) + [row, row] * has_before,
        out_specs=[step, step, step, row, row],
        scratch_shapes=[
            pltpu.VMEM((nb, 3, units, dim), bf16),
            pltpu.VMEM((tokens, dim), f32),
            pltpu.SemaphoreType.DMA((nb, 2)),
        ],
        compiler_params=pltpu.CompilerParams(vmem_limit_bytes=VMEM_LIMIT),
        cost_estimate=BRIEF,
        name="ff_forward",
    )(norm_two, *flat, *(before or ()))


def ff_backward(norm_two, branch_two, blocks, kept, picks, before):
    nb = len(blocks)
    flat = [a for blk in blocks for a in blk]
    gate_all, lin_all, hid_all = kept
    tokens, dim = norm_two.shape
    units = sum(a.shape[1] for a in blocks[0])
    half = tokens // 2
    has_before = before is not None
    first, stride = picks

    def kernel(norm_ref, branch_ref, gate_ref, lin_ref, hid_ref, *refs):
        refs = list(refs)
        ins = [[refs.pop(0) for _ in blk] for blk in blocks]
        if has_before:
            own_in, oth_in = refs.pop(0), refs.pop(0)
        outs = [[refs.pop(0) for _ in blk] for blk in blocks]
        own_out, oth_out, buf, grads, total, sems, out_sems = refs
        i = pl.program_id(0)

        def stores(k):
            at, made = 0, []
            for j, r in enumerate(outs[k]):
                size = r.shape[1]
                made.append(pltpu.make_async_copy(grads.at[k, :, pl.ds(at, size), :], r, out_sems.at[k, j]))
                at += size
            return made

        @pl.when(i == 0)
        def _():
            for k in range(nb):
                for c in load_block(ins[k], buf.at[k], sems, k):
                    c.start()
            if has_before:
                total[:half] = own_in[...]
                total[half:] = oth_in[...]
            else:
                total[...] = jnp.zeros_like(total)

        for k in range(nb):

            @pl.when(i == k)
            def _(k=k):
                for c in load_block(ins[k], buf.at[k], sems, k):
                    c.wait()

        w, g = buf.at[i], grads.at[i]
        back_hidden = mm(branch_ref[...], w[2], (1, 1))
        value, slope = gelu_parts(gate_ref[0])
        back_gate = (back_hidden * lin_ref[0] * slope).astype(bf16)
        back_linear = (back_hidden * value).astype(bf16)
        if units % 128 == 0:
            both = jnp.concatenate([back_gate, back_linear], 1)
            g[:2] = mm(both, norm_ref[...], (0, 0), bf16).reshape(2, units, dim)
            total[...] += mm(both, w[:2].reshape(2 * units, dim), (1, 0))
        else:
            for j, back in enumerate((back_gate, back_linear)):
                g[j] = mm(back, norm_ref[...], (0, 0), bf16)
                total[...] += mm(back, w[j], (1, 0))
        g[2] = mm(hid_ref[0], branch_ref[...], (0, 0), bf16)

        for k in range(nb):

            @pl.when(i == k)
            def _(k=k):
                for c in stores(k):
                    c.start()

        @pl.when(i == nb - 1)
        def _():
            own_out[...] = total[:half]
            oth_out[...] = total[half:]
            for k in range(nb):
                for c in stores(k):
                    c.wait()

    once = pl.BlockSpec((tokens, dim), lambda i: (0, 0))
    row = pl.BlockSpec((half, dim), lambda i: (0, 0))
    step = pl.BlockSpec((1, tokens, units), lambda i: (first + stride * i, 0, 0))
    any_space = pl.BlockSpec(memory_space=pl.ANY)
    made = pl.pallas_call(
        kernel,
        out_shape=[jax.ShapeDtypeStruct(a.shape, bf16) for a in flat]
        + [jax.ShapeDtypeStruct((half, dim), f32)] * 2,
        grid=(nb,),
        in_specs=[once, once, step, step, step] + [any_space] * len(flat) + [row, row] * has_before,
        out_specs=[any_space] * len(flat) + [row, row],
        scratch_shapes=[
            pltpu.VMEM((nb, 3, units, dim), bf16),
            pltpu.VMEM((nb, 3, units, dim), bf16),
            pltpu.VMEM((tokens, dim), f32),
            pltpu.SemaphoreType.DMA((nb, 2)),
            pltpu.SemaphoreType.DMA((nb, 2)),
        ],
        compiler_params=pltpu.CompilerParams(vmem_limit_bytes=VMEM_LIMIT),
        cost_estimate=BRIEF,
        name="ff_backward",
    )(norm_two, branch_two, gate_all, lin_all, hid_all, *flat, *(before or ()))
    made = list(made)
    grads = [tuple(made.pop(0) for _ in blk) for blk in blocks]
    return grads, made


def attention(action_qkv, prefix_kv, allowed):
    tokens, keys = action_qkv.shape[0], allowed.shape[0]
    n_pre = prefix_kv.shape[0]

    def kernel(q_ref, kv_ref, pre_ref, allowed_ref, out_ref, k_all, v_turned):
        @pl.when(pl.program_id(0) == 0)
        def _():
            k_all[:n_pre] = pre_ref[:, :HEAD_DIM]
            k_all[n_pre:] = kv_ref[:, :HEAD_DIM]
            v_turned[:, :n_pre] = pre_ref[:, HEAD_DIM:].T
            v_turned[:, n_pre:] = kv_ref[:, HEAD_DIM:].T

        scores = mm(k_all[...], q_ref[...], (1, 1)) * SCORE_SCALE
        scores = jnp.where(allowed_ref[...] != 0, scores, NEGATIVE)
        exp_scores = jnp.exp(scores - jnp.max(scores, axis=0, keepdims=True))
        soft = exp_scores / jnp.sum(exp_scores, axis=0, keepdims=True)
        out_ref[...] = mm(v_turned[...], soft.astype(bf16), (1, 0)).T.astype(bf16)

    return pl.pallas_call(
        kernel,
        out_shape=jax.ShapeDtypeStruct((tokens, QUERY_WIDTH), bf16),
        grid=(HEADS,),
        in_specs=[
            pl.BlockSpec((tokens, HEAD_DIM), lambda h: (0, h)),
            pl.BlockSpec((tokens, 2 * HEAD_DIM), lambda h: (0, HEADS // 2)),
            pl.BlockSpec((n_pre, 2 * HEAD_DIM), lambda h: (0, 0)),
            pl.BlockSpec((keys, tokens), lambda h: (0, 0)),
        ],
        out_specs=pl.BlockSpec((tokens, HEAD_DIM), lambda h: (0, h)),
        scratch_shapes=[pltpu.VMEM((keys, HEAD_DIM), bf16), pltpu.VMEM((HEAD_DIM, keys), bf16)],
        compiler_params=pltpu.CompilerParams(vmem_limit_bytes=VMEM_LIMIT),
        cost_estimate=BRIEF,
        name="attention",
    )(action_qkv, action_qkv, prefix_kv, allowed)


def attention_back(action_qkv, prefix_kv, allowed, back_mixed, first, heads, before):
    tokens, keys = action_qkv.shape[0], allowed.shape[0]
    n_pre = prefix_kv.shape[0]
    last = first + heads == HEADS
    n_before = len(before)

    def kernel(q_ref, kv_ref, pre_ref, allowed_ref, back_ref, *refs):
        before_refs, refs = refs[:n_before], refs[n_before:]
        if last:
            qkv_out, pre_out, k_sum, v_sum, k_all, v_all, k_turned = refs
        else:
            qkv_out, k_sum, v_sum, k_all, v_all, k_turned = refs
        h = pl.program_id(0)

        @pl.when(h == 0)
        def _():
            k_all[:n_pre] = pre_ref[:, :HEAD_DIM]
            k_all[n_pre:] = kv_ref[:, :HEAD_DIM]
            v_all[:n_pre] = pre_ref[:, HEAD_DIM:]
            v_all[n_pre:] = kv_ref[:, HEAD_DIM:]
            k_turned[...] = k_all[...].T
            if n_before:
                qkv_out[:, : first * HEAD_DIM] = before_refs[0][...]
                k_sum[...] = before_refs[1][...]
                v_sum[...] = before_refs[2][...]
            else:
                k_sum[...] = jnp.zeros_like(k_sum)
                v_sum[...] = jnp.zeros_like(v_sum)

        query, back = q_ref[...], back_ref[...]
        scores = mm(k_all[...], query, (1, 1)) * SCORE_SCALE
        scores = jnp.where(allowed_ref[...] != 0, scores, NEGATIVE)
        exp_scores = jnp.exp(scores - jnp.max(scores, axis=0, keepdims=True))
        soft = exp_scores / jnp.sum(exp_scores, axis=0, keepdims=True)
        v_sum[...] += mm(soft.astype(bf16), back, (1, 0))
        back_soft = mm(v_all[...], back, (1, 1))
        mean = jnp.sum(soft * back_soft, axis=0, keepdims=True)
        back_scores = (soft * (back_soft - mean)).astype(bf16)
        k_sum[...] += mm(back_scores, query, (1, 0))
        turned = mm(k_turned[...], back_scores, (1, 0)) * SCORE_SCALE
        at = pl.ds(pl.multiple_of((first + h) * HEAD_DIM, HEAD_DIM), HEAD_DIM)
        qkv_out[:, at] = turned.T.astype(bf16)

        if last:

            @pl.when(h == heads - 1)
            def _():
                pre_out[:, :HEAD_DIM] = (k_sum[:n_pre] * SCORE_SCALE).astype(bf16)
                pre_out[:, HEAD_DIM:] = v_sum[:n_pre].astype(bf16)
                keys_out = (k_sum[n_pre:] * SCORE_SCALE).astype(bf16)
                qkv_out[:, QUERY_WIDTH : QUERY_WIDTH + HEAD_DIM] = keys_out
                qkv_out[:, QUERY_WIDTH + HEAD_DIM :] = v_sum[n_pre:].astype(bf16)

    def once(shape):
        return pl.BlockSpec(shape, lambda h: (0, 0))

    sums = jax.ShapeDtypeStruct((keys, HEAD_DIM), f32)
    if last:
        out_shapes = [
            jax.ShapeDtypeStruct((tokens, QKV_WIDTH), bf16),
            jax.ShapeDtypeStruct((n_pre, 2 * HEAD_DIM), bf16),
        ]
        kept = [pltpu.VMEM(sums.shape, f32)] * 2
    else:
        out_shapes = [jax.ShapeDtypeStruct((tokens, heads * HEAD_DIM), bf16), sums, sums]
        kept = []
    return pl.pallas_call(
        kernel,
        out_shape=out_shapes,
        grid=(heads,),
        in_specs=[
            pl.BlockSpec((tokens, HEAD_DIM), lambda h: (0, first + h)),
            pl.BlockSpec((tokens, 2 * HEAD_DIM), lambda h: (0, HEADS // 2)),
            once((n_pre, 2 * HEAD_DIM)),
            once((keys, tokens)),
            pl.BlockSpec((tokens, HEAD_DIM), lambda h: (0, first + h)),
        ]
        + [once(v.shape) for v in before],
        out_specs=[once(o.shape) for o in out_shapes],
        scratch_shapes=kept
        + [
            pltpu.VMEM((keys, HEAD_DIM), bf16),
            pltpu.VMEM((keys, HEAD_DIM), bf16),
            pltpu.VMEM((HEAD_DIM, keys), bf16),
        ],
        compiler_params=pltpu.CompilerParams(vmem_limit_bytes=VMEM_LIMIT),
        cost_estimate=BRIEF,
        name="attention_back",
    )(action_qkv, action_qkv, prefix_kv, allowed, back_mixed, *before)


def mid_back(residual, back_final, back_own, back_oth, gain_row, out_weight):
    tokens, dim = residual.shape

    def kernel(res_ref, fin_ref, own_ref, oth_ref, gain_ref, weight_ref, attn_out, mixed_out, gain_out):
        v = res_ref[...]
        s = lax.rsqrt(jnp.mean(v * v, axis=-1, keepdims=True) + NORM_EPSILON)
        normed = v * s
        back = own_ref[...] + oth_ref[...]
        gain_out[...] = jnp.sum(back * normed, axis=0, keepdims=True)
        scaled = back * (1.0 + gain_ref[...])
        mean = jnp.mean(scaled * normed, axis=-1, keepdims=True)
        attn = (fin_ref[...] + s * (scaled - normed * mean)).astype(bf16)
        attn_out[...] = attn
        mixed_out[...] = mm(attn, weight_ref[...], (1, 0), bf16)

    return pl.pallas_call(
        kernel,
        out_shape=[
            jax.ShapeDtypeStruct((tokens, dim), bf16),
            jax.ShapeDtypeStruct((tokens, QUERY_WIDTH), bf16),
            jax.ShapeDtypeStruct((1, dim), f32),
        ],
        compiler_params=pltpu.CompilerParams(vmem_limit_bytes=VMEM_LIMIT),
        cost_estimate=BRIEF,
        name="mid_back",
    )(residual, back_final, back_own, back_oth, gain_row, out_weight)


def on_device(
    ring,
    prefix_in,
    action_in,
    target,
    valid_mask,
    prefix_ids,
    action_ids,
    action_blocks,
    learning_rate,
    prefix_weight,
    attention_weight,
    feedforward_weight,
    prefix_gains,
    action_gains,
    readout_weight,
    prefix_weight_moment,
    attention_weight_moment,
    feedforward_weight_moment,
    prefix_gains_moment,
    action_gains_moment,
    readout_weight_moment,
    prefix_weight_average,
    attention_weight_average,
    feedforward_weight_average,
    prefix_gains_average,
    action_gains_average,
    readout_weight_average,
):
    core = lax.axis_index("wide") % 2
    rows_a, width_a = attention_weight.shape
    width_p = 2 * prefix_weight.shape[1]
    rows_p = prefix_weight.shape[0]
    n_right, n_left = ring.n_right, ring.n_left
    order, swap = Order(), ring.to_core

    def by_core(v, size):
        cut = v.reshape(v.shape[0], ring.chips, 2, size)
        cut = [cut[:, :, c].reshape(v.shape[0], ring.chips * size) for c in (0, 1)]
        return jnp.where(core == 0, cut[0], cut[1]), jnp.where(core == 0, cut[1], cut[0])

    def in_order(mine, other, size):
        cut = [jnp.where(core == c, mine, other).reshape(-1, ring.chips, size) for c in (0, 1)]
        return jnp.stack(cut, 2).reshape(mine.shape[0], -1)

    prefix_bf = prefix_weight.astype(bf16)
    packed = jnp.concatenate(
        [attention_weight.astype(bf16), prefix_bf[:rows_a], prefix_bf[rows_a:]], axis=1
    )
    packed = order(packed)
    att = Gathering(ring, order, 0, True)
    att.start("right", packed)
    att.start("left", packed)
    ff_own = order(jnp.transpose(feedforward_weight, (1, 0, 2)).astype(bf16))
    prefix_rows = order(prefix_in[0])
    if rows_p % 128 == 0:
        halves = norm_by_core(ring, prefix_rows, prefix_gains, rows_p)
    else:
        halves = by_core(rms_norm(prefix_rows.astype(f32), prefix_gains[0]).astype(bf16), rows_p)
    pre_mine, pre_other = order(*halves)
    att.step("right", "left")
    action_rows = order(action_in[0]).astype(f32)
    action_norm = rms_norm(action_rows, action_gains[0]).astype(bf16)
    norm_mine, norm_other = order(*by_core(action_norm, rows_a))
    norm_oth = swap(norm_other)
    att.step("right", "left")
    att.settle(("right", 0), ("left", 0))
    ff = Gathering(ring, order, 1, False)
    while att.d["left"] < n_left:
        att.step("left", "right")
    ff.start("left", order(ff_own))
    while att.d["right"] < n_right:
        att.step("right")
    ff.start("right", order(ff_own))
    allowed = order(visible(prefix_ids[0], *order(action_ids[0], action_blocks[0])))
    norm_rows = order(jnp.concatenate([norm_mine, order(norm_oth)], 0))
    sides = [("right", d) for d in range(n_right)] + [("left", d) for d in range(n_left)]
    by_step = sorted(sides, key=lambda k: k[1])
    att.settle(*by_step[:-1])
    ff.step("right")
    att.settle(by_step[-1])
    ff.step("left")
    whole = repack(
        ring, [(packed,)] + [att.blocks[k] for k in sides], None, rows_a, width_a, width_p
    )
    qkv_own, out_own, pre_own = order(*whole)
    pre_oth, qkv_oth, out_oth = swap(pre_own), swap(qkv_own), swap(out_own)

    pre_oth, qkv_oth = order(pre_oth, qkv_oth)
    prefix_kv = (mm(pre_mine, pre_own, (1, 0)) + mm(pre_other, pre_oth, (1, 0))).astype(bf16)
    action_qkv = (mm(norm_mine, qkv_own, (1, 0)) + mm(norm_other, qkv_oth, (1, 0))).astype(bf16)
    prefix_kv, action_qkv = order(prefix_kv, action_qkv)
    ff.step("right")
    out_own, out_oth = order(out_own, out_oth)
    out_weight = order(interleave(ring, out_own, out_oth, rows_a))
    action_qkv = order(action_qkv)
    mixed_heads = order(attention(action_qkv, prefix_kv, allowed))
    mixed_oth = swap(mixed_heads)
    ff.step("right", "left")
    mixed_heads = order(mixed_heads)
    residual = action_rows + mm(mixed_heads, out_weight, (1, 1))
    tokens = residual.shape[0]
    hidden_norm = rms_norm(residual, action_gains[1]).astype(bf16)
    residual, hidden_norm = order(residual, hidden_norm)
    norm_two = order(jnp.concatenate([hidden_norm, swap(hidden_norm)], 0))

    def weights(key):
        return (ff_own,) if key[0] == "own" else ff.blocks[key]

    early = [("own", 0)] + [x for d in range(n_left - 1) for x in (("left", d), ("right", d))]
    late = [("right", n_left - 1), ("left", n_left - 1)]
    late += [("right", d) for d in range(n_left, n_right)]
    groups = [early, late]
    while ff.d["left"] < n_left - 1:
        ff.step("left", "right")
    kept, branch = [], None
    for group in groups:
        while any(k[0] != "own" and k not in ff.blocks for k in group):
            ff.step("right", "left")
        ff.settle(*group)
        norm_two = order(norm_two)
        *values, own_rows, other_rows = ff_forward(norm_two, [weights(k) for k in group], branch)
        branch = order(own_rows, other_rows)
        kept.append(values)
    final_stream = residual + branch[0] + swap(branch[1])
    final_norm = rms_norm(final_stream, action_gains[2])
    predicted = jnp.dot(final_norm, readout_weight, precision=HIGHEST)
    valid_rows = valid_mask[0].astype(f32)
    error_term = predicted - target[0]

    loss_sum = jnp.sum(valid_rows * error_term * error_term)
    own_count = jnp.sum(valid_rows)
    back_predicted = 2.0 * valid_rows * error_term
    back_final, grad_gain_final = norm_back(
        final_stream, action_gains[2], jnp.dot(back_predicted, readout_weight.T, precision=HIGHEST)
    )
    back_branch = back_final.astype(bf16)
    back_final, back_branch = order(back_final, back_branch)
    branch_two = order(jnp.concatenate([back_branch, swap(back_branch)], 0))
    ff_sum = Summing(ring, order, 1)
    grads, back = {}, None
    for group, values in zip(reversed(groups), reversed(kept)):
        turned = group[::-1]
        branch_two = order(branch_two)
        made, back = ff_backward(
            norm_two, branch_two, [weights(k) for k in turned], values, (len(group) - 1, -1), back
        )
        flat = order(*back, *[p for parts in made for p in parts])
        back, flat = flat[:2], list(flat[2:])
        for k, parts in zip(turned, made):
            grads[k] = tuple(flat.pop(0) for _ in parts)
            if k[0] != "own":
                ff_sum.put(k, grads[k])
        if group is late:
            ff_sum.step("left")
    back_oth = swap(back[1])
    ff_sum.step("right")
    back_own, back_oth = order(back[0], back_oth)
    back_attention, back_mixed, grad_gain_hidden = order(
        *mid_back(residual, back_final, back_own, back_oth, action_gains[1:2], out_weight)
    )
    part = order(
        *attention_back(action_qkv, prefix_kv, allowed, back_mixed, 0, HEADS // 2, ())
    )
    ff_sum.step("left")
    ff_sum.step("right")
    back_mixed, *part = order(back_mixed, *part)
    back_qkv, back_prefix_kv = order(
        *attention_back(action_qkv, prefix_kv, allowed, back_mixed, HEADS // 2, HEADS // 2, part)
    )
    qkv_back_oth = swap(back_qkv)

    attn_mine, attn_other = order(*by_core(order(back_attention), rows_a))
    attn_oth = swap(attn_other)
    other_side = order(mm(pre_other, order(back_prefix_kv), (0, 0), bf16))
    other_side = swap(other_side)
    attn_oth, mixed_oth = order(attn_oth, mixed_oth)
    grad_output = order(
        mm(
            jnp.concatenate([attn_mine, attn_oth], 0),
            jnp.concatenate([mixed_heads, mixed_oth], 0),
            (0, 0),
            bf16,
        )
    )
    ff_sum.step("right")
    qkv_back_oth = order(qkv_back_oth)
    grad_qkv = order(mm(norm_rows, jnp.concatenate([back_qkv, qkv_back_oth], 0), (0, 0), bf16))
    other_side = order(other_side)
    prefix_sum = mm(pre_mine, back_prefix_kv, (0, 0)) + other_side.astype(f32)
    prefix_sum = order(prefix_sum.astype(bf16))
    ff_sum.step("left")
    cut = repack(
        ring,
        [1] + [len(att.blocks[k]) for k in sides],
        [grad_qkv, grad_output, prefix_sum],
        rows_a,
        width_a,
        width_p,
    )
    flat = list(order(*[p for parts in cut for p in parts]))
    cut = [tuple(flat.pop(0) for _ in parts) for parts in cut]
    own_cut, cut = cut[0][0], dict(zip(sides, cut[1:]))
    att_sum = Summing(ring, order, 0)
    far_first = sorted(sides, key=lambda k: (-k[1], k[0] == "left"))
    for k in far_first:
        att_sum.put(k, cut[k])
    split_left = len(cut["left", 0]) == 2
    if split_left:
        att_sum.own(own_cut)
    ff_sum.step("right")

    def gain_gradient(mine, other, size, gain_row):
        sums = [jnp.sum(m, axis=0, keepdims=True) for m in (mine, other)]
        return in_order(*sums, size)[0] / (1.0 + gain_row)

    back_qkv, back_prefix_kv = order(back_qkv, back_prefix_kv)
    grad_gain_action = gain_gradient(
        mm(back_qkv, qkv_own, (1, 1)) * norm_mine.astype(f32),
        mm(back_qkv, qkv_oth, (1, 1)) * norm_other.astype(f32),
        rows_a,
        action_gains[0],
    )
    grad_gain_prefix = gain_gradient(
        mm(back_prefix_kv, pre_own, (1, 1)) * pre_mine.astype(f32),
        mm(back_prefix_kv, pre_oth, (1, 1)) * pre_other.astype(f32),
        rows_p,
        prefix_gains[0],
    )
    back_predicted, final_norm = order(back_predicted, final_norm)
    grad_readout = lax.dot_general(
        back_predicted, final_norm, (((0,), (0,)), ((), ())), precision=HIGHEST
    )
    dim = action_rows.shape[1]
    small = order(
        jnp.concatenate(
            [
                grad_readout,
                grad_gain_prefix.reshape(-1, dim),
                grad_gain_action[None],
                grad_gain_hidden,
                grad_gain_final[None],
                jnp.full((1, dim), loss_sum),
                jnp.full((1, dim), own_count),
            ],
            0,
        )
    )
    while ff_sum.left():
        ff_sum.step("right", "left")
    steps = ring.bits()
    moved = steps.pop(0)(small)
    for i, key in enumerate(far_first):
        att_sum.ready(key, *far_first[i + 1 : i + 2])
        if i == 0:
            ff_sum.land("right")
        att_sum.step(key[0])
        if i == 1:
            ff_sum.own(grads["own", 0][0])
        if moved is not None:
            small, moved = order(small, moved)
            small = order(small + moved)
            moved = steps.pop(0)(small) if steps else None
        if i == 3:
            ff_sum.close()
    while moved is not None:
        small, moved = order(small, moved)
        small = order(small + moved)
        moved = steps.pop(0)(small) if steps else None
    if not split_left:
        att_sum.own(own_cut)
    ff_total = ff_sum.result()
    act = grad_readout.shape[0]
    n_pre = grad_gain_prefix.shape[0] // dim
    count = small[act + n_pre + 4, 0]
    loss_value = small[act + n_pre + 3, 0] / count
    scale = 1.0 / count
    step_rate = learning_rate[0]
    third = order(
        *advance(
            feedforward_weight,
            feedforward_weight_moment,
            feedforward_weight_average,
            jnp.transpose(ff_total, (1, 0, 2)) * scale,
            step_rate,
        )
    )
    att_sum.close()
    packed_total = att_sum.result()
    first = advance(
        prefix_weight,
        prefix_weight_moment,
        prefix_weight_average,
        jnp.concatenate(
            [
                packed_total[:, width_a : width_a + width_p // 2],
                packed_total[:, width_a + width_p // 2 :],
            ],
            0,
        )
        * scale,
        step_rate,
    )
    second = advance(
        attention_weight,
        attention_weight_moment,
        attention_weight_average,
        packed_total[:, :width_a] * scale,
        step_rate,
    )
    fourth = advance(
        prefix_gains,
        prefix_gains_moment,
        prefix_gains_average,
        small[act : act + n_pre].reshape(1, -1) * scale,
        step_rate,
    )
    fifth = advance(
        action_gains,
        action_gains_moment,
        action_gains_average,
        small[act + n_pre : act + n_pre + 3] * scale,
        step_rate,
    )
    sixth = advance(
        readout_weight,
        readout_weight_moment,
        readout_weight_average,
        small[:act].T * scale,
        step_rate,
    )
    return (loss_value,) + tuple(
        group[i]
        for i in range(3)
        for group in (first, second, third, fourth, fifth, sixth)
    )


def solution(mesh):
    rows = P(("batch", "wide"))
    wide = P("wide")
    whole = P()
    weights = (wide, wide, wide, whole, whole, whole)
    return jax.shard_map(
        functools.partial(on_device, Ring(mesh.shape["wide"])),
        mesh=mesh,
        in_specs=(rows,) * 7 + (whole,) + weights * 3,
        out_specs=(whole,) + weights * 3,
        check_vma=False,
    )
```

```python
import functools
import math

import jax
import jax.numpy as jnp
import numpy as np
from jax import lax
from jax.experimental import pallas as pl
from jax.experimental.pallas import tpu as pltpu
from jax.sharding import PartitionSpec as P

HEADS = 8
HEAD_DIM = 256
QUERY_WIDTH = HEADS * HEAD_DIM
QKV_WIDTH = QUERY_WIDTH + 2 * HEAD_DIM
SCORE_SCALE = HEAD_DIM ** (-0.5)

NORM_EPSILON = 1e-06
MOMENTUM = 0.9
AVERAGE_DECAY = 0.8
NEGATIVE = -1e30

bf16 = jnp.bfloat16
f32 = jnp.float32
HIGHEST = lax.Precision.HIGHEST
MIB = 2**20
CUT = 512
PLAN = dict(
    packed=("a>R", "a>L"),
    norm=("aR", "aL", "aXR0", "aXL0"),
    action=("aR", "aL", "aSR0", "aSL0", "aXL1", "aR", "aXR1", "aL", "f>L", "aR", "aXR2", "f>R", "aXR3"),
    swapped=("aSR1", "aSL1", "aXL2", "aSR2", "aSL2"),
    seen=("fR", "fXR0", "fL", "aSR3"),
    assembled=(),
    half=(),
    half2=("fSR0", "fR", "fXR1"),
    woven=(),
    attended=(),
    attended2=("fR", "fSR1", "fXR2", "fL"),
    normed=(),
    early=("fR", "fSR2", "fXR3"),
    back_late=("xfirst", "xsecond"),
    back_early=("R", "L"),
    mid=(),
    back_a=(),
    core=("R", "xthird"),
    back_b=("rthird", "L", "xearly"),
    side=("q", "R", "o"),
    pair=(),
    cut=("xA", "AL"),
    gains=("R",),
    tail=(
        "s", "own", "R", "rA", "AR", "AL", "s", "AR", "close",
        "s", "AR", "s", "AL", "s", "AR", "AL", "AR", "Aown",
    ),
)
COST = dict(
    add=11, assemble=11, half_product=11, gain_sums=11, pair_gradient=11, side_gradient=11,
    disassemble=11, norm_by_core=11, ff_forward=9, ff_backward=0, attention=11, attention_back=8,
    mid_back=11, interleave=11,
)


def cost(name):
    return pl.CostEstimate(flops=10 ** COST[name], transcendentals=0, bytes_accessed=1)


def rms_norm(stream, gain_row):
    return (
        stream
        * lax.rsqrt(jnp.mean(stream * stream, axis=-1, keepdims=True) + NORM_EPSILON)
        * (1.0 + gain_row)
    )


def norm_back(stream, gain_row, cotangent):
    _, pull = jax.vjp(rms_norm, stream, gain_row)
    return pull(cotangent)


def gated_unit(gate_value, linear_value):
    return jax.nn.gelu(gate_value, approximate=True) * linear_value


def visible(prefix_ids, action_ids, block_flags):
    length = block_flags.shape[0]
    place = jnp.arange(length)
    upto = place[None, :] <= place[:, None]
    levels = jnp.sum(jnp.where(upto, block_flags[None, :], 0), axis=1)
    from_prefix = prefix_ids[:, None] == action_ids[None, :]
    from_action = (action_ids[:, None] == action_ids[None, :]) & (
        levels[:, None] <= levels[None, :]
    )
    return jnp.concatenate([from_prefix, from_action], axis=0).astype(jnp.int32)


def advance(weight, moment, average, gradient, step_rate):
    moment_next = MOMENTUM * moment + gradient
    weight_next = weight - step_rate * (gradient + MOMENTUM * moment_next)
    average_next = AVERAGE_DECAY * average + (1.0 - AVERAGE_DECAY) * weight_next
    return (weight_next, moment_next, average_next)


def mm(a, b, contract, out=f32):
    return lax.dot_general(
        a, b, (((contract[0],), (contract[1],)), ((), ())), preferred_element_type=f32
    ).astype(out)


class Order:
    def __init__(self):
        self.token = jnp.zeros((), jnp.int32)

    def __call__(self, *values):
        *values, self.token = lax.optimization_barrier((*values, self.token))
        return values[0] if len(values) == 1 else values


class Ring:
    def __init__(self, wide):
        chips = wide // 2
        self.wide, self.chips = wide, chips
        self.cycle = list(range(0, chips, 2)) + list(range(1, chips, 2))[::-1]
        ahead = [(self.cycle[i], self.cycle[(i + 1) % chips]) for i in range(chips)]
        self.right = [(2 * s + c, 2 * t + c) for s, t in ahead for c in (0, 1)]
        self.left = [(t, s) for s, t in self.right]
        self.core = [(w, w ^ 1) for w in range(wide)]
        self.n_right = chips // 2
        self.n_left = chips - 1 - self.n_right

    def to_right(self, v):
        return lax.ppermute(v, "wide", self.right)

    def to_left(self, v):
        return lax.ppermute(v, "wide", self.left)

    def to_core(self, v):
        return lax.ppermute(v, "wide", self.core)

    def to_peer(self, v):
        return lax.ppermute(v, "batch", [(0, 1), (1, 0)])

    def owners(self, w):
        here = self.cycle.index(w // 2)
        rights = [self.cycle[(here - d) % self.chips] for d in range(1, self.n_right + 1)]
        lefts = [self.cycle[(here + d) % self.chips] for d in range(1, self.n_left + 1)]
        return [w // 2] + rights + lefts

    def bits(self):
        k, steps = 1, [self.to_peer]
        while k < self.wide:
            pairs = [(w, w ^ k) for w in range(self.wide)]
            steps.append(functools.partial(lax.ppermute, axis_name="wide", perm=pairs))
            k *= 2
        return steps


def add(*terms, step=None):
    terms = [t if isinstance(t, tuple) else (t, 0, 1) for t in terms]
    shape = terms[0][0].shape
    cols = shape[-1]
    rows = math.prod(shape[:-1])
    if step is None:
        step = 128 if rows % 128 == 0 and rows > 128 else rows

    def kernel(*refs):
        refs[-1][...] = sum(r[...].astype(f32) for r in refs[:-1]).astype(bf16)

    def block(k, stride):
        return pl.BlockSpec((step, cols), lambda i: (stride * i + k, 0))

    return pl.pallas_call(
        kernel,
        out_shape=jax.ShapeDtypeStruct((rows, cols), bf16),
        grid=(rows // step,),
        in_specs=[block(k, stride) for _, k, stride in terms],
        out_specs=block(0, 1),
        compiler_params=pltpu.CompilerParams(vmem_limit_bytes=8 * MIB),
        cost_estimate=cost("add"),
        name="add",
    )(*[t.reshape(-1, cols) for t, _, _ in terms]).reshape(shape)


class SmallSum:
    def __init__(self, ring, order, rows):
        self.order, self.steps = order, ring.bits()
        self.total = order(jnp.concatenate(rows, 0))
        self.moved = self.steps.pop(0)(self.total)

    def step(self):
        if self.moved is None:
            return False
        total, moved = self.order(self.total, self.moved)
        self.total = self.order(total + moved)
        self.moved = self.steps.pop(0)(self.total) if self.steps else None
        return True


class Gathering:
    def __init__(self, ring, order, halves, axis, split_left):
        self.ring, self.order = ring, order
        self.halves, self.split_left = halves, split_left
        self.whole = jnp.concatenate(halves, axis)
        self.can = halves[0].shape[axis] % 16 == 0
        self.blocks, self.flying = {}, {}
        self.count = {"right": ring.n_right, "left": ring.n_left}
        self.d = {"right": 0, "left": 0}

    def cut(self, side):
        return self.can and (side == "right" or self.split_left)

    def start(self, side):
        self.send(side, self.order(self.halves[0] if self.cut(side) else self.whole))

    def send(self, side, v):
        self.flying[side] = self.ring.to_right(v) if side == "right" else self.ring.to_left(v)

    def land(self, *sides):
        sides = [x for x in sides if self.d[x] < self.count[x] and x in self.flying]
        if not sides:
            return
        came = self.order(*[self.flying[x] for x in sides])
        for side, v in zip(sides, came if len(sides) > 1 else [came]):
            self.blocks[side, self.d[side]] = (v,)
            self.d[side] += 1
            if self.d[side] < self.count[side]:
                self.send(side, v)

    def cross(self, *keys):
        for key in keys:
            if self.cut(key[0]) and len(self.blocks.get(key, (0, 0))) == 1:
                (v,) = self.blocks[key]
                v = self.order(v)
                self.blocks[key] = (v, self.ring.to_peer(v))

    def settle(self, *keys):
        for key in keys:
            if key in self.blocks:
                self.cross(key)
                self.blocks[key] = tuple(self.order(p) for p in self.blocks[key])


class Summing:
    def __init__(self, ring, order, axis, n_right):
        self.ring, self.order, self.axis = ring, order, axis
        self.parts, self.sends, self.spots, self.crossed = {}, {}, {}, {}
        self.came = {"right": None, "left": None}
        self.d = {"right": n_right - 1, "left": ring.chips - 2 - n_right}

    def put(self, parts, sends, spots):
        self.parts.update(parts)
        self.sends.update(sends)
        self.spots.update(spots)

    def cross(self, *names):
        for name in names:
            if name in self.sends and name not in self.crossed:
                self.crossed[name] = self.ring.to_peer(self.order(self.sends[name]))

    def ready(self, *names):
        for name in names:
            if name in self.crossed:
                self.crossed[name] = self.order(self.crossed[name])

    def step(self, *sides):
        for side in sides:
            d = self.d[side]
            if d < 0:
                continue
            terms = [self.parts[side, d]]
            terms += [self.came[side]] if self.came[side] is not None else []
            if (side, d) in self.spots:
                name, spot = self.spots[side, d]
                self.cross(name)
                *terms, self.crossed[name] = self.order(*terms, self.crossed[name])
                rows = math.prod(self.parts[side, d].shape[:-1])
                step = 128 if rows % 128 == 0 and rows > 128 else rows
                terms.append((self.crossed[name], spot * (rows // step), 1))
            else:
                terms = self.order(*terms)
                terms = list(terms) if isinstance(terms, (list, tuple)) else [terms]
            total = self.order(add(*terms)) if len(terms) > 1 else terms[0]
            self.came[side] = self.ring.to_left(total) if side == "right" else self.ring.to_right(total)
            self.d[side] = d - 1

    def land(self, side):
        self.came[side] = self.order(self.came[side])

    def left(self):
        return max(self.d.values()) + 1

    def own(self, halves):
        left = self.order(self.came["left"])
        half = halves[0].shape[self.axis]
        self.split = bool(self.spots)
        if self.split:
            stride = 2 if self.axis else 1
            self.rows = half
            self.mine = [halves[0], (left, 0, stride)]
            other = self.order(add(halves[1], (left, 1, stride), step=half))
            self.across = self.ring.to_peer(other)
        else:
            self.mine = [self.order(add(jnp.concatenate(halves, self.axis), left))]
            self.rows = None

    def close(self):
        self.came["right"] = self.order(self.came["right"])
        terms = self.mine + [self.came["right"]]
        if self.split:
            self.across = self.order(self.across)
            terms.append(self.across)
        self.total = self.order(add(*terms, step=self.rows))
        self.across = self.ring.to_peer(self.total)

    def result(self):
        me = lax.axis_index("batch")
        total, across = [v.astype(f32) for v in self.order(self.total, self.across)]
        if not self.split:
            return total + across
        return jnp.where(
            me == 0,
            jnp.concatenate([total, across], self.axis),
            jnp.concatenate([across, total], self.axis),
        )


def places(ring, counts, rows):
    table = np.zeros((2, ring.wide, 2, sum(counts)), np.int32)
    for me in (0, 1):
        for w in range(ring.wide):
            where, first = [], []
            for owner, n in zip(ring.owners(w), counts):
                where += [owner] * n
                first += [me * rows // 2, (1 - me) * rows // 2] if n == 2 else [0]
            table[me, w] = where, first
    return jnp.array(table)[lax.axis_index("batch"), lax.axis_index("wide")]


def assemble(ring, blocks, rows, width_a):
    counts = [len(b) for b in blocks]
    parts = [p for b in blocks for p in b]
    n = len(parts)
    table = places(ring, counts, rows)
    side_rows = rows * ring.chips
    pw = (parts[0].shape[1] - width_a) // 2
    shapes = ((side_rows, QKV_WIDTH), (side_rows, width_a - QKV_WIDTH), (2 * side_rows, pw))

    def kernel(table_ref, *refs):
        ins, (qkv, out, pre, sems) = refs[:n], refs[n:]
        copies = []

        def copy(i, start, width, to, row):
            size = parts[i].shape[0]
            target = to.at[pl.ds(pl.multiple_of(row, size), size), :]
            copies.append(
                pltpu.make_async_copy(ins[i].at[:, pl.ds(start, width)], target, sems.at[len(copies)])
            )

        for i in range(n):
            chip, first = table_ref[0, i], table_ref[1, i]
            copy(i, 0, QKV_WIDTH, qkv, chip * rows + first)
            copy(i, QKV_WIDTH, width_a - QKV_WIDTH, out, chip * rows + first)
            for j in (0, 1):
                copy(i, width_a + j * pw, pw, pre, (2 * chip + j) * rows + first)
        for c in copies:
            c.start()
        for c in copies:
            c.wait()

    return pl.pallas_call(
        kernel,
        out_shape=[jax.ShapeDtypeStruct(sh, bf16) for sh in shapes],
        grid_spec=pltpu.PrefetchScalarGridSpec(
            num_scalar_prefetch=1,
            grid=(1,),
            in_specs=[pl.BlockSpec(memory_space=pl.ANY)] * n,
            out_specs=[pl.BlockSpec(sh, lambda i, t: (0, 0)) for sh in shapes],
            scratch_shapes=[pltpu.SemaphoreType.DMA((4 * n,))],
        ),
        compiler_params=pltpu.CompilerParams(vmem_limit_bytes=16 * MIB),
        cost_estimate=cost("assemble"),
        name="assemble",
    )(table, *parts)


def interleave(ring, own, other, rows):
    core = (lax.axis_index("wide") % 2).reshape(1)

    def kernel(core_ref, own_ref, other_ref, out_ref, sems):
        copies = []
        for chip in range(ring.chips):
            for j, ref in enumerate((own_ref, other_ref)):
                side = core_ref[0] if j == 0 else 1 - core_ref[0]
                to = pl.ds(pl.multiple_of((2 * chip + side) * rows, rows), rows)
                copies.append(
                    pltpu.make_async_copy(
                        ref.at[pl.ds(chip * rows, rows), :], out_ref.at[to, :], sems.at[chip, j]
                    )
                )
        for c in copies:
            c.start()
        for c in copies:
            c.wait()

    shape = (2 * own.shape[0], own.shape[1])
    return pl.pallas_call(
        kernel,
        out_shape=jax.ShapeDtypeStruct(shape, bf16),
        grid_spec=pltpu.PrefetchScalarGridSpec(
            num_scalar_prefetch=1,
            grid=(1,),
            in_specs=[pl.BlockSpec(memory_space=pl.ANY)] * 2,
            out_specs=pl.BlockSpec(shape, lambda i, t: (0, 0)),
            scratch_shapes=[pltpu.SemaphoreType.DMA((ring.chips, 2))],
        ),
        compiler_params=pltpu.CompilerParams(vmem_limit_bytes=12 * MIB),
        cost_estimate=cost("interleave"),
        name="interleave",
    )(core, own, other)


def side_gradient(rows, cols, which=0):
    tokens, width = rows.shape[0], rows.shape[1] // 2

    def kernel(rows_ref, cols_ref, out_ref):
        out_ref[...] = mm(rows_ref[...], cols_ref[...], (0, 0), bf16)

    return pl.pallas_call(
        kernel,
        out_shape=jax.ShapeDtypeStruct((width, cols.shape[1]), bf16),
        grid=(1,),
        in_specs=[
            pl.BlockSpec((tokens, width), lambda i: (0, which)),
            pl.BlockSpec(cols.shape, lambda i: (0, 0)),
        ],
        out_specs=pl.BlockSpec((width, cols.shape[1]), lambda i: (0, 0)),
        compiler_params=pltpu.CompilerParams(vmem_limit_bytes=16 * MIB),
        cost_estimate=cost("side_gradient"),
        name="side_gradient",
    )(rows, cols)


def half_product(rows, side, weight, before):
    tokens, width = rows.shape[0], rows.shape[1] // 2
    cols = weight.shape[1]
    kind = f32 if before is None else bf16

    def kernel(rows_ref, weight_ref, *refs):
        out_ref = refs[-1]
        for c in range(cols // CUT):
            at = slice(c * CUT, (c + 1) * CUT)
            total = mm(rows_ref[...], weight_ref[:, at], (1, 0))
            out_ref[:, at] = (total if before is None else total + refs[0][:, at]).astype(kind)

    extra = [] if before is None else [before]
    return pl.pallas_call(
        kernel,
        out_shape=jax.ShapeDtypeStruct((tokens, cols), kind),
        grid=(1,),
        in_specs=[
            pl.BlockSpec((tokens, width), lambda i: (0, side)),
            pl.BlockSpec(weight.shape, lambda i: (0, 0)),
        ]
        + [pl.BlockSpec((tokens, cols), lambda i: (0, 0)) for _ in extra],
        out_specs=pl.BlockSpec((tokens, cols), lambda i: (0, 0)),
        compiler_params=pltpu.CompilerParams(vmem_limit_bytes=30 * MIB),
        cost_estimate=cost("half_product"),
        name="half_product",
    )(rows, weight, *extra)


def gain_sums(back, rows, own, other):
    tokens, width = rows.shape[0], rows.shape[1] // 2
    cols = own.shape[1]
    step = 256

    def kernel(back_ref, rows_ref, own_ref, other_ref, out_ref):
        @pl.when(pl.program_id(0) == 0)
        def _():
            out_ref[...] = jnp.zeros_like(out_ref)

        for side, ref in enumerate((own_ref, other_ref)):
            at = slice(side * width, (side + 1) * width)
            total = mm(back_ref[...], ref[...], (1, 1)) * rows_ref[:, at].astype(f32)
            out_ref[:, at] += jnp.sum(total, axis=0, keepdims=True)

    return pl.pallas_call(
        kernel,
        out_shape=jax.ShapeDtypeStruct((1, 2 * width), f32),
        grid=(tokens // step,),
        in_specs=[
            pl.BlockSpec((step, cols), lambda i: (i, 0)),
            pl.BlockSpec((step, 2 * width), lambda i: (i, 0)),
        ]
        + [pl.BlockSpec(w.shape, lambda i: (0, 0)) for w in (own, other)],
        out_specs=pl.BlockSpec((1, 2 * width), lambda i: (0, 0)),
        compiler_params=pltpu.CompilerParams(vmem_limit_bytes=24 * MIB),
        cost_estimate=cost("gain_sums"),
        name="gain_sums",
    )(back, rows, own, other)


def pair_gradient(rows, cols):
    width, step = rows[0].shape[1], 512

    def kernel(r0, r1, c0, c1, out_ref):
        out_ref[...] = (mm(r0[...], c0[...], (0, 0)) + mm(r1[...], c1[...], (0, 0))).astype(bf16)

    once = [pl.BlockSpec(r.shape, lambda i: (0, 0)) for r in rows]
    return pl.pallas_call(
        kernel,
        out_shape=jax.ShapeDtypeStruct((width, cols[0].shape[1]), bf16),
        grid=(cols[0].shape[1] // step,),
        in_specs=once + [pl.BlockSpec((c.shape[0], step), lambda i: (0, i)) for c in cols],
        out_specs=pl.BlockSpec((width, step), lambda i: (0, i)),
        compiler_params=pltpu.CompilerParams(vmem_limit_bytes=14 * MIB),
        cost_estimate=cost("pair_gradient"),
        name="pair_gradient",
    )(*rows, *cols)


def disassemble(ring, halved, norm_rows, qkv_back, pre_rel, back_prefix_kv, other_side, grad_output, rows):
    cuts = 2 if halved else 1
    size = rows // cuts
    table = places(ring, [cuts] * ring.chips, rows)
    spots, sizes = [], []
    for j in range(ring.chips):
        right = 1 <= j <= ring.n_right
        sizes.append(size if right else rows)
        if right and halved:
            spots += [(j, 0), (ring.chips, (j - 1) * size)]
        else:
            spots += [(j, k * size) for k in range(cuts)]
    if halved:
        sizes.append(ring.n_right * size)
    n = len(sizes)
    side_rows = rows * ring.chips
    pre_cols = back_prefix_kv.shape[1]
    out_cols = grad_output.shape[1]
    width = QKV_WIDTH + out_cols + 2 * pre_cols
    step = 512

    def kernel(table_ref, n0, n1, q0, q1, pre_ref, back_ref, side_ref, out_ref, *refs):
        parts, (qkv_sum, pre_sum, sems) = refs[:n], refs[n:]

        def copies(i, k):
            chip, first = table_ref[0, i], table_ref[1, i]
            part, top = spots[i]

            def piece(ref, row, at, w, j):
                source = ref.at[pl.ds(pl.multiple_of(row, size), size), :]
                target = parts[part].at[pl.ds(top, size), pl.ds(at, w)]
                return pltpu.make_async_copy(source, target, sems.at[i, j])

            if k == 0:
                return [piece(out_ref, chip * rows + first, QKV_WIDTH, out_cols, 0)]
            if k == 1:
                at = QKV_WIDTH + out_cols
                return [
                    piece(pre_sum, (2 * chip + j) * rows + first, at + j * pre_cols, pre_cols, 1 + j)
                    for j in (0, 1)
                ]
            return [piece(qkv_sum, chip * rows + first, 0, QKV_WIDTH, 3)]

        def start(k):
            for i in range(len(spots)):
                for c in copies(i, k):
                    c.start()

        start(0)
        total = mm(pre_ref[...], back_ref[...], (0, 0)) + side_ref[...].astype(f32)
        pre_sum[...] = total.astype(bf16)
        start(1)
        for c in range(QKV_WIDTH // step):
            at = slice(c * step, (c + 1) * step)
            total = mm(n0[...], q0[:, at], (0, 0)) + mm(n1[...], q1[:, at], (0, 0))
            qkv_sum[:, at] = total.astype(bf16)
        start(2)
        for i in range(len(spots)):
            for k in (0, 1, 2):
                for c in copies(i, k):
                    c.wait()

    def once(v):
        return pl.BlockSpec(v.shape, lambda i, t: (0, 0))

    tokens = pre_rel.shape[0]
    out = pl.pallas_call(
        kernel,
        out_shape=[jax.ShapeDtypeStruct((size, width), bf16) for size in sizes],
        grid_spec=pltpu.PrefetchScalarGridSpec(
            num_scalar_prefetch=1,
            grid=(1,),
            in_specs=[once(v) for v in (*norm_rows, *qkv_back)]
            + [pl.BlockSpec((tokens, 2 * side_rows), lambda i, t: (0, 0))]
            + [once(v) for v in (back_prefix_kv, other_side, grad_output)],
            out_specs=[pl.BlockSpec(memory_space=pltpu.HBM)] * n,
            scratch_shapes=[
                pltpu.VMEM((side_rows, QKV_WIDTH), bf16),
                pltpu.VMEM((2 * side_rows, pre_cols), bf16),
                pltpu.SemaphoreType.DMA((len(spots), 4)),
            ],
        ),
        compiler_params=pltpu.CompilerParams(vmem_limit_bytes=28 * MIB),
        cost_estimate=cost("disassemble"),
        name="disassemble",
    )(table, *norm_rows, *qkv_back, pre_rel, back_prefix_kv, other_side, grad_output)
    return out


def norm_by_core(ring, rows, gains, size):
    core = (lax.axis_index("wide") % 2).reshape(1)
    tokens, dim = rows.shape
    step = 128

    def kernel(core_ref, rows_ref, gains_ref, out_ref):
        v = rows_ref[...].astype(f32)
        normed = rms_norm(v, gains_ref[0]).astype(bf16)
        for swapped in (0, 1):

            @pl.when(core_ref[0] == swapped)
            def _(swapped=swapped):
                for chip in range(ring.chips):
                    for side in (0, 1):
                        at = (2 * chip + (side ^ swapped)) * size
                        to = side * (dim // 2) + chip * size
                        out_ref[:, to : to + size] = normed[:, at : at + size]

    return pl.pallas_call(
        kernel,
        out_shape=jax.ShapeDtypeStruct((tokens, dim), bf16),
        grid_spec=pltpu.PrefetchScalarGridSpec(
            num_scalar_prefetch=1,
            grid=(tokens // step,),
            in_specs=[
                pl.BlockSpec((step, dim), lambda i, t: (i, 0)),
                pl.BlockSpec((1, dim), lambda i, t: (0, 0)),
            ],
            out_specs=pl.BlockSpec((step, dim), lambda i, t: (i, 0)),
        ),
        compiler_params=pltpu.CompilerParams(vmem_limit_bytes=12 * MIB),
        cost_estimate=cost("norm_by_core"),
        name="norm_by_core",
    )(core, rows, gains)


def gelu_parts(v):
    c = math.sqrt(2.0 / math.pi)
    square = v * v
    t = jnp.tanh(c * v * (1.0 + 0.044715 * square))
    half = 0.5 * (1.0 + t)
    slope = half + 0.5 * v * (1.0 - t * t) * c * (1.0 + 3.0 * 0.044715 * square)
    return v * half, slope


def load_block(refs, buf, sems, k):
    at, made = 0, []
    for j, r in enumerate(refs):
        size = r.shape[1]
        made.append(pltpu.make_async_copy(r, buf.at[:, pl.ds(at, size), :], sems.at[k, j]))
        at += size
    return made


def ff_forward(norm_two, blocks, before):
    nb = len(blocks)
    flat = [a for blk in blocks for a in blk]
    tokens, dim = norm_two.shape
    units = sum(a.shape[1] for a in blocks[0])
    half = tokens // 2
    has_before = before is not None

    def kernel(norm_ref, *refs):
        refs = list(refs)
        ins = [[refs.pop(0) for _ in blk] for blk in blocks]
        if has_before:
            own_in, oth_in = refs.pop(0), refs.pop(0)
        gate_out, lin_out, hid_out, own_out, oth_out, buf, total, sems = refs
        i = pl.program_id(0)

        @pl.when(i == 0)
        def _():
            for k in range(nb):
                for c in load_block(ins[k], buf.at[k], sems, k):
                    c.start()
            if has_before:
                total[:half] = own_in[...]
                total[half:] = oth_in[...]
            else:
                total[...] = jnp.zeros_like(total)

        for k in range(nb):

            @pl.when(i == k)
            def _(k=k):
                for c in load_block(ins[k], buf.at[k], sems, k):
                    c.wait()

        w = buf.at[i]
        if units % 128 == 0:
            both = mm(norm_ref[...], w[:2].reshape(2 * units, dim), (1, 1))
            gate, linear = both[:, :units], both[:, units:]
        else:
            gate, linear = (mm(norm_ref[...], w[j], (1, 1)) for j in (0, 1))
        gate_out[0] = gate
        lin_out[0] = linear
        hidden = (gelu_parts(gate)[0] * linear).astype(bf16)
        hid_out[0] = hidden
        total[...] += mm(hidden, w[2], (1, 0))

        @pl.when(i == nb - 1)
        def _():
            own_out[...] = total[:half]
            oth_out[...] = total[half:]

    once = pl.BlockSpec((tokens, dim), lambda i: (0, 0))
    row = pl.BlockSpec((half, dim), lambda i: (0, 0))
    step = pl.BlockSpec((1, tokens, units), lambda i: (i, 0, 0))
    any_space = pl.BlockSpec(memory_space=pl.ANY)
    return pl.pallas_call(
        kernel,
        out_shape=[
            jax.ShapeDtypeStruct((nb, tokens, units), f32),
            jax.ShapeDtypeStruct((nb, tokens, units), f32),
            jax.ShapeDtypeStruct((nb, tokens, units), bf16),
            jax.ShapeDtypeStruct((half, dim), f32),
            jax.ShapeDtypeStruct((half, dim), f32),
        ],
        grid=(nb,),
        in_specs=[once] + [any_space] * len(flat) + [row, row] * has_before,
        out_specs=[step, step, step, row, row],
        scratch_shapes=[
            pltpu.VMEM((nb, 3, units, dim), bf16),
            pltpu.VMEM((tokens, dim), f32),
            pltpu.SemaphoreType.DMA((nb, 2)),
        ],
        compiler_params=pltpu.CompilerParams(vmem_limit_bytes=28 * MIB),
        cost_estimate=cost("ff_forward"),
        name="ff_forward",
    )(norm_two, *flat, *(before or ()))


def ff_backward(norm_two, branch_two, blocks, sends, kept, picks, before):
    nb = len(blocks)
    flat = [a for blk in blocks for a in blk]
    gate_all, lin_all, hid_all = kept
    tokens, dim = norm_two.shape
    units = sum(a.shape[1] for a in blocks[0])
    half = tokens // 2
    has_before = before is not None
    first, stride = picks

    def kernel(norm_ref, branch_ref, gate_ref, lin_ref, hid_ref, *refs):
        refs = list(refs)
        ins = [[refs.pop(0) for _ in blk] for blk in blocks]
        if has_before:
            own_in, oth_in = refs.pop(0), refs.pop(0)
        outs = [[refs.pop(0)] for _ in blocks]
        for keys in sends:
            ref = refs.pop(0)
            for spot, k in enumerate(keys):
                outs[k].append(ref.at[spot])
        own_out, oth_out, buf, grads, total, sems, out_sems = refs
        i = pl.program_id(0)

        def stores(k):
            at, made = 0, []
            for j, r in enumerate(outs[k]):
                size = r.shape[1]
                made.append(pltpu.make_async_copy(grads.at[k, :, pl.ds(at, size), :], r, out_sems.at[k, j]))
                at += size
            return made

        @pl.when(i == 0)
        def _():
            for k in range(nb):
                for c in load_block(ins[k], buf.at[k], sems, k):
                    c.start()
            if has_before:
                total[:half] = own_in[...]
                total[half:] = oth_in[...]
            else:
                total[...] = jnp.zeros_like(total)

        for k in range(nb):

            @pl.when(i == k)
            def _(k=k):
                for c in load_block(ins[k], buf.at[k], sems, k):
                    c.wait()

        w, g = buf.at[i], grads.at[i]
        back_hidden = mm(branch_ref[...], w[2], (1, 1))
        value, slope = gelu_parts(gate_ref[0])
        back_gate = (back_hidden * lin_ref[0] * slope).astype(bf16)
        back_linear = (back_hidden * value).astype(bf16)
        if units % 128 == 0:
            both = jnp.concatenate([back_gate, back_linear], 1)
            g[:2] = mm(both, norm_ref[...], (0, 0), bf16).reshape(2, units, dim)
            total[...] += mm(both, w[:2].reshape(2 * units, dim), (1, 0))
        else:
            for j, back in enumerate((back_gate, back_linear)):
                g[j] = mm(back, norm_ref[...], (0, 0), bf16)
                total[...] += mm(back, w[j], (1, 0))
        g[2] = mm(hid_ref[0], branch_ref[...], (0, 0), bf16)

        for k in range(nb):

            @pl.when(i == k)
            def _(k=k):
                for c in stores(k):
                    c.start()

        @pl.when(i == nb - 1)
        def _():
            own_out[...] = total[:half]
            oth_out[...] = total[half:]
            for k in range(nb):
                for c in stores(k):
                    c.wait()

    once = pl.BlockSpec((tokens, dim), lambda i: (0, 0))
    row = pl.BlockSpec((half, dim), lambda i: (0, 0))
    step = pl.BlockSpec((1, tokens, units), lambda i: (first + stride * i, 0, 0))
    any_space = pl.BlockSpec(memory_space=pl.ANY)
    hbm = pl.BlockSpec(memory_space=pltpu.HBM)
    made = pl.pallas_call(
        kernel,
        out_shape=[
            jax.ShapeDtypeStruct((3, units // (2 if any(k in x for x in sends) else 1), dim), bf16)
            for k in range(nb)
        ]
        + [jax.ShapeDtypeStruct((len(x), 3, units // 2, dim), bf16) for x in sends]
        + [jax.ShapeDtypeStruct((half, dim), f32)] * 2,
        grid=(nb,),
        in_specs=[once, once, step, step, step] + [any_space] * len(flat) + [row, row] * has_before,
        out_specs=[hbm] * (nb + len(sends)) + [row, row],
        scratch_shapes=[
            pltpu.VMEM((nb, 3, units, dim), bf16),
            pltpu.VMEM((nb, 3, units, dim), bf16),
            pltpu.VMEM((tokens, dim), f32),
            pltpu.SemaphoreType.DMA((nb, 2)),
            pltpu.SemaphoreType.DMA((nb, 2)),
        ],
        compiler_params=pltpu.CompilerParams(vmem_limit_bytes=42 * MIB),
        cost_estimate=cost("ff_backward"),
        name="ff_backward",
    )(norm_two, branch_two, gate_all, lin_all, hid_all, *flat, *(before or ()))
    made = list(made)
    return made[:nb], made[nb:-2], made[-2:]


def attention(action_qkv, prefix_kv, allowed, first, heads, before):
    tokens, keys = action_qkv.shape[0], allowed.shape[0]
    n_pre = prefix_kv.shape[0]

    def kernel(q_ref, kv_ref, pre_ref, allowed_ref, *refs):
        out_ref, k_all, v_turned = refs[-3:]
        h = pl.program_id(0)

        @pl.when(h == 0)
        def _():
            k_all[:n_pre] = pre_ref[:, :HEAD_DIM]
            k_all[n_pre:] = kv_ref[:, :HEAD_DIM]
            v_turned[:, :n_pre] = pre_ref[:, HEAD_DIM:].T
            v_turned[:, n_pre:] = kv_ref[:, HEAD_DIM:].T
            if before:
                out_ref[:, : first * HEAD_DIM] = refs[0][...]

        scores = mm(k_all[...], q_ref[...], (1, 1)) * SCORE_SCALE
        scores = jnp.where(allowed_ref[...] != 0, scores, NEGATIVE)
        exp_scores = jnp.exp(scores - jnp.max(scores, axis=0, keepdims=True))
        soft = exp_scores / jnp.sum(exp_scores, axis=0, keepdims=True)
        at = pl.ds(pl.multiple_of((first + h) * HEAD_DIM, HEAD_DIM), HEAD_DIM)
        out_ref[:, at] = mm(v_turned[...], soft.astype(bf16), (1, 0)).T.astype(bf16)

    width = (first + heads) * HEAD_DIM
    return pl.pallas_call(
        kernel,
        out_shape=jax.ShapeDtypeStruct((tokens, width), bf16),
        grid=(heads,),
        in_specs=[
            pl.BlockSpec((tokens, HEAD_DIM), lambda h: (0, first + h)),
            pl.BlockSpec((tokens, 2 * HEAD_DIM), lambda h: (0, HEADS // 2)),
            pl.BlockSpec((n_pre, 2 * HEAD_DIM), lambda h: (0, 0)),
            pl.BlockSpec((keys, tokens), lambda h: (0, 0)),
        ]
        + [pl.BlockSpec(v.shape, lambda h: (0, 0)) for v in before],
        out_specs=pl.BlockSpec((tokens, width), lambda h: (0, 0)),
        scratch_shapes=[pltpu.VMEM((keys, HEAD_DIM), bf16), pltpu.VMEM((HEAD_DIM, keys), bf16)],
        compiler_params=pltpu.CompilerParams(vmem_limit_bytes=24 * MIB),
        cost_estimate=cost("attention"),
        name="attention",
    )(action_qkv, action_qkv, prefix_kv, allowed, *before)


def attention_back(action_qkv, prefix_kv, allowed, back_mixed, first, heads, before):
    tokens, keys = action_qkv.shape[0], allowed.shape[0]
    n_pre = prefix_kv.shape[0]
    last = first + heads == HEADS
    n_before = len(before)

    def kernel(q_ref, kv_ref, pre_ref, allowed_ref, back_ref, *refs):
        before_refs, refs = refs[:n_before], refs[n_before:]
        if last:
            qkv_out, pre_out, k_sum, v_sum, k_all, v_all, k_turned = refs
        else:
            qkv_out, k_sum, v_sum, k_all, v_all, k_turned = refs
        h = pl.program_id(0)

        @pl.when(h == 0)
        def _():
            k_all[:n_pre] = pre_ref[:, :HEAD_DIM]
            k_all[n_pre:] = kv_ref[:, :HEAD_DIM]
            v_all[:n_pre] = pre_ref[:, HEAD_DIM:]
            v_all[n_pre:] = kv_ref[:, HEAD_DIM:]
            k_turned[...] = k_all[...].T
            if n_before:
                qkv_out[:, : first * HEAD_DIM] = before_refs[0][...]
                k_sum[...] = before_refs[1][...]
                v_sum[...] = before_refs[2][...]
            else:
                k_sum[...] = jnp.zeros_like(k_sum)
                v_sum[...] = jnp.zeros_like(v_sum)

        query, back = q_ref[...], back_ref[...]
        scores = mm(k_all[...], query, (1, 1)) * SCORE_SCALE
        scores = jnp.where(allowed_ref[...] != 0, scores, NEGATIVE)
        exp_scores = jnp.exp(scores - jnp.max(scores, axis=0, keepdims=True))
        soft = exp_scores / jnp.sum(exp_scores, axis=0, keepdims=True)
        v_sum[...] += mm(soft.astype(bf16), back, (1, 0))
        back_soft = mm(v_all[...], back, (1, 1))
        mean = jnp.sum(soft * back_soft, axis=0, keepdims=True)
        back_scores = (soft * (back_soft - mean)).astype(bf16)
        k_sum[...] += mm(back_scores, query, (1, 0))
        turned = mm(k_turned[...], back_scores, (1, 0)) * SCORE_SCALE
        at = pl.ds(pl.multiple_of((first + h) * HEAD_DIM, HEAD_DIM), HEAD_DIM)
        qkv_out[:, at] = turned.T.astype(bf16)

        if last:

            @pl.when(h == heads - 1)
            def _():
                pre_out[:, :HEAD_DIM] = (k_sum[:n_pre] * SCORE_SCALE).astype(bf16)
                pre_out[:, HEAD_DIM:] = v_sum[:n_pre].astype(bf16)
                keys_out = (k_sum[n_pre:] * SCORE_SCALE).astype(bf16)
                qkv_out[:, QUERY_WIDTH : QUERY_WIDTH + HEAD_DIM] = keys_out
                qkv_out[:, QUERY_WIDTH + HEAD_DIM :] = v_sum[n_pre:].astype(bf16)

    def once(shape):
        return pl.BlockSpec(shape, lambda h: (0, 0))

    sums = jax.ShapeDtypeStruct((keys, HEAD_DIM), f32)
    if last:
        out_shapes = [
            jax.ShapeDtypeStruct((tokens, QKV_WIDTH), bf16),
            jax.ShapeDtypeStruct((n_pre, 2 * HEAD_DIM), bf16),
        ]
        kept = [pltpu.VMEM(sums.shape, f32)] * 2
    else:
        out_shapes = [jax.ShapeDtypeStruct((tokens, heads * HEAD_DIM), bf16), sums, sums]
        kept = []
    return pl.pallas_call(
        kernel,
        out_shape=out_shapes,
        grid=(heads,),
        in_specs=[
            pl.BlockSpec((tokens, HEAD_DIM), lambda h: (0, first + h)),
            pl.BlockSpec((tokens, 2 * HEAD_DIM), lambda h: (0, HEADS // 2)),
            once((n_pre, 2 * HEAD_DIM)),
            once((keys, tokens)),
            pl.BlockSpec((tokens, HEAD_DIM), lambda h: (0, first + h)),
        ]
        + [once(v.shape) for v in before],
        out_specs=[once(o.shape) for o in out_shapes],
        scratch_shapes=kept
        + [
            pltpu.VMEM((keys, HEAD_DIM), bf16),
            pltpu.VMEM((keys, HEAD_DIM), bf16),
            pltpu.VMEM((HEAD_DIM, keys), bf16),
        ],
        compiler_params=pltpu.CompilerParams(vmem_limit_bytes=28 * MIB),
        cost_estimate=cost("attention_back"),
        name="attention_back",
    )(action_qkv, action_qkv, prefix_kv, allowed, back_mixed, *before)


def mid_back(residual, back_final, back_own, back_oth, gain_row, out_weight):
    tokens, dim = residual.shape

    def kernel(res_ref, fin_ref, own_ref, oth_ref, gain_ref, weight_ref, attn_out, mixed_out, gain_out):
        v = res_ref[...]
        s = lax.rsqrt(jnp.mean(v * v, axis=-1, keepdims=True) + NORM_EPSILON)
        normed = v * s
        back = own_ref[...] + oth_ref[...]
        gain_out[...] = jnp.sum(back * normed, axis=0, keepdims=True)
        scaled = back * (1.0 + gain_ref[...])
        mean = jnp.mean(scaled * normed, axis=-1, keepdims=True)
        attn = (fin_ref[...] + s * (scaled - normed * mean)).astype(bf16)
        attn_out[...] = attn
        mixed_out[...] = mm(attn, weight_ref[...], (1, 0), bf16)

    return pl.pallas_call(
        kernel,
        out_shape=[
            jax.ShapeDtypeStruct((tokens, dim), bf16),
            jax.ShapeDtypeStruct((tokens, QUERY_WIDTH), bf16),
            jax.ShapeDtypeStruct((1, dim), f32),
        ],
        compiler_params=pltpu.CompilerParams(vmem_limit_bytes=22 * MIB),
        cost_estimate=cost("mid_back"),
        name="mid_back",
    )(residual, back_final, back_own, back_oth, gain_row, out_weight)


def on_device(
    ring,
    prefix_in,
    action_in,
    target,
    valid_mask,
    prefix_ids,
    action_ids,
    action_blocks,
    learning_rate,
    prefix_weight,
    attention_weight,
    feedforward_weight,
    prefix_gains,
    action_gains,
    readout_weight,
    prefix_weight_moment,
    attention_weight_moment,
    feedforward_weight_moment,
    prefix_gains_moment,
    action_gains_moment,
    readout_weight_moment,
    prefix_weight_average,
    attention_weight_average,
    feedforward_weight_average,
    prefix_gains_average,
    action_gains_average,
    readout_weight_average,
):
    core = lax.axis_index("wide") % 2
    rows_a, width_a = attention_weight.shape
    width_p = 2 * prefix_weight.shape[1]
    rows_p = prefix_weight.shape[0]
    n_right, n_left = ring.n_right, ring.n_left
    order, swap = Order(), ring.to_core

    def by_core(v, size):
        cut = v.reshape(v.shape[0], ring.chips, 2, size)
        cut = [cut[:, :, c].reshape(v.shape[0], ring.chips * size) for c in (0, 1)]
        return jnp.where(core == 0, cut[0], cut[1]), jnp.where(core == 0, cut[1], cut[0])

    def in_order(v, size):
        cut = v.reshape(2, ring.chips, size)
        return jnp.where(core == 0, cut, cut[::-1]).transpose(1, 0, 2).reshape(-1)

    def halves_of(v, axis):
        half = v.shape[axis] // 2
        if half % 16:
            return jnp.split(v, 2, axis)
        me = lax.axis_index("batch")
        return [lax.dynamic_slice_in_dim(v, at * half, half, axis) for at in (me, 1 - me)]

    prefix_bf = prefix_weight.astype(bf16)
    packed = jnp.concatenate(
        [attention_weight.astype(bf16), prefix_bf[:rows_a], prefix_bf[rows_a:]], axis=1
    )
    sides = [("right", d) for d in range(n_right)] + [("left", d) for d in range(n_left)]
    packed_halves = order(*halves_of(packed, 0))
    att = Gathering(ring, order, packed_halves, 0, True)
    ff_halves = order(*halves_of(jnp.transpose(feedforward_weight, (1, 0, 2)).astype(bf16), 1))
    ff = Gathering(ring, order, ff_halves, 1, False)
    side_of = {"R": "right", "L": "left"}

    def serve(step):
        for word in PLAN[step]:
            chain, what = {"a": att, "f": ff}[word[0]], word[1]
            if what == ">":
                chain.start(side_of[word[2]])
            elif what in side_of:
                chain.land(side_of[what])
            else:
                key = (side_of[word[2]], int(word[3]))
                (chain.cross if what == "X" else chain.settle)(key)

    serve("packed")
    ff.whole = order(ff.whole)
    own_parts = packed_halves if att.can else (packed,)
    prefix_rows = order(prefix_in[0])
    if rows_p % 128 == 0:
        pre_rel = order(norm_by_core(ring, prefix_rows, prefix_gains, rows_p))
    else:
        normed = rms_norm(prefix_rows.astype(f32), prefix_gains[0]).astype(bf16)
        pre_rel = order(jnp.concatenate(by_core(normed, rows_p), 1))
    serve("norm")
    action_rows = order(action_in[0]).astype(f32)
    action_norm = rms_norm(action_rows, action_gains[0]).astype(bf16)
    norm_mine, norm_other = order(*by_core(action_norm, rows_a))
    serve("action")
    norm_oth = order(swap(order(norm_other)))
    norm_rel = order(jnp.concatenate([norm_mine, norm_other], 1))
    serve("swapped")
    allowed = order(visible(prefix_ids[0], *order(action_ids[0], action_blocks[0])))
    serve("seen")
    while any(att.d[x] < att.count[x] for x in att.d):
        att.land("right", "left")
    att.settle(*[k for k in sides if len(att.blocks[k]) == 1])
    blocks = [own_parts] + [att.blocks[k] for k in sides]
    qkv_own, out_own, pre_own = order(*assemble(ring, blocks, rows_a, width_a))
    pre_oth, qkv_oth = swap(pre_own), swap(qkv_own)
    serve("assembled")

    prefix_kv = order(half_product(pre_rel, 0, order(pre_own), None))
    action_qkv = order(half_product(norm_rel, 0, order(qkv_own), None))
    serve("half")
    pre_oth, qkv_oth, out_own = order(pre_oth, qkv_oth, out_own)
    out_oth = swap(out_own)
    prefix_kv = order(half_product(pre_rel, 1, order(pre_oth), prefix_kv))
    action_qkv = order(half_product(norm_rel, 1, order(qkv_oth), action_qkv))
    serve("half2")
    out_own, out_oth = order(out_own, out_oth)
    out_weight = order(interleave(ring, out_own, out_oth, rows_a))
    serve("woven")
    action_qkv = order(action_qkv)
    part = order(attention(action_qkv, prefix_kv, allowed, 0, HEADS // 2, ()))
    serve("attended")
    part = order(part)
    mixed_heads = order(
        attention(action_qkv, prefix_kv, allowed, HEADS // 2, HEADS // 2, (part,))
    )
    mixed_oth = swap(mixed_heads)
    serve("attended2")
    mixed_heads = order(mixed_heads)
    residual = action_rows + mm(mixed_heads, out_weight, (1, 1))
    tokens = residual.shape[0]
    hidden_norm = rms_norm(residual, action_gains[1]).astype(bf16)
    residual, hidden_norm, mixed_oth = order(residual, hidden_norm, mixed_oth)
    norm_two = order(jnp.concatenate([hidden_norm, order(swap(hidden_norm))], 0))
    serve("normed")

    def weights(key):
        return (ff.whole,) if key[0] == "own" else ff.blocks[key]

    early = [("own", 0)] + [x for d in range(n_left - 1) for x in (("left", d), ("right", d))]
    late = [("right", n_left - 1), ("left", n_left - 1)]
    late += [("right", d) for d in range(n_left, n_right)]
    groups = [early, late]
    kept, branch = [], None
    for group in groups:
        for side, d in group:
            while side != "own" and ff.d[side] <= d:
                ff.land(side)
        ff.cross(*[k for k in group if k[0] != "own"])
        ff.settle(*[k for k in group if len(ff.blocks.get(k, ())) == 2])
        norm_two = order(norm_two)
        *values, own_rows, other_rows = ff_forward(norm_two, [weights(k) for k in group], branch)
        branch = order(own_rows, other_rows)
        kept.append(values)
        if group is early:
            serve("early")
    final_stream = residual + branch[0] + swap(branch[1])
    final_norm = rms_norm(final_stream, action_gains[2])
    predicted = jnp.dot(final_norm, readout_weight, precision=HIGHEST)
    valid_rows = valid_mask[0].astype(f32)
    error_term = predicted - target[0]

    loss_sum = jnp.sum(valid_rows * error_term * error_term)
    own_count = jnp.sum(valid_rows)
    back_predicted = 2.0 * valid_rows * error_term
    back_final, grad_gain_final = norm_back(
        final_stream, action_gains[2], jnp.dot(back_predicted, readout_weight.T, precision=HIGHEST)
    )
    back_branch = back_final.astype(bf16)
    back_final, back_branch = order(back_final, back_branch)
    dim = action_rows.shape[1]
    branch_two = order(jnp.concatenate([back_branch, swap(back_branch)], 0))
    grad_readout = lax.dot_general(
        back_predicted, final_norm, (((0,), (0,)), ((), ())), precision=HIGHEST
    )
    small_rows = order(
        grad_readout,
        grad_gain_final[None],
        jnp.full((1, dim), loss_sum),
        jnp.full((1, dim), own_count),
    )
    n_back = n_right + (n_left > 1)
    ff_sum = Summing(ring, order, 1, n_back)

    def way_back(key):
        side, d = key
        return ("right", ring.chips - 2 - d) if side == "left" and ring.chips - 2 - d < n_back else key

    own_key, back = ("own", 0), None
    att_sum = Summing(ring, order, 0, n_right)
    small_sum, swapped = None, {}

    def serve_back(step):
        nonlocal small_sum
        for word in PLAN[step]:
            chain, rest = (att_sum, word[1:]) if word[0] == "A" else (ff_sum, word)
            if word in ("q", "o"):
                if word in swapped:
                    swapped[word] = order(swapped[word])
            elif word == "Aown":
                while att_sum.d["left"] >= 0:
                    att_sum.step("left")
                att_sum.own(jnp.split(cut[0], 2, 0))
            elif rest in side_of:
                side = side_of[rest]
                if (side, chain.d[side]) in chain.parts:
                    chain.step(side)
            elif rest == "own":
                while ff_sum.d["left"] >= 0:
                    ff_sum.step("left")
                own_grads = [ff_sum.parts[own_key]]
                if ff.can:
                    own_grads.append(ff_sum.sends["own"].reshape(own_grads[0].shape))
                else:
                    own_grads = jnp.split(own_grads[0], 2, 1)
                ff_sum.own(own_grads)
            elif rest == "close":
                while ff_sum.d["right"] >= 0:
                    ff_sum.step("right")
                ff_sum.close()
            elif rest == "s":
                if small_sum is None:
                    small_sum = SmallSum(ring, order, small_rows)
                else:
                    small_sum.step()
            else:
                chain = att_sum if rest[1:] == "A" else ff_sum
                name = "all" if rest[1:] == "A" else rest[1:]
                (chain.cross if rest[0] == "x" else chain.ready)(name)

    for name, group, values in (("late", late, kept[1]), ("early", early, kept[0])):
        turned = [way_back(k) for k in group[::-1]]
        rights = sorted((k for k in turned if k[0] == "right"), key=lambda k: -k[1])
        if not ff.can:
            lists = {}
        elif name == "late":
            lists = {"first": rights[:1], "second": rights[1:2], "third": rights[2:]}
        else:
            lists = {"early": rights, "own": [own_key]}
        lists = {k: v for k, v in lists.items() if v}
        branch_two = order(branch_two)
        made, sent, back = ff_backward(
            norm_two,
            branch_two,
            [weights(k) for k in group[::-1]],
            [[turned.index(k) for k in keys] for keys in lists.values()],
            values,
            (len(group) - 1, -1),
            back,
        )
        flat = list(order(*back, *made, *sent))
        back, made, sent = flat[:2], flat[2 : 2 + len(turned)], flat[2 + len(turned) :]
        ff_sum.put(
            dict(zip(turned, made)),
            dict(zip(lists, sent)),
            {k: (n, i) for n, keys in lists.items() for i, k in enumerate(keys)},
        )
        if name == "late":
            serve_back("back_late")
    back_oth = swap(back[1])
    serve_back("back_early")
    back_own, back_oth = order(back[0], back_oth)
    back_attention, back_mixed, grad_gain_hidden = order(
        *mid_back(residual, back_final, back_own, back_oth, action_gains[1:2], out_weight)
    )
    serve_back("mid")
    back_mixed = order(back_mixed)
    part = order(
        *attention_back(action_qkv, prefix_kv, allowed, back_mixed, 0, HEADS // 2, ())
    )
    serve_back("back_a")
    attn_mine, attn_other = order(*by_core(order(back_attention), rows_a))
    attn_oth = swap(attn_other)
    serve_back("core")
    back_mixed, attn_oth, *part = order(back_mixed, attn_oth, *part)
    back_qkv, back_prefix_kv = order(
        *attention_back(action_qkv, prefix_kv, allowed, back_mixed, HEADS // 2, HEADS // 2, part)
    )
    swapped["q"] = swap(back_qkv)
    serve_back("back_b")

    swapped["o"] = swap(order(side_gradient(pre_rel, order(back_prefix_kv), 1)))
    serve_back("side")
    grad_output = order(pair_gradient((attn_mine, attn_oth), order(mixed_heads, mixed_oth)))
    serve_back("pair")
    cut = order(
        *disassemble(
            ring,
            att.can,
            (norm_mine, norm_oth),
            (back_qkv, order(swapped["q"])),
            pre_rel,
            back_prefix_kv,
            order(swapped["o"]),
            order(grad_output),
            rows_a,
        )
    )
    att_sum.put(
        dict(zip(sides, cut[1:])),
        {"all": cut[ring.chips]} if att.can else {},
        {("right", d): ("all", d) for d in range(n_right)} if att.can else {},
    )
    serve_back("cut")
    back_qkv, back_prefix_kv = order(back_qkv, back_prefix_kv)
    sums = order(
        gain_sums(back_qkv, norm_rel, qkv_own, qkv_oth),
        gain_sums(back_prefix_kv, pre_rel, pre_own, pre_oth),
    )
    grad_gain_action = in_order(sums[0][0], rows_a) / (1.0 + action_gains[0])
    grad_gain_prefix = in_order(sums[1][0], rows_p) / (1.0 + prefix_gains[0])
    late_rows = order(grad_gain_prefix.reshape(-1, dim), grad_gain_action[None], grad_gain_hidden)
    small_rows = [*small_rows, *late_rows]
    serve_back("gains")
    serve_back("tail")
    while att_sum.d["right"] >= 0:
        att_sum.step("right")
    if small_sum is None:
        small_sum = SmallSum(ring, order, small_rows)
    while small_sum.step():
        pass
    ff_total = ff_sum.result()
    small = small_sum.total
    act = grad_readout.shape[0]
    n_pre = grad_gain_prefix.shape[0] // dim
    count = small[act + 2, 0]
    loss_value = small[act + 1, 0] / count
    scale = 1.0 / count
    step_rate = learning_rate[0]
    third = order(
        *advance(
            feedforward_weight,
            feedforward_weight_moment,
            feedforward_weight_average,
            jnp.transpose(ff_total, (1, 0, 2)) * scale,
            step_rate,
        )
    )
    att_sum.close()
    packed_total = att_sum.result()
    first = advance(
        prefix_weight,
        prefix_weight_moment,
        prefix_weight_average,
        jnp.concatenate(
            [
                packed_total[:, width_a : width_a + width_p // 2],
                packed_total[:, width_a + width_p // 2 :],
            ],
            0,
        )
        * scale,
        step_rate,
    )
    second = advance(
        attention_weight,
        attention_weight_moment,
        attention_weight_average,
        packed_total[:, :width_a] * scale,
        step_rate,
    )
    fourth = advance(
        prefix_gains,
        prefix_gains_moment,
        prefix_gains_average,
        small[act + 3 : act + 3 + n_pre].reshape(1, -1) * scale,
        step_rate,
    )
    fifth = advance(
        action_gains,
        action_gains_moment,
        action_gains_average,
        jnp.concatenate([small[act + 3 + n_pre :], small[act : act + 1]], 0) * scale,
        step_rate,
    )
    sixth = advance(
        readout_weight,
        readout_weight_moment,
        readout_weight_average,
        small[:act].T * scale,
        step_rate,
    )
    loss_value = loss_value + order.token.astype(f32)
    return (loss_value,) + tuple(
        group[i]
        for i in range(3)
        for group in (first, second, third, fourth, fifth, sixth)
    )


def solution(mesh):
    rows = P(("batch", "wide"))
    wide = P("wide")
    whole = P()
    weights = (wide, wide, wide, whole, whole, whole)
    return jax.shard_map(
        functools.partial(on_device, Ring(mesh.shape["wide"])),
        mesh=mesh,
        in_specs=(rows,) * 7 + (whole,) + weights * 3,
        out_specs=(whole,) + weights * 3,
        check_vma=False,
    )
```

```python
import functools
import math

import jax
import jax.numpy as jnp
import numpy as np
from jax import lax
from jax.experimental import pallas as pl
from jax.experimental.pallas import tpu as pltpu
from jax.sharding import PartitionSpec as P

HEADS = 8
HEAD_DIM = 256
QUERY_WIDTH = HEADS * HEAD_DIM
QKV_WIDTH = QUERY_WIDTH + 2 * HEAD_DIM
SCORE_SCALE = HEAD_DIM ** (-0.5)

NORM_EPSILON = 1e-06
MOMENTUM = 0.9
AVERAGE_DECAY = 0.8
NEGATIVE = -1e30

bf16 = jnp.bfloat16
f32 = jnp.float32
HIGHEST = lax.Precision.HIGHEST
MIB = 2**20
CUT = 512
PLAN = dict(
    norm=("aR", "aL", "aXR0", "aXL0", "aR"),
    action=("aL", "aSL0", "aXL1", "aR", "aXR1", "aSR0", "aL", "f>L", "aSL1", "aR", "aXR2", "f>R", "aXR3"),
    swapped=("aSR1", "aXL2", "aSR2", "aSL2"),
    seen=("fR", "fXR0", "fL", "aSR3"),
    assembled=(),
    half=(),
    half2=("fSR0", "fR", "fXR1"),
    woven=(),
    attended=(),
    attended2=("fR", "fSR1", "fXR2", "fL"),
    normed=(),
    early=("fR", "fSR2", "fXR3"),
    back_late=("xfirst", "xsecond"),
    back_early=("R", "L"),
    mid=(),
    back_a=(),
    core=("R", "xearly", "xthird"),
    back_b=("rthird", "L"),
    side=("q", "R", "o"),
    pair=(),
    cut=("xA", "AL"),
    gains=("R",),
    tail=(
        "s", "own", "R", "rA", "AR", "s", "AL", "s", "AR",
        "AL", "close", "s", "AR", "s", "AR", "AL", "AR", "Aown",
    ),
)
COST = dict(
    add=11, assemble=11, half_product=11, gain_sums=11, pair_gradient=11, side_gradient=11,
    disassemble=11, norm_by_core=11, ff_forward=9, ff_backward=0, attention=11, attention_back=8,
    mid_back=8, interleave=11, readout_loss=11,
)


def cost(name):
    return pl.CostEstimate(flops=10 ** COST[name], transcendentals=0, bytes_accessed=1)


def rms_norm(stream, gain_row):
    return (
        stream
        * lax.rsqrt(jnp.mean(stream * stream, axis=-1, keepdims=True) + NORM_EPSILON)
        * (1.0 + gain_row)
    )


def norm_back(stream, gain_row, cotangent):
    _, pull = jax.vjp(rms_norm, stream, gain_row)
    return pull(cotangent)


def gated_unit(gate_value, linear_value):
    return jax.nn.gelu(gate_value, approximate=True) * linear_value


def visible(prefix_ids, action_ids, block_flags):
    length = block_flags.shape[0]
    place = jnp.arange(length)
    upto = place[None, :] <= place[:, None]
    levels = jnp.sum(jnp.where(upto, block_flags[None, :], 0), axis=1)
    from_prefix = prefix_ids[:, None] == action_ids[None, :]
    from_action = (action_ids[:, None] == action_ids[None, :]) & (
        levels[:, None] <= levels[None, :]
    )
    return jnp.concatenate([from_prefix, from_action], axis=0).astype(jnp.int32)


def advance(weight, moment, average, gradient, step_rate):
    moment_next = MOMENTUM * moment + gradient
    weight_next = weight - step_rate * (gradient + MOMENTUM * moment_next)
    average_next = AVERAGE_DECAY * average + (1.0 - AVERAGE_DECAY) * weight_next
    return (weight_next, moment_next, average_next)


def mm(a, b, contract, out=f32):
    return lax.dot_general(
        a, b, (((contract[0],), (contract[1],)), ((), ())), preferred_element_type=f32
    ).astype(out)


class Order:
    def __init__(self):
        self.token = jnp.zeros((), jnp.int32)

    def __call__(self, *values):
        *values, self.token = lax.optimization_barrier((*values, self.token))
        return values[0] if len(values) == 1 else values


class Ring:
    def __init__(self, wide):
        chips = wide // 2
        self.wide, self.chips = wide, chips
        self.cycle = list(range(0, chips, 2)) + list(range(1, chips, 2))[::-1]
        ahead = [(self.cycle[i], self.cycle[(i + 1) % chips]) for i in range(chips)]
        self.right = [(2 * s + c, 2 * t + c) for s, t in ahead for c in (0, 1)]
        self.left = [(t, s) for s, t in self.right]
        self.core = [(w, w ^ 1) for w in range(wide)]
        self.n_right = chips // 2
        self.n_left = chips - 1 - self.n_right

    def to_right(self, v):
        return lax.ppermute(v, "wide", self.right)

    def to_left(self, v):
        return lax.ppermute(v, "wide", self.left)

    def to_core(self, v):
        return lax.ppermute(v, "wide", self.core)

    def to_peer(self, v):
        return lax.ppermute(v, "batch", [(0, 1), (1, 0)])

    def owners(self, w):
        here = self.cycle.index(w // 2)
        rights = [self.cycle[(here - d) % self.chips] for d in range(1, self.n_right + 1)]
        lefts = [self.cycle[(here + d) % self.chips] for d in range(1, self.n_left + 1)]
        return [w // 2] + rights + lefts

    def bits(self):
        k, steps = 1, [self.to_peer]
        while k < self.wide:
            pairs = [(w, w ^ k) for w in range(self.wide)]
            steps.append(functools.partial(lax.ppermute, axis_name="wide", perm=pairs))
            k *= 2
        return steps


def add(*terms, step=None):
    terms = [t if isinstance(t, tuple) else (t, 0, 1) for t in terms]
    shape = terms[0][0].shape
    cols = shape[-1]
    rows = math.prod(shape[:-1])
    if step is None:
        step = 128 if rows % 128 == 0 and rows > 128 else rows

    def kernel(*refs):
        refs[-1][...] = sum(r[...].astype(f32) for r in refs[:-1]).astype(bf16)

    def block(k, stride):
        return pl.BlockSpec((step, cols), lambda i: (stride * i + k, 0))

    return pl.pallas_call(
        kernel,
        out_shape=jax.ShapeDtypeStruct((rows, cols), bf16),
        grid=(rows // step,),
        in_specs=[block(k, stride) for _, k, stride in terms],
        out_specs=block(0, 1),
        compiler_params=pltpu.CompilerParams(vmem_limit_bytes=8 * MIB),
        cost_estimate=cost("add"),
        name="add",
    )(*[t.reshape(-1, cols) for t, _, _ in terms]).reshape(shape)


class SmallSum:
    def __init__(self, ring, order, rows):
        self.order, self.steps = order, ring.bits()
        self.total = order(jnp.concatenate(rows, 0))
        self.moved = self.steps.pop(0)(self.total)

    def step(self):
        if self.moved is None:
            return False
        total, moved = self.order(self.total, self.moved)
        self.total = self.order(total + moved)
        self.moved = self.steps.pop(0)(self.total) if self.steps else None
        return True


class Gathering:
    def __init__(self, ring, order, halves, axis, split_left):
        self.ring, self.order = ring, order
        self.halves, self.split_left = halves, split_left
        self.whole = jnp.concatenate(halves, axis)
        self.can = halves[0].shape[axis] % 16 == 0
        self.blocks, self.flying = {}, {}
        self.count = {"right": ring.n_right, "left": ring.n_left}
        self.d = {"right": 0, "left": 0}

    def cut(self, side):
        return self.can and (side == "right" or self.split_left)

    def start(self, side):
        self.send(side, self.order(self.halves[0] if self.cut(side) else self.whole))

    def send(self, side, v):
        self.flying[side] = self.ring.to_right(v) if side == "right" else self.ring.to_left(v)

    def land(self, *sides):
        sides = [x for x in sides if self.d[x] < self.count[x] and x in self.flying]
        if not sides:
            return
        came = self.order(*[self.flying[x] for x in sides])
        for side, v in zip(sides, came if len(sides) > 1 else [came]):
            self.blocks[side, self.d[side]] = (v,)
            self.d[side] += 1
            if self.d[side] < self.count[side]:
                self.send(side, v)

    def cross(self, *keys):
        for key in keys:
            if self.cut(key[0]) and len(self.blocks.get(key, (0, 0))) == 1:
                (v,) = self.blocks[key]
                v = self.order(v)
                self.blocks[key] = (v, self.ring.to_peer(v))

    def settle(self, *keys):
        for key in keys:
            if key in self.blocks:
                self.cross(key)
                self.blocks[key] = tuple(self.order(p) for p in self.blocks[key])


class Summing:
    def __init__(self, ring, order, axis, n_right):
        self.ring, self.order, self.axis = ring, order, axis
        self.parts, self.sends, self.spots, self.crossed = {}, {}, {}, {}
        self.came = {"right": None, "left": None}
        self.d = {"right": n_right - 1, "left": ring.chips - 2 - n_right}

    def put(self, parts, sends, spots):
        self.parts.update(parts)
        self.sends.update(sends)
        self.spots.update(spots)

    def cross(self, *names):
        for name in names:
            if name in self.sends and name not in self.crossed:
                self.crossed[name] = self.ring.to_peer(self.order(self.sends[name]))

    def ready(self, *names):
        for name in names:
            if name in self.crossed:
                self.crossed[name] = self.order(self.crossed[name])

    def step(self, *sides):
        for side in sides:
            d = self.d[side]
            if d < 0:
                continue
            terms = [self.parts[side, d]]
            terms += [self.came[side]] if self.came[side] is not None else []
            if (side, d) in self.spots:
                name, spot = self.spots[side, d]
                self.cross(name)
                *terms, self.crossed[name] = self.order(*terms, self.crossed[name])
                rows = math.prod(self.parts[side, d].shape[:-1])
                step = 128 if rows % 128 == 0 and rows > 128 else rows
                terms.append((self.crossed[name], spot * (rows // step), 1))
            else:
                terms = self.order(*terms)
                terms = list(terms) if isinstance(terms, (list, tuple)) else [terms]
            total = self.order(add(*terms)) if len(terms) > 1 else terms[0]
            self.came[side] = self.ring.to_left(total) if side == "right" else self.ring.to_right(total)
            self.d[side] = d - 1

    def land(self, side):
        self.came[side] = self.order(self.came[side])

    def left(self):
        return max(self.d.values()) + 1

    def own(self, halves):
        left = self.order(self.came["left"])
        half = halves[0].shape[self.axis]
        self.split = bool(self.spots)
        if self.split:
            stride = 2 if self.axis else 1
            self.rows = half
            self.mine = [halves[0], (left, 0, stride)]
            other = self.order(add(halves[1], (left, 1, stride), step=half))
            self.across = self.ring.to_peer(other)
        else:
            self.mine = [self.order(add(jnp.concatenate(halves, self.axis), left))]
            self.rows = None

    def close(self):
        self.came["right"] = self.order(self.came["right"])
        terms = self.mine + [self.came["right"]]
        if self.split:
            self.across = self.order(self.across)
            terms.append(self.across)
        self.total = self.order(add(*terms, step=self.rows))
        self.across = self.ring.to_peer(self.total)

    def result(self):
        me = lax.axis_index("batch")
        total, across = [v.astype(f32) for v in self.order(self.total, self.across)]
        if not self.split:
            return total + across
        return jnp.where(
            me == 0,
            jnp.concatenate([total, across], self.axis),
            jnp.concatenate([across, total], self.axis),
        )


def places(ring, counts, rows):
    table = np.zeros((2, ring.wide, 2, sum(counts)), np.int32)
    for me in (0, 1):
        for w in range(ring.wide):
            where, first = [], []
            for owner, n in zip(ring.owners(w), counts):
                where += [owner] * n
                first += [me * rows // 2, (1 - me) * rows // 2] if n == 2 else [0]
            table[me, w] = where, first
    return jnp.array(table)[lax.axis_index("batch"), lax.axis_index("wide")]


def assemble(ring, blocks, rows, width_a):
    counts = [len(b) for b in blocks]
    parts = [p for b in blocks for p in b]
    n = len(parts)
    table = places(ring, counts, rows)
    side_rows = rows * ring.chips
    pw = (parts[0].shape[1] - width_a) // 2
    shapes = ((side_rows, QKV_WIDTH), (side_rows, width_a - QKV_WIDTH), (2 * side_rows, pw))

    def kernel(table_ref, *refs):
        ins, (qkv, out, pre, sems) = refs[:n], refs[n:]
        copies = []

        def copy(i, start, width, to, row):
            size = parts[i].shape[0]
            target = to.at[pl.ds(pl.multiple_of(row, size), size), :]
            copies.append(
                pltpu.make_async_copy(ins[i].at[:, pl.ds(start, width)], target, sems.at[len(copies)])
            )

        for i in range(n):
            chip, first = table_ref[0, i], table_ref[1, i]
            copy(i, 0, QKV_WIDTH, qkv, chip * rows + first)
            copy(i, QKV_WIDTH, width_a - QKV_WIDTH, out, chip * rows + first)
            for j in (0, 1):
                copy(i, width_a + j * pw, pw, pre, (2 * chip + j) * rows + first)
        for c in copies:
            c.start()
        for c in copies:
            c.wait()

    return pl.pallas_call(
        kernel,
        out_shape=[jax.ShapeDtypeStruct(sh, bf16) for sh in shapes],
        grid_spec=pltpu.PrefetchScalarGridSpec(
            num_scalar_prefetch=1,
            grid=(1,),
            in_specs=[pl.BlockSpec(memory_space=pl.ANY)] * n,
            out_specs=[pl.BlockSpec(sh, lambda i, t: (0, 0)) for sh in shapes],
            scratch_shapes=[pltpu.SemaphoreType.DMA((4 * n,))],
        ),
        compiler_params=pltpu.CompilerParams(vmem_limit_bytes=16 * MIB),
        cost_estimate=cost("assemble"),
        name="assemble",
    )(table, *parts)


def interleave(ring, own, other, rows):
    core = (lax.axis_index("wide") % 2).reshape(1)

    def kernel(core_ref, own_ref, other_ref, out_ref, sems):
        copies = []
        for chip in range(ring.chips):
            for j, ref in enumerate((own_ref, other_ref)):
                side = core_ref[0] if j == 0 else 1 - core_ref[0]
                to = pl.ds(pl.multiple_of((2 * chip + side) * rows, rows), rows)
                copies.append(
                    pltpu.make_async_copy(
                        ref.at[pl.ds(chip * rows, rows), :], out_ref.at[to, :], sems.at[chip, j]
                    )
                )
        for c in copies:
            c.start()
        for c in copies:
            c.wait()

    shape = (2 * own.shape[0], own.shape[1])
    return pl.pallas_call(
        kernel,
        out_shape=jax.ShapeDtypeStruct(shape, bf16),
        grid_spec=pltpu.PrefetchScalarGridSpec(
            num_scalar_prefetch=1,
            grid=(1,),
            in_specs=[pl.BlockSpec(memory_space=pl.ANY)] * 2,
            out_specs=pl.BlockSpec(shape, lambda i, t: (0, 0)),
            scratch_shapes=[pltpu.SemaphoreType.DMA((ring.chips, 2))],
        ),
        compiler_params=pltpu.CompilerParams(vmem_limit_bytes=12 * MIB),
        cost_estimate=cost("interleave"),
        name="interleave",
    )(core, own, other)


def side_gradient(rows, cols, which=0):
    tokens, width = rows.shape[0], rows.shape[1] // 2

    def kernel(rows_ref, cols_ref, out_ref):
        out_ref[...] = mm(rows_ref[...], cols_ref[...], (0, 0), bf16)

    return pl.pallas_call(
        kernel,
        out_shape=jax.ShapeDtypeStruct((width, cols.shape[1]), bf16),
        grid=(1,),
        in_specs=[
            pl.BlockSpec((tokens, width), lambda i: (0, which)),
            pl.BlockSpec(cols.shape, lambda i: (0, 0)),
        ],
        out_specs=pl.BlockSpec((width, cols.shape[1]), lambda i: (0, 0)),
        compiler_params=pltpu.CompilerParams(vmem_limit_bytes=16 * MIB),
        cost_estimate=cost("side_gradient"),
        name="side_gradient",
    )(rows, cols)


def half_product(rows, side, weight, before):
    tokens, width = rows.shape[0], rows.shape[1] // 2
    cols = weight.shape[1]
    kind = f32 if before is None else bf16

    def kernel(rows_ref, weight_ref, *refs):
        out_ref = refs[-1]
        for c in range(cols // CUT):
            at = slice(c * CUT, (c + 1) * CUT)
            total = mm(rows_ref[...], weight_ref[:, at], (1, 0))
            out_ref[:, at] = (total if before is None else total + refs[0][:, at]).astype(kind)

    extra = [] if before is None else [before]
    return pl.pallas_call(
        kernel,
        out_shape=jax.ShapeDtypeStruct((tokens, cols), kind),
        grid=(1,),
        in_specs=[
            pl.BlockSpec((tokens, width), lambda i: (0, side)),
            pl.BlockSpec(weight.shape, lambda i: (0, 0)),
        ]
        + [pl.BlockSpec((tokens, cols), lambda i: (0, 0)) for _ in extra],
        out_specs=pl.BlockSpec((tokens, cols), lambda i: (0, 0)),
        compiler_params=pltpu.CompilerParams(vmem_limit_bytes=30 * MIB),
        cost_estimate=cost("half_product"),
        name="half_product",
    )(rows, weight, *extra)


def gain_sums(back, rows, own, other):
    tokens, width = rows.shape[0], rows.shape[1] // 2
    cols = own.shape[1]
    step = 256

    def kernel(back_ref, rows_ref, own_ref, other_ref, out_ref):
        @pl.when(pl.program_id(0) == 0)
        def _():
            out_ref[...] = jnp.zeros_like(out_ref)

        for side, ref in enumerate((own_ref, other_ref)):
            at = slice(side * width, (side + 1) * width)
            total = mm(back_ref[...], ref[...], (1, 1)) * rows_ref[:, at].astype(f32)
            out_ref[:, at] += jnp.sum(total, axis=0, keepdims=True)

    return pl.pallas_call(
        kernel,
        out_shape=jax.ShapeDtypeStruct((1, 2 * width), f32),
        grid=(tokens // step,),
        in_specs=[
            pl.BlockSpec((step, cols), lambda i: (i, 0)),
            pl.BlockSpec((step, 2 * width), lambda i: (i, 0)),
        ]
        + [pl.BlockSpec(w.shape, lambda i: (0, 0)) for w in (own, other)],
        out_specs=pl.BlockSpec((1, 2 * width), lambda i: (0, 0)),
        compiler_params=pltpu.CompilerParams(vmem_limit_bytes=24 * MIB),
        cost_estimate=cost("gain_sums"),
        name="gain_sums",
    )(back, rows, own, other)


def pair_gradient(rows, cols):
    width, step = rows[0].shape[1], 512

    def kernel(r0, r1, c0, c1, out_ref):
        out_ref[...] = (mm(r0[...], c0[...], (0, 0)) + mm(r1[...], c1[...], (0, 0))).astype(bf16)

    once = [pl.BlockSpec(r.shape, lambda i: (0, 0)) for r in rows]
    return pl.pallas_call(
        kernel,
        out_shape=jax.ShapeDtypeStruct((width, cols[0].shape[1]), bf16),
        grid=(cols[0].shape[1] // step,),
        in_specs=once + [pl.BlockSpec((c.shape[0], step), lambda i: (0, i)) for c in cols],
        out_specs=pl.BlockSpec((width, step), lambda i: (0, i)),
        compiler_params=pltpu.CompilerParams(vmem_limit_bytes=14 * MIB),
        cost_estimate=cost("pair_gradient"),
        name="pair_gradient",
    )(*rows, *cols)


def disassemble(ring, halved, norm_rows, qkv_back, pre_rel, back_prefix_kv, other_side, grad_output, rows):
    cuts = 2 if halved else 1
    size = rows // cuts
    table = places(ring, [cuts] * ring.chips, rows)
    spots, sizes = [], []
    for j in range(ring.chips):
        right = 1 <= j <= ring.n_right
        sizes.append(size if right else rows)
        if right and halved:
            spots += [(j, 0), (ring.chips, (j - 1) * size)]
        else:
            spots += [(j, k * size) for k in range(cuts)]
    if halved:
        sizes.append(ring.n_right * size)
    n = len(sizes)
    side_rows = rows * ring.chips
    pre_cols = back_prefix_kv.shape[1]
    out_cols = grad_output.shape[1]
    width = QKV_WIDTH + out_cols + 2 * pre_cols
    step = 512

    def kernel(table_ref, n0, n1, q0, q1, pre_ref, back_ref, side_ref, out_ref, *refs):
        parts, (qkv_sum, pre_sum, sems) = refs[:n], refs[n:]

        def copies(i, k):
            chip, first = table_ref[0, i], table_ref[1, i]
            part, top = spots[i]

            def piece(ref, row, at, w, j):
                source = ref.at[pl.ds(pl.multiple_of(row, size), size), :]
                target = parts[part].at[pl.ds(top, size), pl.ds(at, w)]
                return pltpu.make_async_copy(source, target, sems.at[i, j])

            if k == 0:
                return [piece(out_ref, chip * rows + first, QKV_WIDTH, out_cols, 0)]
            if k == 1:
                at = QKV_WIDTH + out_cols
                return [
                    piece(pre_sum, (2 * chip + j) * rows + first, at + j * pre_cols, pre_cols, 1 + j)
                    for j in (0, 1)
                ]
            return [piece(qkv_sum, chip * rows + first, 0, QKV_WIDTH, 3)]

        def start(k):
            for i in range(len(spots)):
                for c in copies(i, k):
                    c.start()

        start(0)
        total = mm(pre_ref[...], back_ref[...], (0, 0)) + side_ref[...].astype(f32)
        pre_sum[...] = total.astype(bf16)
        start(1)
        for c in range(QKV_WIDTH // step):
            at = slice(c * step, (c + 1) * step)
            total = mm(n0[...], q0[:, at], (0, 0)) + mm(n1[...], q1[:, at], (0, 0))
            qkv_sum[:, at] = total.astype(bf16)
        start(2)
        for i in range(len(spots)):
            for k in (0, 1, 2):
                for c in copies(i, k):
                    c.wait()

    def once(v):
        return pl.BlockSpec(v.shape, lambda i, t: (0, 0))

    tokens = pre_rel.shape[0]
    out = pl.pallas_call(
        kernel,
        out_shape=[jax.ShapeDtypeStruct((size, width), bf16) for size in sizes],
        grid_spec=pltpu.PrefetchScalarGridSpec(
            num_scalar_prefetch=1,
            grid=(1,),
            in_specs=[once(v) for v in (*norm_rows, *qkv_back)]
            + [pl.BlockSpec((tokens, 2 * side_rows), lambda i, t: (0, 0))]
            + [once(v) for v in (back_prefix_kv, other_side, grad_output)],
            out_specs=[pl.BlockSpec(memory_space=pltpu.HBM)] * n,
            scratch_shapes=[
                pltpu.VMEM((side_rows, QKV_WIDTH), bf16),
                pltpu.VMEM((2 * side_rows, pre_cols), bf16),
                pltpu.SemaphoreType.DMA((len(spots), 4)),
            ],
        ),
        compiler_params=pltpu.CompilerParams(vmem_limit_bytes=28 * MIB),
        cost_estimate=cost("disassemble"),
        name="disassemble",
    )(table, *norm_rows, *qkv_back, pre_rel, back_prefix_kv, other_side, grad_output)
    return out


def norm_by_core(ring, rows, gains, size):
    core = (lax.axis_index("wide") % 2).reshape(1)
    tokens, dim = rows.shape
    step = 128

    def kernel(core_ref, rows_ref, gains_ref, out_ref):
        v = rows_ref[...].astype(f32)
        normed = rms_norm(v, gains_ref[0]).astype(bf16)
        for swapped in (0, 1):

            @pl.when(core_ref[0] == swapped)
            def _(swapped=swapped):
                for chip in range(ring.chips):
                    for side in (0, 1):
                        at = (2 * chip + (side ^ swapped)) * size
                        to = side * (dim // 2) + chip * size
                        out_ref[:, to : to + size] = normed[:, at : at + size]

    return pl.pallas_call(
        kernel,
        out_shape=jax.ShapeDtypeStruct((tokens, dim), bf16),
        grid_spec=pltpu.PrefetchScalarGridSpec(
            num_scalar_prefetch=1,
            grid=(tokens // step,),
            in_specs=[
                pl.BlockSpec((step, dim), lambda i, t: (i, 0)),
                pl.BlockSpec((1, dim), lambda i, t: (0, 0)),
            ],
            out_specs=pl.BlockSpec((step, dim), lambda i, t: (i, 0)),
        ),
        compiler_params=pltpu.CompilerParams(vmem_limit_bytes=12 * MIB),
        cost_estimate=cost("norm_by_core"),
        name="norm_by_core",
    )(core, rows, gains)


def gelu_parts(v):
    c = math.sqrt(2.0 / math.pi)
    square = v * v
    t = jnp.tanh(c * v * (1.0 + 0.044715 * square))
    half = 0.5 * (1.0 + t)
    slope = half + 0.5 * v * (1.0 - t * t) * c * (1.0 + 3.0 * 0.044715 * square)
    return v * half, slope


def load_block(refs, buf, sems, k):
    at, made = 0, []
    for j, r in enumerate(refs):
        size = r.shape[1]
        made.append(pltpu.make_async_copy(r, buf.at[:, pl.ds(at, size), :], sems.at[k, j]))
        at += size
    return made


def ff_forward(norm_two, blocks, before):
    nb = len(blocks)
    flat = [a for blk in blocks for a in blk]
    tokens, dim = norm_two.shape
    units = sum(a.shape[1] for a in blocks[0])
    half = tokens // 2
    has_before = before is not None

    def kernel(norm_ref, *refs):
        refs = list(refs)
        ins = [[refs.pop(0) for _ in blk] for blk in blocks]
        if has_before:
            own_in, oth_in = refs.pop(0), refs.pop(0)
        gate_out, lin_out, hid_out, own_out, oth_out, buf, total, sems = refs
        i = pl.program_id(0)

        @pl.when(i == 0)
        def _():
            for k in range(nb):
                for c in load_block(ins[k], buf.at[k], sems, k):
                    c.start()
            if has_before:
                total[:half] = own_in[...]
                total[half:] = oth_in[...]
            else:
                total[...] = jnp.zeros_like(total)

        for k in range(nb):

            @pl.when(i == k)
            def _(k=k):
                for c in load_block(ins[k], buf.at[k], sems, k):
                    c.wait()

        w = buf.at[i]
        if units % 128 == 0:
            both = mm(norm_ref[...], w[:2].reshape(2 * units, dim), (1, 1))
            gate, linear = both[:, :units], both[:, units:]
        else:
            gate, linear = (mm(norm_ref[...], w[j], (1, 1)) for j in (0, 1))
        gate_out[0] = gate
        lin_out[0] = linear
        hidden = (gelu_parts(gate)[0] * linear).astype(bf16)
        hid_out[0] = hidden
        total[...] += mm(hidden, w[2], (1, 0))

        @pl.when(i == nb - 1)
        def _():
            own_out[...] = total[:half]
            oth_out[...] = total[half:]

    once = pl.BlockSpec((tokens, dim), lambda i: (0, 0))
    row = pl.BlockSpec((half, dim), lambda i: (0, 0))
    step = pl.BlockSpec((1, tokens, units), lambda i: (i, 0, 0))
    any_space = pl.BlockSpec(memory_space=pl.ANY)
    return pl.pallas_call(
        kernel,
        out_shape=[
            jax.ShapeDtypeStruct((nb, tokens, units), f32),
            jax.ShapeDtypeStruct((nb, tokens, units), f32),
            jax.ShapeDtypeStruct((nb, tokens, units), bf16),
            jax.ShapeDtypeStruct((half, dim), f32),
            jax.ShapeDtypeStruct((half, dim), f32),
        ],
        grid=(nb,),
        in_specs=[once] + [any_space] * len(flat) + [row, row] * has_before,
        out_specs=[step, step, step, row, row],
        scratch_shapes=[
            pltpu.VMEM((nb, 3, units, dim), bf16),
            pltpu.VMEM((tokens, dim), f32),
            pltpu.SemaphoreType.DMA((nb, 2)),
        ],
        compiler_params=pltpu.CompilerParams(vmem_limit_bytes=28 * MIB),
        cost_estimate=cost("ff_forward"),
        name="ff_forward",
    )(norm_two, *flat, *(before or ()))


def ff_backward(norm_two, branch_two, blocks, sends, kept, picks, before):
    nb = len(blocks)
    flat = [a for blk in blocks for a in blk]
    gate_all, lin_all, hid_all = kept
    tokens, dim = norm_two.shape
    units = sum(a.shape[1] for a in blocks[0])
    half = tokens // 2
    has_before = before is not None
    first, stride = picks

    def kernel(norm_ref, branch_ref, gate_ref, lin_ref, hid_ref, *refs):
        refs = list(refs)
        ins = [[refs.pop(0) for _ in blk] for blk in blocks]
        if has_before:
            own_in, oth_in = refs.pop(0), refs.pop(0)
        outs = [[refs.pop(0)] for _ in blocks]
        for keys in sends:
            ref = refs.pop(0)
            for spot, k in enumerate(keys):
                outs[k].append(ref.at[spot])
        own_out, oth_out, buf, grads, total, sems, out_sems = refs
        i = pl.program_id(0)

        def stores(k):
            at, made = 0, []
            for j, r in enumerate(outs[k]):
                size = r.shape[1]
                made.append(pltpu.make_async_copy(grads.at[k, :, pl.ds(at, size), :], r, out_sems.at[k, j]))
                at += size
            return made

        @pl.when(i == 0)
        def _():
            for k in range(nb):
                for c in load_block(ins[k], buf.at[k], sems, k):
                    c.start()
            if has_before:
                total[:half] = own_in[...]
                total[half:] = oth_in[...]
            else:
                total[...] = jnp.zeros_like(total)

        for k in range(nb):

            @pl.when(i == k)
            def _(k=k):
                for c in load_block(ins[k], buf.at[k], sems, k):
                    c.wait()

        w, g = buf.at[i], grads.at[i]
        back_hidden = mm(branch_ref[...], w[2], (1, 1))
        value, slope = gelu_parts(gate_ref[0])
        back_gate = (back_hidden * lin_ref[0] * slope).astype(bf16)
        back_linear = (back_hidden * value).astype(bf16)
        if units % 128 == 0:
            both = jnp.concatenate([back_gate, back_linear], 1)
            g[:2] = mm(both, norm_ref[...], (0, 0), bf16).reshape(2, units, dim)
            total[...] += mm(both, w[:2].reshape(2 * units, dim), (1, 0))
        else:
            for j, back in enumerate((back_gate, back_linear)):
                g[j] = mm(back, norm_ref[...], (0, 0), bf16)
                total[...] += mm(back, w[j], (1, 0))
        g[2] = mm(hid_ref[0], branch_ref[...], (0, 0), bf16)

        for k in range(nb):

            @pl.when(i == k)
            def _(k=k):
                for c in stores(k):
                    c.start()

        @pl.when(i == nb - 1)
        def _():
            own_out[...] = total[:half]
            oth_out[...] = total[half:]
            for k in range(nb):
                for c in stores(k):
                    c.wait()

    once = pl.BlockSpec((tokens, dim), lambda i: (0, 0))
    row = pl.BlockSpec((half, dim), lambda i: (0, 0))
    step = pl.BlockSpec((1, tokens, units), lambda i: (first + stride * i, 0, 0))
    any_space = pl.BlockSpec(memory_space=pl.ANY)
    hbm = pl.BlockSpec(memory_space=pltpu.HBM)
    made = pl.pallas_call(
        kernel,
        out_shape=[
            jax.ShapeDtypeStruct((3, units // (2 if any(k in x for x in sends) else 1), dim), bf16)
            for k in range(nb)
        ]
        + [jax.ShapeDtypeStruct((len(x), 3, units // 2, dim), bf16) for x in sends]
        + [jax.ShapeDtypeStruct((half, dim), f32)] * 2,
        grid=(nb,),
        in_specs=[once, once, step, step, step] + [any_space] * len(flat) + [row, row] * has_before,
        out_specs=[hbm] * (nb + len(sends)) + [row, row],
        scratch_shapes=[
            pltpu.VMEM((nb, 3, units, dim), bf16),
            pltpu.VMEM((nb, 3, units, dim), bf16),
            pltpu.VMEM((tokens, dim), f32),
            pltpu.SemaphoreType.DMA((nb, 2)),
            pltpu.SemaphoreType.DMA((nb, 2)),
        ],
        compiler_params=pltpu.CompilerParams(vmem_limit_bytes=42 * MIB),
        cost_estimate=cost("ff_backward"),
        name="ff_backward",
    )(norm_two, branch_two, gate_all, lin_all, hid_all, *flat, *(before or ()))
    made = list(made)
    return made[:nb], made[nb:-2], made[-2:]


def attention(action_qkv, prefix_kv, allowed, first, heads, before):
    tokens, keys = action_qkv.shape[0], allowed.shape[0]
    n_pre = prefix_kv.shape[0]

    def kernel(q_ref, kv_ref, pre_ref, allowed_ref, *refs):
        out_ref, k_all, v_turned = refs[-3:]
        h = pl.program_id(0)

        @pl.when(h == 0)
        def _():
            k_all[:n_pre] = pre_ref[:, :HEAD_DIM]
            k_all[n_pre:] = kv_ref[:, :HEAD_DIM]
            v_turned[:, :n_pre] = pre_ref[:, HEAD_DIM:].T
            v_turned[:, n_pre:] = kv_ref[:, HEAD_DIM:].T
            if before:
                out_ref[:, : first * HEAD_DIM] = refs[0][...]

        scores = mm(k_all[...], q_ref[...], (1, 1)) * SCORE_SCALE
        scores = jnp.where(allowed_ref[...] != 0, scores, NEGATIVE)
        exp_scores = jnp.exp(scores - jnp.max(scores, axis=0, keepdims=True))
        soft = exp_scores / jnp.sum(exp_scores, axis=0, keepdims=True)
        at = pl.ds(pl.multiple_of((first + h) * HEAD_DIM, HEAD_DIM), HEAD_DIM)
        out_ref[:, at] = mm(v_turned[...], soft.astype(bf16), (1, 0)).T.astype(bf16)

    width = (first + heads) * HEAD_DIM
    return pl.pallas_call(
        kernel,
        out_shape=jax.ShapeDtypeStruct((tokens, width), bf16),
        grid=(heads,),
        in_specs=[
            pl.BlockSpec((tokens, HEAD_DIM), lambda h: (0, first + h)),
            pl.BlockSpec((tokens, 2 * HEAD_DIM), lambda h: (0, HEADS // 2)),
            pl.BlockSpec((n_pre, 2 * HEAD_DIM), lambda h: (0, 0)),
            pl.BlockSpec((keys, tokens), lambda h: (0, 0)),
        ]
        + [pl.BlockSpec(v.shape, lambda h: (0, 0)) for v in before],
        out_specs=pl.BlockSpec((tokens, width), lambda h: (0, 0)),
        scratch_shapes=[pltpu.VMEM((keys, HEAD_DIM), bf16), pltpu.VMEM((HEAD_DIM, keys), bf16)],
        compiler_params=pltpu.CompilerParams(vmem_limit_bytes=24 * MIB),
        cost_estimate=cost("attention"),
        name="attention",
    )(action_qkv, action_qkv, prefix_kv, allowed, *before)


def attention_back(action_qkv, prefix_kv, allowed, back_mixed, first, heads, before):
    tokens, keys = action_qkv.shape[0], allowed.shape[0]
    n_pre = prefix_kv.shape[0]
    last = first + heads == HEADS
    n_before = len(before)

    def kernel(q_ref, kv_ref, pre_ref, allowed_ref, back_ref, *refs):
        before_refs, refs = refs[:n_before], refs[n_before:]
        if last:
            qkv_out, pre_out, k_sum, v_sum, k_all, v_all, k_turned = refs
        else:
            qkv_out, k_sum, v_sum, k_all, v_all, k_turned = refs
        h = pl.program_id(0)

        @pl.when(h == 0)
        def _():
            k_all[:n_pre] = pre_ref[:, :HEAD_DIM]
            k_all[n_pre:] = kv_ref[:, :HEAD_DIM]
            v_all[:n_pre] = pre_ref[:, HEAD_DIM:]
            v_all[n_pre:] = kv_ref[:, HEAD_DIM:]
            k_turned[...] = k_all[...].T
            if n_before:
                qkv_out[:, : first * HEAD_DIM] = before_refs[0][...]
                k_sum[...] = before_refs[1][...]
                v_sum[...] = before_refs[2][...]
            else:
                k_sum[...] = jnp.zeros_like(k_sum)
                v_sum[...] = jnp.zeros_like(v_sum)

        query, back = q_ref[...], back_ref[...]
        scores = mm(k_all[...], query, (1, 1)) * SCORE_SCALE
        scores = jnp.where(allowed_ref[...] != 0, scores, NEGATIVE)
        exp_scores = jnp.exp(scores - jnp.max(scores, axis=0, keepdims=True))
        soft = exp_scores / jnp.sum(exp_scores, axis=0, keepdims=True)
        v_sum[...] += mm(soft.astype(bf16), back, (1, 0))
        back_soft = mm(v_all[...], back, (1, 1))
        mean = jnp.sum(soft * back_soft, axis=0, keepdims=True)
        back_scores = (soft * (back_soft - mean)).astype(bf16)
        k_sum[...] += mm(back_scores, query, (1, 0))
        turned = mm(k_turned[...], back_scores, (1, 0)) * SCORE_SCALE
        at = pl.ds(pl.multiple_of((first + h) * HEAD_DIM, HEAD_DIM), HEAD_DIM)
        qkv_out[:, at] = turned.T.astype(bf16)

        if last:

            @pl.when(h == heads - 1)
            def _():
                pre_out[:, :HEAD_DIM] = (k_sum[:n_pre] * SCORE_SCALE).astype(bf16)
                pre_out[:, HEAD_DIM:] = v_sum[:n_pre].astype(bf16)
                keys_out = (k_sum[n_pre:] * SCORE_SCALE).astype(bf16)
                qkv_out[:, QUERY_WIDTH : QUERY_WIDTH + HEAD_DIM] = keys_out
                qkv_out[:, QUERY_WIDTH + HEAD_DIM :] = v_sum[n_pre:].astype(bf16)

    def once(shape):
        return pl.BlockSpec(shape, lambda h: (0, 0))

    sums = jax.ShapeDtypeStruct((keys, HEAD_DIM), f32)
    if last:
        out_shapes = [
            jax.ShapeDtypeStruct((tokens, QKV_WIDTH), bf16),
            jax.ShapeDtypeStruct((n_pre, 2 * HEAD_DIM), bf16),
        ]
        kept = [pltpu.VMEM(sums.shape, f32)] * 2
    else:
        out_shapes = [jax.ShapeDtypeStruct((tokens, heads * HEAD_DIM), bf16), sums, sums]
        kept = []
    return pl.pallas_call(
        kernel,
        out_shape=out_shapes,
        grid=(heads,),
        in_specs=[
            pl.BlockSpec((tokens, HEAD_DIM), lambda h: (0, first + h)),
            pl.BlockSpec((tokens, 2 * HEAD_DIM), lambda h: (0, HEADS // 2)),
            once((n_pre, 2 * HEAD_DIM)),
            once((keys, tokens)),
            pl.BlockSpec((tokens, HEAD_DIM), lambda h: (0, first + h)),
        ]
        + [once(v.shape) for v in before],
        out_specs=[once(o.shape) for o in out_shapes],
        scratch_shapes=kept
        + [
            pltpu.VMEM((keys, HEAD_DIM), bf16),
            pltpu.VMEM((keys, HEAD_DIM), bf16),
            pltpu.VMEM((HEAD_DIM, keys), bf16),
        ],
        compiler_params=pltpu.CompilerParams(vmem_limit_bytes=28 * MIB),
        cost_estimate=cost("attention_back"),
        name="attention_back",
    )(action_qkv, action_qkv, prefix_kv, allowed, back_mixed, *before)


def mid_back(residual, back_final, back_own, back_oth, gain_row, out_weight):
    tokens, dim = residual.shape

    def kernel(res_ref, fin_ref, own_ref, oth_ref, gain_ref, weight_ref, attn_out, mixed_out, gain_out):
        v = res_ref[...]
        s = lax.rsqrt(jnp.mean(v * v, axis=-1, keepdims=True) + NORM_EPSILON)
        normed = v * s
        back = own_ref[...] + oth_ref[...]
        gain_out[...] = jnp.sum(back * normed, axis=0, keepdims=True)
        scaled = back * (1.0 + gain_ref[...])
        mean = jnp.mean(scaled * normed, axis=-1, keepdims=True)
        attn = (fin_ref[...] + s * (scaled - normed * mean)).astype(bf16)
        attn_out[...] = attn
        mixed_out[...] = mm(attn, weight_ref[...], (1, 0), bf16)

    return pl.pallas_call(
        kernel,
        out_shape=[
            jax.ShapeDtypeStruct((tokens, dim), bf16),
            jax.ShapeDtypeStruct((tokens, QUERY_WIDTH), bf16),
            jax.ShapeDtypeStruct((1, dim), f32),
        ],
        compiler_params=pltpu.CompilerParams(vmem_limit_bytes=22 * MIB),
        cost_estimate=cost("mid_back"),
        name="mid_back",
    )(residual, back_final, back_own, back_oth, gain_row, out_weight)


def readout_loss(residual, branch_own, branch_oth, gain_row, readout, target, valid):
    tokens, dim = residual.shape
    act = readout.shape[0]

    def full(a, b, contract):
        return lax.dot_general(
            a, b, (((contract[0],), (contract[1],)), ((), ())),
            precision=HIGHEST, preferred_element_type=f32,
        )

    def kernel(res_ref, own_ref, oth_ref, gain_ref, read_ref, target_ref, valid_ref, final_out, branch_out, rows_out):
        v = res_ref[...] + own_ref[...] + oth_ref[...]
        s = lax.rsqrt(jnp.mean(v * v, axis=-1, keepdims=True) + NORM_EPSILON)
        normed = v * s
        scale = 1.0 + gain_ref[...]
        final = normed * scale
        valid_rows = valid_ref[...].astype(f32)
        error = full(read_ref[...], final, (1, 1)) - target_ref[...]
        counted = valid_rows * error
        back = 2.0 * counted
        rows_out[:act] = full(back, final, (1, 0))
        back_norm = full(back.T, read_ref[...], (1, 0))
        rows_out[act : act + 1] = jnp.sum(back_norm * normed, axis=0, keepdims=True)
        loss = jnp.sum(jnp.sum(counted * error, axis=0, keepdims=True), axis=1, keepdims=True)
        count = jnp.sum(jnp.sum(valid_rows, axis=0, keepdims=True), axis=1, keepdims=True)
        rows_out[act + 1 : act + 2] = jnp.broadcast_to(loss, (1, dim))
        rows_out[act + 2 : act + 3] = jnp.broadcast_to(count, (1, dim))
        scaled = back_norm * scale
        mean = jnp.mean(scaled * normed, axis=-1, keepdims=True)
        final_back = s * (scaled - normed * mean)
        final_out[...] = final_back
        branch_out[...] = final_back.astype(bf16)

    return pl.pallas_call(
        kernel,
        out_shape=[
            jax.ShapeDtypeStruct((tokens, dim), f32),
            jax.ShapeDtypeStruct((tokens, dim), bf16),
            jax.ShapeDtypeStruct((act + 3, dim), f32),
        ],
        compiler_params=pltpu.CompilerParams(vmem_limit_bytes=24 * MIB),
        cost_estimate=cost("readout_loss"),
        name="readout_loss",
    )(residual, branch_own, branch_oth, gain_row, readout, target, valid)


def on_device(
    ring,
    prefix_in,
    action_in,
    target,
    valid_mask,
    prefix_ids,
    action_ids,
    action_blocks,
    learning_rate,
    prefix_weight,
    attention_weight,
    feedforward_weight,
    prefix_gains,
    action_gains,
    readout_weight,
    prefix_weight_moment,
    attention_weight_moment,
    feedforward_weight_moment,
    prefix_gains_moment,
    action_gains_moment,
    readout_weight_moment,
    prefix_weight_average,
    attention_weight_average,
    feedforward_weight_average,
    prefix_gains_average,
    action_gains_average,
    readout_weight_average,
):
    core = lax.axis_index("wide") % 2
    rows_a, width_a = attention_weight.shape
    width_p = 2 * prefix_weight.shape[1]
    rows_p = prefix_weight.shape[0]
    n_right, n_left = ring.n_right, ring.n_left
    order, swap = Order(), ring.to_core

    def by_core(v, size):
        cut = v.reshape(v.shape[0], ring.chips, 2, size)
        cut = [cut[:, :, c].reshape(v.shape[0], ring.chips * size) for c in (0, 1)]
        return jnp.where(core == 0, cut[0], cut[1]), jnp.where(core == 0, cut[1], cut[0])

    def in_order(v, size):
        cut = v.reshape(2, ring.chips, size)
        return jnp.where(core == 0, cut, cut[::-1]).transpose(1, 0, 2).reshape(-1)

    def halves_of(v, axis):
        half = v.shape[axis] // 2
        if half % 16:
            return jnp.split(v, 2, axis)
        me = lax.axis_index("batch")
        return [lax.dynamic_slice_in_dim(v, at * half, half, axis) for at in (me, 1 - me)]

    prefix_bf = prefix_weight.astype(bf16)
    packed = jnp.concatenate(
        [attention_weight.astype(bf16), prefix_bf[:rows_a], prefix_bf[rows_a:]], axis=1
    )
    sides = [("right", d) for d in range(n_right)] + [("left", d) for d in range(n_left)]
    packed_halves = order(*halves_of(packed, 0))
    att = Gathering(ring, order, packed_halves, 0, True)
    att.start("right")
    att.start("left")
    ff_halves = order(*halves_of(jnp.transpose(feedforward_weight, (1, 0, 2)).astype(bf16), 1))
    ff = Gathering(ring, order, ff_halves, 1, False)
    side_of = {"R": "right", "L": "left"}

    def serve(step):
        for word in PLAN[step]:
            chain, what = {"a": att, "f": ff}[word[0]], word[1]
            if what == ">":
                chain.start(side_of[word[2]])
            elif what in side_of:
                chain.land(side_of[what])
            else:
                key = (side_of[word[2]], int(word[3]))
                (chain.cross if what == "X" else chain.settle)(key)

    ff.whole = order(ff.whole)
    own_parts = packed_halves if att.can else (packed,)
    prefix_rows = order(prefix_in[0])
    if rows_p % 128 == 0:
        pre_rel = order(norm_by_core(ring, prefix_rows, prefix_gains, rows_p))
    else:
        normed = rms_norm(prefix_rows.astype(f32), prefix_gains[0]).astype(bf16)
        pre_rel = order(jnp.concatenate(by_core(normed, rows_p), 1))
    serve("norm")
    action_rows = order(action_in[0]).astype(f32)
    action_norm = rms_norm(action_rows, action_gains[0]).astype(bf16)
    norm_mine, norm_other = order(*by_core(action_norm, rows_a))
    serve("action")
    norm_oth = order(swap(order(norm_other)))
    norm_rel = order(jnp.concatenate([norm_mine, norm_other], 1))
    serve("swapped")
    allowed = order(visible(prefix_ids[0], *order(action_ids[0], action_blocks[0])))
    serve("seen")
    while any(att.d[x] < att.count[x] for x in att.d):
        att.land("right", "left")
    att.settle(*[k for k in sides if len(att.blocks[k]) == 1])
    blocks = [own_parts] + [att.blocks[k] for k in sides]
    qkv_own, out_own, pre_own = order(*assemble(ring, blocks, rows_a, width_a))
    pre_oth, qkv_oth = swap(pre_own), swap(qkv_own)
    serve("assembled")

    prefix_kv = order(half_product(pre_rel, 0, order(pre_own), None))
    action_qkv = order(half_product(norm_rel, 0, order(qkv_own), None))
    serve("half")
    pre_oth, qkv_oth, out_own = order(pre_oth, qkv_oth, out_own)
    out_oth = swap(out_own)
    prefix_kv = order(half_product(pre_rel, 1, order(pre_oth), prefix_kv))
    action_qkv = order(half_product(norm_rel, 1, order(qkv_oth), action_qkv))
    serve("half2")
    out_own, out_oth = order(out_own, out_oth)
    out_weight = order(interleave(ring, out_own, out_oth, rows_a))
    serve("woven")
    action_qkv = order(action_qkv)
    part = order(attention(action_qkv, prefix_kv, allowed, 0, HEADS // 2, ()))
    serve("attended")
    part = order(part)
    mixed_heads = order(
        attention(action_qkv, prefix_kv, allowed, HEADS // 2, HEADS // 2, (part,))
    )
    mixed_oth = swap(mixed_heads)
    serve("attended2")
    mixed_heads = order(mixed_heads)
    residual = action_rows + mm(mixed_heads, out_weight, (1, 1))
    tokens = residual.shape[0]
    hidden_norm = rms_norm(residual, action_gains[1]).astype(bf16)
    residual, hidden_norm, mixed_oth = order(residual, hidden_norm, mixed_oth)
    norm_two = order(jnp.concatenate([hidden_norm, order(swap(hidden_norm))], 0))
    serve("normed")

    def weights(key):
        return (ff.whole,) if key[0] == "own" else ff.blocks[key]

    early = [("own", 0)] + [x for d in range(n_left - 1) for x in (("left", d), ("right", d))]
    late = [("right", n_left - 1), ("left", n_left - 1)]
    late += [("right", d) for d in range(n_left, n_right)]
    groups = [early, late]
    kept, branch = [], None
    for group in groups:
        for side, d in group:
            while side != "own" and ff.d[side] <= d:
                ff.land(side)
        ff.cross(*[k for k in group if k[0] != "own"])
        ff.settle(*[k for k in group if len(ff.blocks.get(k, ())) == 2])
        norm_two = order(norm_two)
        *values, own_rows, other_rows = ff_forward(norm_two, [weights(k) for k in group], branch)
        branch = order(own_rows, other_rows)
        kept.append(values)
        if group is early:
            serve("early")
    dim = action_rows.shape[1]
    branch_own, branch_oth = order(branch[0], swap(branch[1]))
    back_final, back_branch, small_rows = order(
        *readout_loss(
            residual,
            branch_own,
            branch_oth,
            action_gains[2:3],
            readout_weight.T,
            target[0].T,
            valid_mask[0].T,
        )
    )
    branch_two = order(jnp.concatenate([back_branch, swap(back_branch)], 0))
    act = readout_weight.shape[1]
    n_back = n_right + (n_left > 1)
    ff_sum = Summing(ring, order, 1, n_back)

    def way_back(key):
        side, d = key
        return ("right", ring.chips - 2 - d) if side == "left" and ring.chips - 2 - d < n_back else key

    own_key, back = ("own", 0), None
    att_sum = Summing(ring, order, 0, n_right)
    small_sum, swapped = None, {}

    def serve_back(step):
        nonlocal small_sum
        for word in PLAN[step]:
            chain, rest = (att_sum, word[1:]) if word[0] == "A" else (ff_sum, word)
            if word in ("q", "o"):
                if word in swapped:
                    swapped[word] = order(swapped[word])
            elif word == "Aown":
                while att_sum.d["left"] >= 0:
                    att_sum.step("left")
                att_sum.own(jnp.split(cut[0], 2, 0))
            elif rest in side_of:
                side = side_of[rest]
                if (side, chain.d[side]) in chain.parts:
                    chain.step(side)
            elif rest == "own":
                while ff_sum.d["left"] >= 0:
                    ff_sum.step("left")
                own_grads = [ff_sum.parts[own_key]]
                if ff.can:
                    own_grads.append(ff_sum.sends["own"].reshape(own_grads[0].shape))
                else:
                    own_grads = jnp.split(own_grads[0], 2, 1)
                ff_sum.own(own_grads)
            elif rest == "close":
                while ff_sum.d["right"] >= 0:
                    ff_sum.step("right")
                ff_sum.close()
            elif rest == "s":
                if small_sum is None:
                    small_sum = SmallSum(ring, order, small_rows)
                else:
                    small_sum.step()
            else:
                chain = att_sum if rest[1:] == "A" else ff_sum
                name = "all" if rest[1:] == "A" else rest[1:]
                (chain.cross if rest[0] == "x" else chain.ready)(name)

    for name, group, values in (("late", late, kept[1]), ("early", early, kept[0])):
        turned = [way_back(k) for k in group[::-1]]
        rights = sorted((k for k in turned if k[0] == "right"), key=lambda k: -k[1])
        if not ff.can:
            lists = {}
        elif name == "late":
            lists = {"first": rights[:1], "second": rights[1:2], "third": rights[2:]}
        else:
            lists = {"early": rights, "own": [own_key]}
        lists = {k: v for k, v in lists.items() if v}
        branch_two = order(branch_two)
        made, sent, back = ff_backward(
            norm_two,
            branch_two,
            [weights(k) for k in group[::-1]],
            [[turned.index(k) for k in keys] for keys in lists.values()],
            values,
            (len(group) - 1, -1),
            back,
        )
        flat = list(order(*back, *made, *sent))
        back, made, sent = flat[:2], flat[2 : 2 + len(turned)], flat[2 + len(turned) :]
        ff_sum.put(
            dict(zip(turned, made)),
            dict(zip(lists, sent)),
            {k: (n, i) for n, keys in lists.items() for i, k in enumerate(keys)},
        )
        if name == "late":
            serve_back("back_late")
    back_oth = swap(back[1])
    serve_back("back_early")
    back_own, back_oth = order(back[0], back_oth)
    back_attention, back_mixed, grad_gain_hidden = order(
        *mid_back(residual, back_final, back_own, back_oth, action_gains[1:2], out_weight)
    )
    serve_back("mid")
    back_mixed = order(back_mixed)
    part = order(
        *attention_back(action_qkv, prefix_kv, allowed, back_mixed, 0, HEADS // 2, ())
    )
    serve_back("back_a")
    attn_mine, attn_other = order(*by_core(order(back_attention), rows_a))
    attn_oth = swap(attn_other)
    serve_back("core")
    back_mixed, attn_oth, *part = order(back_mixed, attn_oth, *part)
    back_qkv, back_prefix_kv = order(
        *attention_back(action_qkv, prefix_kv, allowed, back_mixed, HEADS // 2, HEADS // 2, part)
    )
    swapped["q"] = swap(back_qkv)
    serve_back("back_b")

    swapped["o"] = swap(order(side_gradient(pre_rel, order(back_prefix_kv), 1)))
    serve_back("side")
    grad_output = order(pair_gradient((attn_mine, attn_oth), order(mixed_heads, mixed_oth)))
    serve_back("pair")
    cut = order(
        *disassemble(
            ring,
            att.can,
            (norm_mine, norm_oth),
            (back_qkv, order(swapped["q"])),
            pre_rel,
            back_prefix_kv,
            order(swapped["o"]),
            order(grad_output),
            rows_a,
        )
    )
    att_sum.put(
        dict(zip(sides, cut[1:])),
        {"all": cut[ring.chips]} if att.can else {},
        {("right", d): ("all", d) for d in range(n_right)} if att.can else {},
    )
    serve_back("cut")
    back_qkv, back_prefix_kv = order(back_qkv, back_prefix_kv)
    sums = order(
        gain_sums(back_qkv, norm_rel, qkv_own, qkv_oth),
        gain_sums(back_prefix_kv, pre_rel, pre_own, pre_oth),
    )
    grad_gain_action = in_order(sums[0][0], rows_a) / (1.0 + action_gains[0])
    grad_gain_prefix = in_order(sums[1][0], rows_p) / (1.0 + prefix_gains[0])
    late_rows = order(grad_gain_prefix.reshape(-1, dim), grad_gain_action[None], grad_gain_hidden)
    small_rows = [small_rows, *late_rows]
    serve_back("gains")
    serve_back("tail")
    while att_sum.d["right"] >= 0:
        att_sum.step("right")
    if small_sum is None:
        small_sum = SmallSum(ring, order, small_rows)
    while small_sum.step():
        pass
    ff_total = ff_sum.result()
    small = small_sum.total
    n_pre = grad_gain_prefix.shape[0] // dim
    count = small[act + 2, 0]
    loss_value = small[act + 1, 0] / count
    scale = 1.0 / count
    step_rate = learning_rate[0]
    third = order(
        *advance(
            feedforward_weight,
            feedforward_weight_moment,
            feedforward_weight_average,
            jnp.transpose(ff_total, (1, 0, 2)) * scale,
            step_rate,
        )
    )
    att_sum.close()
    packed_total = att_sum.result()
    first = advance(
        prefix_weight,
        prefix_weight_moment,
        prefix_weight_average,
        jnp.concatenate(
            [
                packed_total[:, width_a : width_a + width_p // 2],
                packed_total[:, width_a + width_p // 2 :],
            ],
            0,
        )
        * scale,
        step_rate,
    )
    second = advance(
        attention_weight,
        attention_weight_moment,
        attention_weight_average,
        packed_total[:, :width_a] * scale,
        step_rate,
    )
    fourth = advance(
        prefix_gains,
        prefix_gains_moment,
        prefix_gains_average,
        small[act + 3 : act + 3 + n_pre].reshape(1, -1) * scale,
        step_rate,
    )
    fifth = advance(
        action_gains,
        action_gains_moment,
        action_gains_average,
        jnp.concatenate([small[act + 3 + n_pre :], small[act : act + 1]], 0) * scale,
        step_rate,
    )
    sixth = advance(
        readout_weight,
        readout_weight_moment,
        readout_weight_average,
        small[:act].T * scale,
        step_rate,
    )
    loss_value = loss_value + order.token.astype(f32)
    return (loss_value,) + tuple(
        group[i]
        for i in range(3)
        for group in (first, second, third, fourth, fifth, sixth)
    )


def solution(mesh):
    rows = P(("batch", "wide"))
    wide = P("wide")
    whole = P()
    weights = (wide, wide, wide, whole, whole, whole)
    return jax.shard_map(
        functools.partial(on_device, Ring(mesh.shape["wide"])),
        mesh=mesh,
        in_specs=(rows,) * 7 + (whole,) + weights * 3,
        out_specs=(whole,) + weights * 3,
        check_vma=False,
    )
```

```python
import functools
import math

import jax
import jax.numpy as jnp
import numpy as np
from jax import lax
from jax.experimental import pallas as pl
from jax.experimental.pallas import tpu as pltpu
from jax.sharding import PartitionSpec as P

HEADS = 8
HEAD_DIM = 256
QUERY_WIDTH = HEADS * HEAD_DIM
QKV_WIDTH = QUERY_WIDTH + 2 * HEAD_DIM
SCORE_SCALE = HEAD_DIM ** (-0.5)

NORM_EPSILON = 1e-06
MOMENTUM = 0.9
AVERAGE_DECAY = 0.8
NEGATIVE = -1e30

bf16 = jnp.bfloat16
f32 = jnp.float32
HIGHEST = lax.Precision.HIGHEST
MIB = 2**20
CUT = 512
PLAN = dict(
    norm=("aR", "aL", "aXR0", "aXL0", "aR"),
    action=("aL", "aSL0", "aXL1", "aR", "aXR1", "aSR0", "aL", "f>L", "aSL1", "aR", "aXR2", "f>R", "aXR3"),
    swapped=("aSR1", "aXL2", "aSR2", "aSL2"),
    seen=("fR", "fXR0", "fL", "aSR3"),
    assembled=(),
    half=(),
    half2=("fSR0", "fR", "fXR1"),
    woven=(),
    attended=(),
    attended2=("fR", "fSR1", "fXR2", "fL"),
    normed=(),
    early=("fR", "fSR2", "fXR3"),
    back_late=("xfirst", "xsecond"),
    back_early=("R", "L"),
    mid=(),
    back_a=(),
    core=("R", "xearly", "xthird"),
    back_b=("rthird", "L"),
    side=("q", "R", "o"),
    pair=(),
    cut=("xA", "AL"),
    gains=("R",),
    tail=(
        "s", "own", "R", "rA", "AR", "s", "AL", "s", "AR",
        "AL", "close", "s", "AR", "s", "AR", "AL", "AR", "Aown",
    ),
)
COST = dict(
    add=11, assemble=11, half_product=11, gain_sums=11, pair_gradient=11, side_gradient=11,
    disassemble=11, norm_by_core=11, ff_forward=9, ff_backward=0, attention=11, attention_back=8,
    mid_back=8, interleave=11, readout_loss=11,
)


def cost(name):
    return pl.CostEstimate(flops=10 ** COST[name], transcendentals=0, bytes_accessed=1)


def rms_norm(stream, gain_row):
    return (
        stream
        * lax.rsqrt(jnp.mean(stream * stream, axis=-1, keepdims=True) + NORM_EPSILON)
        * (1.0 + gain_row)
    )


def norm_back(stream, gain_row, cotangent):
    _, pull = jax.vjp(rms_norm, stream, gain_row)
    return pull(cotangent)


def gated_unit(gate_value, linear_value):
    return jax.nn.gelu(gate_value, approximate=True) * linear_value


def visible(prefix_ids, action_ids, block_flags):
    length = block_flags.shape[0]
    place = jnp.arange(length)
    upto = place[None, :] <= place[:, None]
    levels = jnp.sum(jnp.where(upto, block_flags[None, :], 0), axis=1)
    from_prefix = prefix_ids[:, None] == action_ids[None, :]
    from_action = (action_ids[:, None] == action_ids[None, :]) & (
        levels[:, None] <= levels[None, :]
    )
    return jnp.concatenate([from_prefix, from_action], axis=0).astype(jnp.int32)


def advance(weight, moment, average, gradient, step_rate):
    moment_next = MOMENTUM * moment + gradient
    weight_next = weight - step_rate * (gradient + MOMENTUM * moment_next)
    average_next = AVERAGE_DECAY * average + (1.0 - AVERAGE_DECAY) * weight_next
    return (weight_next, moment_next, average_next)


def mm(a, b, contract, out=f32):
    return lax.dot_general(
        a, b, (((contract[0],), (contract[1],)), ((), ())), preferred_element_type=f32
    ).astype(out)


class Order:
    def __init__(self):
        self.token = jnp.zeros((), jnp.int32)

    def __call__(self, *values):
        *values, self.token = lax.optimization_barrier((*values, self.token))
        return values[0] if len(values) == 1 else values


class Ring:
    def __init__(self, wide):
        chips = wide // 2
        self.wide, self.chips = wide, chips
        self.cycle = list(range(0, chips, 2)) + list(range(1, chips, 2))[::-1]
        ahead = [(self.cycle[i], self.cycle[(i + 1) % chips]) for i in range(chips)]
        self.right = [(2 * s + c, 2 * t + c) for s, t in ahead for c in (0, 1)]
        self.left = [(t, s) for s, t in self.right]
        self.core = [(w, w ^ 1) for w in range(wide)]
        self.n_right = chips // 2
        self.n_left = chips - 1 - self.n_right

    def to_right(self, v):
        return lax.ppermute(v, "wide", self.right)

    def to_left(self, v):
        return lax.ppermute(v, "wide", self.left)

    def to_core(self, v):
        return lax.ppermute(v, "wide", self.core)

    def to_peer(self, v):
        return lax.ppermute(v, "batch", [(0, 1), (1, 0)])

    def owners(self, w):
        here = self.cycle.index(w // 2)
        rights = [self.cycle[(here - d) % self.chips] for d in range(1, self.n_right + 1)]
        lefts = [self.cycle[(here + d) % self.chips] for d in range(1, self.n_left + 1)]
        return [w // 2] + rights + lefts

    def bits(self):
        k, steps = 1, [self.to_peer]
        while k < self.wide:
            pairs = [(w, w ^ k) for w in range(self.wide)]
            steps.append(functools.partial(lax.ppermute, axis_name="wide", perm=pairs))
            k *= 2
        return steps


def add(*terms, step=None):
    terms = [t if isinstance(t, tuple) else (t, 0, 1) for t in terms]
    shape = terms[0][0].shape
    cols = shape[-1]
    rows = math.prod(shape[:-1])
    if step is None:
        step = 128 if rows % 128 == 0 and rows > 128 else rows

    def kernel(*refs):
        refs[-1][...] = sum(r[...].astype(f32) for r in refs[:-1]).astype(bf16)

    def block(k, stride):
        return pl.BlockSpec((step, cols), lambda i: (stride * i + k, 0))

    return pl.pallas_call(
        kernel,
        out_shape=jax.ShapeDtypeStruct((rows, cols), bf16),
        grid=(rows // step,),
        in_specs=[block(k, stride) for _, k, stride in terms],
        out_specs=block(0, 1),
        compiler_params=pltpu.CompilerParams(vmem_limit_bytes=8 * MIB),
        cost_estimate=cost("add"),
        name="add",
    )(*[t.reshape(-1, cols) for t, _, _ in terms]).reshape(shape)


class SmallSum:
    def __init__(self, ring, order, rows):
        self.order, self.steps = order, ring.bits()
        self.total = order(jnp.concatenate(rows, 0))
        self.moved = self.steps.pop(0)(self.total)

    def step(self):
        if self.moved is None:
            return False
        total, moved = self.order(self.total, self.moved)
        self.total = self.order(total + moved)
        self.moved = self.steps.pop(0)(self.total) if self.steps else None
        return True


class Gathering:
    def __init__(self, ring, order, halves, axis, split_left):
        self.ring, self.order = ring, order
        self.halves, self.split_left = halves, split_left
        self.whole = jnp.concatenate(halves, axis)
        self.can = halves[0].shape[axis] % 16 == 0
        self.blocks, self.flying = {}, {}
        self.count = {"right": ring.n_right, "left": ring.n_left}
        self.d = {"right": 0, "left": 0}

    def cut(self, side):
        return self.can and (side == "right" or self.split_left)

    def start(self, side):
        self.send(side, self.order(self.halves[0] if self.cut(side) else self.whole))

    def send(self, side, v):
        self.flying[side] = self.ring.to_right(v) if side == "right" else self.ring.to_left(v)

    def land(self, *sides):
        sides = [x for x in sides if self.d[x] < self.count[x] and x in self.flying]
        if not sides:
            return
        came = self.order(*[self.flying[x] for x in sides])
        for side, v in zip(sides, came if len(sides) > 1 else [came]):
            self.blocks[side, self.d[side]] = (v,)
            self.d[side] += 1
            if self.d[side] < self.count[side]:
                self.send(side, v)

    def cross(self, *keys):
        for key in keys:
            if self.cut(key[0]) and len(self.blocks.get(key, (0, 0))) == 1:
                (v,) = self.blocks[key]
                v = self.order(v)
                self.blocks[key] = (v, self.ring.to_peer(v))

    def settle(self, *keys):
        for key in keys:
            if key in self.blocks:
                self.cross(key)
                self.blocks[key] = tuple(self.order(p) for p in self.blocks[key])


class Summing:
    def __init__(self, ring, order, axis, n_right):
        self.ring, self.order, self.axis = ring, order, axis
        self.parts, self.sends, self.spots, self.crossed = {}, {}, {}, {}
        self.came = {"right": None, "left": None}
        self.d = {"right": n_right - 1, "left": ring.chips - 2 - n_right}

    def put(self, parts, sends, spots):
        self.parts.update(parts)
        self.sends.update(sends)
        self.spots.update(spots)

    def cross(self, *names):
        for name in names:
            if name in self.sends and name not in self.crossed:
                self.crossed[name] = self.ring.to_peer(self.order(self.sends[name]))

    def ready(self, *names):
        for name in names:
            if name in self.crossed:
                self.crossed[name] = self.order(self.crossed[name])

    def step(self, *sides):
        for side in sides:
            d = self.d[side]
            if d < 0:
                continue
            terms = [self.parts[side, d]]
            terms += [self.came[side]] if self.came[side] is not None else []
            if (side, d) in self.spots:
                name, spot = self.spots[side, d]
                self.cross(name)
                *terms, self.crossed[name] = self.order(*terms, self.crossed[name])
                rows = math.prod(self.parts[side, d].shape[:-1])
                step = 128 if rows % 128 == 0 and rows > 128 else rows
                terms.append((self.crossed[name], spot * (rows // step), 1))
            else:
                terms = self.order(*terms)
                terms = list(terms) if isinstance(terms, (list, tuple)) else [terms]
            total = self.order(add(*terms)) if len(terms) > 1 else terms[0]
            self.came[side] = self.ring.to_left(total) if side == "right" else self.ring.to_right(total)
            self.d[side] = d - 1

    def land(self, side):
        self.came[side] = self.order(self.came[side])

    def left(self):
        return max(self.d.values()) + 1

    def own(self, halves):
        left = self.order(self.came["left"])
        half = halves[0].shape[self.axis]
        self.split = bool(self.spots)
        if self.split:
            stride = 2 if self.axis else 1
            self.rows = half
            self.mine = [halves[0], (left, 0, stride)]
            other = self.order(add(halves[1], (left, 1, stride), step=half))
            self.across = self.ring.to_peer(other)
        else:
            self.mine = [self.order(add(jnp.concatenate(halves, self.axis), left))]
            self.rows = None

    def close(self):
        self.came["right"] = self.order(self.came["right"])
        terms = self.mine + [self.came["right"]]
        if self.split:
            self.across = self.order(self.across)
            terms.append(self.across)
        self.total = self.order(add(*terms, step=self.rows))
        self.across = self.ring.to_peer(self.total)

    def result(self):
        me = lax.axis_index("batch")
        total, across = [v.astype(f32) for v in self.order(self.total, self.across)]
        if not self.split:
            return total + across
        return jnp.where(
            me == 0,
            jnp.concatenate([total, across], self.axis),
            jnp.concatenate([across, total], self.axis),
        )


def places(ring, counts, rows):
    table = np.zeros((2, ring.wide, 2, sum(counts)), np.int32)
    for me in (0, 1):
        for w in range(ring.wide):
            where, first = [], []
            for owner, n in zip(ring.owners(w), counts):
                where += [owner] * n
                first += [me * rows // 2, (1 - me) * rows // 2] if n == 2 else [0]
            table[me, w] = where, first
    return jnp.array(table)[lax.axis_index("batch"), lax.axis_index("wide")]


def assemble(ring, blocks, rows, width_a):
    counts = [len(b) for b in blocks]
    parts = [p for b in blocks for p in b]
    n = len(parts)
    table = places(ring, counts, rows)
    side_rows = rows * ring.chips
    pw = (parts[0].shape[1] - width_a) // 2
    shapes = ((side_rows, QKV_WIDTH), (side_rows, width_a - QKV_WIDTH), (2 * side_rows, pw))

    def kernel(table_ref, *refs):
        ins, (qkv, out, pre, sems) = refs[:n], refs[n:]
        copies = []

        def copy(i, start, width, to, row):
            size = parts[i].shape[0]
            target = to.at[pl.ds(pl.multiple_of(row, size), size), :]
            copies.append(
                pltpu.make_async_copy(ins[i].at[:, pl.ds(start, width)], target, sems.at[len(copies)])
            )

        for i in range(n):
            chip, first = table_ref[0, i], table_ref[1, i]
            copy(i, 0, QKV_WIDTH, qkv, chip * rows + first)
            copy(i, QKV_WIDTH, width_a - QKV_WIDTH, out, chip * rows + first)
            for j in (0, 1):
                copy(i, width_a + j * pw, pw, pre, (2 * chip + j) * rows + first)
        for c in copies:
            c.start()
        for c in copies:
            c.wait()

    return pl.pallas_call(
        kernel,
        out_shape=[jax.ShapeDtypeStruct(sh, bf16) for sh in shapes],
        grid_spec=pltpu.PrefetchScalarGridSpec(
            num_scalar_prefetch=1,
            grid=(1,),
            in_specs=[pl.BlockSpec(memory_space=pl.ANY)] * n,
            out_specs=[pl.BlockSpec(sh, lambda i, t: (0, 0)) for sh in shapes],
            scratch_shapes=[pltpu.SemaphoreType.DMA((4 * n,))],
        ),
        compiler_params=pltpu.CompilerParams(vmem_limit_bytes=14 * MIB),
        cost_estimate=cost("assemble"),
        name="assemble",
    )(table, *parts)


def interleave(ring, own, other, rows):
    core = (lax.axis_index("wide") % 2).reshape(1)

    def kernel(core_ref, own_ref, other_ref, out_ref, sems):
        copies = []
        for chip in range(ring.chips):
            for j, ref in enumerate((own_ref, other_ref)):
                side = core_ref[0] if j == 0 else 1 - core_ref[0]
                to = pl.ds(pl.multiple_of((2 * chip + side) * rows, rows), rows)
                copies.append(
                    pltpu.make_async_copy(
                        ref.at[pl.ds(chip * rows, rows), :], out_ref.at[to, :], sems.at[chip, j]
                    )
                )
        for c in copies:
            c.start()
        for c in copies:
            c.wait()

    shape = (2 * own.shape[0], own.shape[1])
    return pl.pallas_call(
        kernel,
        out_shape=jax.ShapeDtypeStruct(shape, bf16),
        grid_spec=pltpu.PrefetchScalarGridSpec(
            num_scalar_prefetch=1,
            grid=(1,),
            in_specs=[pl.BlockSpec(memory_space=pl.ANY)] * 2,
            out_specs=pl.BlockSpec(shape, lambda i, t: (0, 0)),
            scratch_shapes=[pltpu.SemaphoreType.DMA((ring.chips, 2))],
        ),
        compiler_params=pltpu.CompilerParams(vmem_limit_bytes=12 * MIB),
        cost_estimate=cost("interleave"),
        name="interleave",
    )(core, own, other)


def side_gradient(rows, cols, which=0):
    tokens, width = rows.shape[0], rows.shape[1] // 2

    def kernel(rows_ref, cols_ref, out_ref):
        out_ref[...] = mm(rows_ref[...], cols_ref[...], (0, 0), bf16)

    return pl.pallas_call(
        kernel,
        out_shape=jax.ShapeDtypeStruct((width, cols.shape[1]), bf16),
        grid=(1,),
        in_specs=[
            pl.BlockSpec((tokens, width), lambda i: (0, which)),
            pl.BlockSpec(cols.shape, lambda i: (0, 0)),
        ],
        out_specs=pl.BlockSpec((width, cols.shape[1]), lambda i: (0, 0)),
        compiler_params=pltpu.CompilerParams(vmem_limit_bytes=14 * MIB),
        cost_estimate=cost("side_gradient"),
        name="side_gradient",
    )(rows, cols)


def half_product(rows, side, weight, before):
    tokens, width = rows.shape[0], rows.shape[1] // 2
    cols = weight.shape[1]
    kind = f32 if before is None else bf16

    def kernel(rows_ref, weight_ref, *refs):
        out_ref = refs[-1]
        for c in range(cols // CUT):
            at = slice(c * CUT, (c + 1) * CUT)
            total = mm(rows_ref[...], weight_ref[:, at], (1, 0))
            out_ref[:, at] = (total if before is None else total + refs[0][:, at]).astype(kind)

    extra = [] if before is None else [before]
    return pl.pallas_call(
        kernel,
        out_shape=jax.ShapeDtypeStruct((tokens, cols), kind),
        grid=(1,),
        in_specs=[
            pl.BlockSpec((tokens, width), lambda i: (0, side)),
            pl.BlockSpec(weight.shape, lambda i: (0, 0)),
        ]
        + [pl.BlockSpec((tokens, cols), lambda i: (0, 0)) for _ in extra],
        out_specs=pl.BlockSpec((tokens, cols), lambda i: (0, 0)),
        compiler_params=pltpu.CompilerParams(vmem_limit_bytes=30 * MIB),
        cost_estimate=cost("half_product"),
        name="half_product",
    )(rows, weight, *extra)


def gain_sums(back, rows, own, other):
    tokens, width = rows.shape[0], rows.shape[1] // 2
    cols = own.shape[1]
    step = 256

    def kernel(back_ref, rows_ref, own_ref, other_ref, out_ref):
        @pl.when(pl.program_id(0) == 0)
        def _():
            out_ref[...] = jnp.zeros_like(out_ref)

        for side, ref in enumerate((own_ref, other_ref)):
            at = slice(side * width, (side + 1) * width)
            total = mm(back_ref[...], ref[...], (1, 1)) * rows_ref[:, at].astype(f32)
            out_ref[:, at] += jnp.sum(total, axis=0, keepdims=True)

    return pl.pallas_call(
        kernel,
        out_shape=jax.ShapeDtypeStruct((1, 2 * width), f32),
        grid=(tokens // step,),
        in_specs=[
            pl.BlockSpec((step, cols), lambda i: (i, 0)),
            pl.BlockSpec((step, 2 * width), lambda i: (i, 0)),
        ]
        + [pl.BlockSpec(w.shape, lambda i: (0, 0)) for w in (own, other)],
        out_specs=pl.BlockSpec((1, 2 * width), lambda i: (0, 0)),
        compiler_params=pltpu.CompilerParams(vmem_limit_bytes=20 * MIB),
        cost_estimate=cost("gain_sums"),
        name="gain_sums",
    )(back, rows, own, other)


def pair_gradient(rows, cols):
    width, step = rows[0].shape[1], 512

    def kernel(r0, r1, c0, c1, out_ref):
        out_ref[...] = (mm(r0[...], c0[...], (0, 0)) + mm(r1[...], c1[...], (0, 0))).astype(bf16)

    once = [pl.BlockSpec(r.shape, lambda i: (0, 0)) for r in rows]
    return pl.pallas_call(
        kernel,
        out_shape=jax.ShapeDtypeStruct((width, cols[0].shape[1]), bf16),
        grid=(cols[0].shape[1] // step,),
        in_specs=once + [pl.BlockSpec((c.shape[0], step), lambda i: (0, i)) for c in cols],
        out_specs=pl.BlockSpec((width, step), lambda i: (0, i)),
        compiler_params=pltpu.CompilerParams(vmem_limit_bytes=14 * MIB),
        cost_estimate=cost("pair_gradient"),
        name="pair_gradient",
    )(*rows, *cols)


def disassemble(ring, halved, norm_rows, qkv_back, pre_rel, back_prefix_kv, other_side, grad_output, rows):
    cuts = 2 if halved else 1
    size = rows // cuts
    table = places(ring, [cuts] * ring.chips, rows)
    spots, sizes = [], []
    for j in range(ring.chips):
        right = 1 <= j <= ring.n_right
        sizes.append(size if right else rows)
        if right and halved:
            spots += [(j, 0), (ring.chips, (j - 1) * size)]
        else:
            spots += [(j, k * size) for k in range(cuts)]
    if halved:
        sizes.append(ring.n_right * size)
    n = len(sizes)
    side_rows = rows * ring.chips
    pre_cols = back_prefix_kv.shape[1]
    out_cols = grad_output.shape[1]
    width = QKV_WIDTH + out_cols + 2 * pre_cols
    step = 512

    def kernel(table_ref, n0, n1, q0, q1, pre_ref, back_ref, side_ref, out_ref, *refs):
        parts, (qkv_sum, pre_sum, sems) = refs[:n], refs[n:]

        def copies(i, k):
            chip, first = table_ref[0, i], table_ref[1, i]
            part, top = spots[i]

            def piece(ref, row, at, w, j):
                source = ref.at[pl.ds(pl.multiple_of(row, size), size), :]
                target = parts[part].at[pl.ds(top, size), pl.ds(at, w)]
                return pltpu.make_async_copy(source, target, sems.at[i, j])

            if k == 0:
                return [piece(out_ref, chip * rows + first, QKV_WIDTH, out_cols, 0)]
            if k == 1:
                at = QKV_WIDTH + out_cols
                return [
                    piece(pre_sum, (2 * chip + j) * rows + first, at + j * pre_cols, pre_cols, 1 + j)
                    for j in (0, 1)
                ]
            return [piece(qkv_sum, chip * rows + first, 0, QKV_WIDTH, 3)]

        def start(k):
            for i in range(len(spots)):
                for c in copies(i, k):
                    c.start()

        start(0)
        total = mm(pre_ref[...], back_ref[...], (0, 0)) + side_ref[...].astype(f32)
        pre_sum[...] = total.astype(bf16)
        start(1)
        for c in range(QKV_WIDTH // step):
            at = slice(c * step, (c + 1) * step)
            total = mm(n0[...], q0[:, at], (0, 0)) + mm(n1[...], q1[:, at], (0, 0))
            qkv_sum[:, at] = total.astype(bf16)
        start(2)
        for i in range(len(spots)):
            for k in (0, 1, 2):
                for c in copies(i, k):
                    c.wait()

    def once(v):
        return pl.BlockSpec(v.shape, lambda i, t: (0, 0))

    tokens = pre_rel.shape[0]
    out = pl.pallas_call(
        kernel,
        out_shape=[jax.ShapeDtypeStruct((size, width), bf16) for size in sizes],
        grid_spec=pltpu.PrefetchScalarGridSpec(
            num_scalar_prefetch=1,
            grid=(1,),
            in_specs=[once(v) for v in (*norm_rows, *qkv_back)]
            + [pl.BlockSpec((tokens, 2 * side_rows), lambda i, t: (0, 0))]
            + [once(v) for v in (back_prefix_kv, other_side, grad_output)],
            out_specs=[pl.BlockSpec(memory_space=pltpu.HBM)] * n,
            scratch_shapes=[
                pltpu.VMEM((side_rows, QKV_WIDTH), bf16),
                pltpu.VMEM((2 * side_rows, pre_cols), bf16),
                pltpu.SemaphoreType.DMA((len(spots), 4)),
            ],
        ),
        compiler_params=pltpu.CompilerParams(vmem_limit_bytes=22 * MIB),
        cost_estimate=cost("disassemble"),
        name="disassemble",
    )(table, *norm_rows, *qkv_back, pre_rel, back_prefix_kv, other_side, grad_output)
    return out


def norm_by_core(ring, rows, gains, size):
    core = (lax.axis_index("wide") % 2).reshape(1)
    tokens, dim = rows.shape
    step = 128

    def kernel(core_ref, rows_ref, gains_ref, out_ref):
        v = rows_ref[...].astype(f32)
        normed = rms_norm(v, gains_ref[0]).astype(bf16)
        for swapped in (0, 1):

            @pl.when(core_ref[0] == swapped)
            def _(swapped=swapped):
                for chip in range(ring.chips):
                    for side in (0, 1):
                        at = (2 * chip + (side ^ swapped)) * size
                        to = side * (dim // 2) + chip * size
                        out_ref[:, to : to + size] = normed[:, at : at + size]

    return pl.pallas_call(
        kernel,
        out_shape=jax.ShapeDtypeStruct((tokens, dim), bf16),
        grid_spec=pltpu.PrefetchScalarGridSpec(
            num_scalar_prefetch=1,
            grid=(tokens // step,),
            in_specs=[
                pl.BlockSpec((step, dim), lambda i, t: (i, 0)),
                pl.BlockSpec((1, dim), lambda i, t: (0, 0)),
            ],
            out_specs=pl.BlockSpec((step, dim), lambda i, t: (i, 0)),
        ),
        compiler_params=pltpu.CompilerParams(vmem_limit_bytes=12 * MIB),
        cost_estimate=cost("norm_by_core"),
        name="norm_by_core",
    )(core, rows, gains)


def gelu_parts(v):
    c = math.sqrt(2.0 / math.pi)
    square = v * v
    t = jnp.tanh(c * v * (1.0 + 0.044715 * square))
    half = 0.5 * (1.0 + t)
    slope = half + 0.5 * v * (1.0 - t * t) * c * (1.0 + 3.0 * 0.044715 * square)
    return v * half, slope


def load_block(refs, buf, sems, k):
    at, made = 0, []
    for j, r in enumerate(refs):
        size = r.shape[1]
        made.append(pltpu.make_async_copy(r, buf.at[:, pl.ds(at, size), :], sems.at[k, j]))
        at += size
    return made


def ff_forward(norm_two, blocks, before):
    nb = len(blocks)
    flat = [a for blk in blocks for a in blk]
    tokens, dim = norm_two.shape
    units = sum(a.shape[1] for a in blocks[0])
    half = tokens // 2
    has_before = before is not None

    def kernel(norm_ref, *refs):
        refs = list(refs)
        ins = [[refs.pop(0) for _ in blk] for blk in blocks]
        if has_before:
            own_in, oth_in = refs.pop(0), refs.pop(0)
        gate_out, lin_out, hid_out, own_out, oth_out, buf, total, sems = refs
        i = pl.program_id(0)

        @pl.when(i == 0)
        def _():
            for k in range(nb):
                for c in load_block(ins[k], buf.at[k], sems, k):
                    c.start()
            if has_before:
                total[:half] = own_in[...]
                total[half:] = oth_in[...]
            else:
                total[...] = jnp.zeros_like(total)

        for k in range(nb):

            @pl.when(i == k)
            def _(k=k):
                for c in load_block(ins[k], buf.at[k], sems, k):
                    c.wait()

        w = buf.at[i]
        if units % 128 == 0:
            both = mm(norm_ref[...], w[:2].reshape(2 * units, dim), (1, 1))
            gate, linear = both[:, :units], both[:, units:]
        else:
            gate, linear = (mm(norm_ref[...], w[j], (1, 1)) for j in (0, 1))
        gate_out[0] = gate
        lin_out[0] = linear
        hidden = (gelu_parts(gate)[0] * linear).astype(bf16)
        hid_out[0] = hidden
        total[...] += mm(hidden, w[2], (1, 0))

        @pl.when(i == nb - 1)
        def _():
            own_out[...] = total[:half]
            oth_out[...] = total[half:]

    once = pl.BlockSpec((tokens, dim), lambda i: (0, 0))
    row = pl.BlockSpec((half, dim), lambda i: (0, 0))
    step = pl.BlockSpec((1, tokens, units), lambda i: (i, 0, 0))
    any_space = pl.BlockSpec(memory_space=pl.ANY)
    return pl.pallas_call(
        kernel,
        out_shape=[
            jax.ShapeDtypeStruct((nb, tokens, units), f32),
            jax.ShapeDtypeStruct((nb, tokens, units), f32),
            jax.ShapeDtypeStruct((nb, tokens, units), bf16),
            jax.ShapeDtypeStruct((half, dim), f32),
            jax.ShapeDtypeStruct((half, dim), f32),
        ],
        grid=(nb,),
        in_specs=[once] + [any_space] * len(flat) + [row, row] * has_before,
        out_specs=[step, step, step, row, row],
        scratch_shapes=[
            pltpu.VMEM((nb, 3, units, dim), bf16),
            pltpu.VMEM((tokens, dim), f32),
            pltpu.SemaphoreType.DMA((nb, 2)),
        ],
        compiler_params=pltpu.CompilerParams(vmem_limit_bytes=22 * MIB),
        cost_estimate=cost("ff_forward"),
        name="ff_forward",
    )(norm_two, *flat, *(before or ()))


def ff_backward(norm_two, branch_two, blocks, sends, kept, picks, before):
    nb = len(blocks)
    flat = [a for blk in blocks for a in blk]
    gate_all, lin_all, hid_all = kept
    tokens, dim = norm_two.shape
    units = sum(a.shape[1] for a in blocks[0])
    half = tokens // 2
    has_before = before is not None
    first, stride = picks

    def kernel(norm_ref, branch_ref, gate_ref, lin_ref, hid_ref, *refs):
        refs = list(refs)
        ins = [[refs.pop(0) for _ in blk] for blk in blocks]
        if has_before:
            own_in, oth_in = refs.pop(0), refs.pop(0)
        outs = [[refs.pop(0)] for _ in blocks]
        for keys in sends:
            ref = refs.pop(0)
            for spot, k in enumerate(keys):
                outs[k].append(ref.at[spot])
        own_out, oth_out, buf, grads, total, sems, out_sems = refs
        i = pl.program_id(0)

        def stores(k):
            at, made = 0, []
            for j, r in enumerate(outs[k]):
                size = r.shape[1]
                made.append(pltpu.make_async_copy(grads.at[k, :, pl.ds(at, size), :], r, out_sems.at[k, j]))
                at += size
            return made

        @pl.when(i == 0)
        def _():
            for k in range(nb):
                for c in load_block(ins[k], buf.at[k], sems, k):
                    c.start()
            if has_before:
                total[:half] = own_in[...]
                total[half:] = oth_in[...]
            else:
                total[...] = jnp.zeros_like(total)

        for k in range(nb):

            @pl.when(i == k)
            def _(k=k):
                for c in load_block(ins[k], buf.at[k], sems, k):
                    c.wait()

        w, g = buf.at[i], grads.at[i]
        back_hidden = mm(branch_ref[...], w[2], (1, 1))
        value, slope = gelu_parts(gate_ref[0])
        back_gate = (back_hidden * lin_ref[0] * slope).astype(bf16)
        back_linear = (back_hidden * value).astype(bf16)
        if units % 128 == 0:
            both = jnp.concatenate([back_gate, back_linear], 1)
            g[:2] = mm(both, norm_ref[...], (0, 0), bf16).reshape(2, units, dim)
            total[...] += mm(both, w[:2].reshape(2 * units, dim), (1, 0))
        else:
            for j, back in enumerate((back_gate, back_linear)):
                g[j] = mm(back, norm_ref[...], (0, 0), bf16)
                total[...] += mm(back, w[j], (1, 0))
        g[2] = mm(hid_ref[0], branch_ref[...], (0, 0), bf16)

        for k in range(nb):

            @pl.when(i == k)
            def _(k=k):
                for c in stores(k):
                    c.start()

        @pl.when(i == nb - 1)
        def _():
            own_out[...] = total[:half]
            oth_out[...] = total[half:]
            for k in range(nb):
                for c in stores(k):
                    c.wait()

    once = pl.BlockSpec((tokens, dim), lambda i: (0, 0))
    row = pl.BlockSpec((half, dim), lambda i: (0, 0))
    step = pl.BlockSpec((1, tokens, units), lambda i: (first + stride * i, 0, 0))
    any_space = pl.BlockSpec(memory_space=pl.ANY)
    hbm = pl.BlockSpec(memory_space=pltpu.HBM)
    made = pl.pallas_call(
        kernel,
        out_shape=[
            jax.ShapeDtypeStruct((3, units // (2 if any(k in x for x in sends) else 1), dim), bf16)
            for k in range(nb)
        ]
        + [jax.ShapeDtypeStruct((len(x), 3, units // 2, dim), bf16) for x in sends]
        + [jax.ShapeDtypeStruct((half, dim), f32)] * 2,
        grid=(nb,),
        in_specs=[once, once, step, step, step] + [any_space] * len(flat) + [row, row] * has_before,
        out_specs=[hbm] * (nb + len(sends)) + [row, row],
        scratch_shapes=[
            pltpu.VMEM((nb, 3, units, dim), bf16),
            pltpu.VMEM((nb, 3, units, dim), bf16),
            pltpu.VMEM((tokens, dim), f32),
            pltpu.SemaphoreType.DMA((nb, 2)),
            pltpu.SemaphoreType.DMA((nb, 2)),
        ],
        compiler_params=pltpu.CompilerParams(vmem_limit_bytes=36 * MIB),
        cost_estimate=cost("ff_backward"),
        name="ff_backward",
    )(norm_two, branch_two, gate_all, lin_all, hid_all, *flat, *(before or ()))
    made = list(made)
    return made[:nb], made[nb:-2], made[-2:]


def attention(action_qkv, prefix_kv, allowed, first, heads, before):
    tokens, keys = action_qkv.shape[0], allowed.shape[0]
    n_pre = prefix_kv.shape[0]

    def kernel(q_ref, kv_ref, pre_ref, allowed_ref, *refs):
        out_ref, k_all, v_turned = refs[-3:]
        h = pl.program_id(0)

        @pl.when(h == 0)
        def _():
            k_all[:n_pre] = pre_ref[:, :HEAD_DIM]
            k_all[n_pre:] = kv_ref[:, :HEAD_DIM]
            v_turned[:, :n_pre] = pre_ref[:, HEAD_DIM:].T
            v_turned[:, n_pre:] = kv_ref[:, HEAD_DIM:].T
            if before:
                out_ref[:, : first * HEAD_DIM] = refs[0][...]

        scores = mm(k_all[...], q_ref[...], (1, 1)) * SCORE_SCALE
        scores = jnp.where(allowed_ref[...] != 0, scores, NEGATIVE)
        exp_scores = jnp.exp(scores - jnp.max(scores, axis=0, keepdims=True))
        soft = exp_scores / jnp.sum(exp_scores, axis=0, keepdims=True)
        at = pl.ds(pl.multiple_of((first + h) * HEAD_DIM, HEAD_DIM), HEAD_DIM)
        out_ref[:, at] = mm(v_turned[...], soft.astype(bf16), (1, 0)).T.astype(bf16)

    width = (first + heads) * HEAD_DIM
    return pl.pallas_call(
        kernel,
        out_shape=jax.ShapeDtypeStruct((tokens, width), bf16),
        grid=(heads,),
        in_specs=[
            pl.BlockSpec((tokens, HEAD_DIM), lambda h: (0, first + h)),
            pl.BlockSpec((tokens, 2 * HEAD_DIM), lambda h: (0, HEADS // 2)),
            pl.BlockSpec((n_pre, 2 * HEAD_DIM), lambda h: (0, 0)),
            pl.BlockSpec((keys, tokens), lambda h: (0, 0)),
        ]
        + [pl.BlockSpec(v.shape, lambda h: (0, 0)) for v in before],
        out_specs=pl.BlockSpec((tokens, width), lambda h: (0, 0)),
        scratch_shapes=[pltpu.VMEM((keys, HEAD_DIM), bf16), pltpu.VMEM((HEAD_DIM, keys), bf16)],
        compiler_params=pltpu.CompilerParams(vmem_limit_bytes=20 * MIB),
        cost_estimate=cost("attention"),
        name="attention",
    )(action_qkv, action_qkv, prefix_kv, allowed, *before)


def attention_back(action_qkv, prefix_kv, allowed, back_mixed, first, heads, before):
    tokens, keys = action_qkv.shape[0], allowed.shape[0]
    n_pre = prefix_kv.shape[0]
    last = first + heads == HEADS
    n_before = len(before)

    def kernel(q_ref, kv_ref, pre_ref, allowed_ref, back_ref, *refs):
        before_refs, refs = refs[:n_before], refs[n_before:]
        if last:
            qkv_out, pre_out, k_sum, v_sum, k_all, v_all, k_turned = refs
        else:
            qkv_out, k_sum, v_sum, k_all, v_all, k_turned = refs
        h = pl.program_id(0)

        @pl.when(h == 0)
        def _():
            k_all[:n_pre] = pre_ref[:, :HEAD_DIM]
            k_all[n_pre:] = kv_ref[:, :HEAD_DIM]
            v_all[:n_pre] = pre_ref[:, HEAD_DIM:]
            v_all[n_pre:] = kv_ref[:, HEAD_DIM:]
            k_turned[...] = k_all[...].T
            if n_before:
                qkv_out[:, : first * HEAD_DIM] = before_refs[0][...]
                k_sum[...] = before_refs[1][...]
                v_sum[...] = before_refs[2][...]
            else:
                k_sum[...] = jnp.zeros_like(k_sum)
                v_sum[...] = jnp.zeros_like(v_sum)

        query, back = q_ref[...], back_ref[...]
        scores = mm(k_all[...], query, (1, 1)) * SCORE_SCALE
        scores = jnp.where(allowed_ref[...] != 0, scores, NEGATIVE)
        exp_scores = jnp.exp(scores - jnp.max(scores, axis=0, keepdims=True))
        soft = exp_scores / jnp.sum(exp_scores, axis=0, keepdims=True)
        v_sum[...] += mm(soft.astype(bf16), back, (1, 0))
        back_soft = mm(v_all[...], back, (1, 1))
        mean = jnp.sum(soft * back_soft, axis=0, keepdims=True)
        back_scores = (soft * (back_soft - mean)).astype(bf16)
        k_sum[...] += mm(back_scores, query, (1, 0))
        turned = mm(k_turned[...], back_scores, (1, 0)) * SCORE_SCALE
        at = pl.ds(pl.multiple_of((first + h) * HEAD_DIM, HEAD_DIM), HEAD_DIM)
        qkv_out[:, at] = turned.T.astype(bf16)

        if last:

            @pl.when(h == heads - 1)
            def _():
                pre_out[:, :HEAD_DIM] = (k_sum[:n_pre] * SCORE_SCALE).astype(bf16)
                pre_out[:, HEAD_DIM:] = v_sum[:n_pre].astype(bf16)
                keys_out = (k_sum[n_pre:] * SCORE_SCALE).astype(bf16)
                qkv_out[:, QUERY_WIDTH : QUERY_WIDTH + HEAD_DIM] = keys_out
                qkv_out[:, QUERY_WIDTH + HEAD_DIM :] = v_sum[n_pre:].astype(bf16)

    def once(shape):
        return pl.BlockSpec(shape, lambda h: (0, 0))

    sums = jax.ShapeDtypeStruct((keys, HEAD_DIM), f32)
    if last:
        out_shapes = [
            jax.ShapeDtypeStruct((tokens, QKV_WIDTH), bf16),
            jax.ShapeDtypeStruct((n_pre, 2 * HEAD_DIM), bf16),
        ]
        kept = [pltpu.VMEM(sums.shape, f32)] * 2
    else:
        out_shapes = [jax.ShapeDtypeStruct((tokens, heads * HEAD_DIM), bf16), sums, sums]
        kept = []
    return pl.pallas_call(
        kernel,
        out_shape=out_shapes,
        grid=(heads,),
        in_specs=[
            pl.BlockSpec((tokens, HEAD_DIM), lambda h: (0, first + h)),
            pl.BlockSpec((tokens, 2 * HEAD_DIM), lambda h: (0, HEADS // 2)),
            once((n_pre, 2 * HEAD_DIM)),
            once((keys, tokens)),
            pl.BlockSpec((tokens, HEAD_DIM), lambda h: (0, first + h)),
        ]
        + [once(v.shape) for v in before],
        out_specs=[once(o.shape) for o in out_shapes],
        scratch_shapes=kept
        + [
            pltpu.VMEM((keys, HEAD_DIM), bf16),
            pltpu.VMEM((keys, HEAD_DIM), bf16),
            pltpu.VMEM((HEAD_DIM, keys), bf16),
        ],
        compiler_params=pltpu.CompilerParams(vmem_limit_bytes=22 * MIB),
        cost_estimate=cost("attention_back"),
        name="attention_back",
    )(action_qkv, action_qkv, prefix_kv, allowed, back_mixed, *before)


def mid_back(residual, back_final, back_own, back_oth, gain_row, out_weight):
    tokens, dim = residual.shape

    def kernel(res_ref, fin_ref, own_ref, oth_ref, gain_ref, weight_ref, attn_out, mixed_out, gain_out):
        v = res_ref[...]
        s = lax.rsqrt(jnp.mean(v * v, axis=-1, keepdims=True) + NORM_EPSILON)
        normed = v * s
        back = own_ref[...] + oth_ref[...]
        gain_out[...] = jnp.sum(back * normed, axis=0, keepdims=True)
        scaled = back * (1.0 + gain_ref[...])
        mean = jnp.mean(scaled * normed, axis=-1, keepdims=True)
        attn = (fin_ref[...] + s * (scaled - normed * mean)).astype(bf16)
        attn_out[...] = attn
        mixed_out[...] = mm(attn, weight_ref[...], (1, 0), bf16)

    return pl.pallas_call(
        kernel,
        out_shape=[
            jax.ShapeDtypeStruct((tokens, dim), bf16),
            jax.ShapeDtypeStruct((tokens, QUERY_WIDTH), bf16),
            jax.ShapeDtypeStruct((1, dim), f32),
        ],
        compiler_params=pltpu.CompilerParams(vmem_limit_bytes=22 * MIB),
        cost_estimate=cost("mid_back"),
        name="mid_back",
    )(residual, back_final, back_own, back_oth, gain_row, out_weight)


def readout_loss(residual, branch_own, branch_oth, gain_row, readout, target, valid):
    tokens, dim = residual.shape
    act = readout.shape[0]

    def full(a, b, contract):
        return lax.dot_general(
            a, b, (((contract[0],), (contract[1],)), ((), ())),
            precision=HIGHEST, preferred_element_type=f32,
        )

    def kernel(res_ref, own_ref, oth_ref, gain_ref, read_ref, target_ref, valid_ref, final_out, branch_out, rows_out):
        v = res_ref[...] + own_ref[...] + oth_ref[...]
        s = lax.rsqrt(jnp.mean(v * v, axis=-1, keepdims=True) + NORM_EPSILON)
        normed = v * s
        scale = 1.0 + gain_ref[...]
        final = normed * scale
        valid_rows = valid_ref[...].astype(f32)
        error = full(read_ref[...], final, (1, 1)) - target_ref[...]
        counted = valid_rows * error
        back = 2.0 * counted
        rows_out[:act] = full(back, final, (1, 0))
        back_norm = full(back.T, read_ref[...], (1, 0))
        rows_out[act : act + 1] = jnp.sum(back_norm * normed, axis=0, keepdims=True)
        loss = jnp.sum(jnp.sum(counted * error, axis=0, keepdims=True), axis=1, keepdims=True)
        count = jnp.sum(jnp.sum(valid_rows, axis=0, keepdims=True), axis=1, keepdims=True)
        rows_out[act + 1 : act + 2] = jnp.broadcast_to(loss, (1, dim))
        rows_out[act + 2 : act + 3] = jnp.broadcast_to(count, (1, dim))
        scaled = back_norm * scale
        mean = jnp.mean(scaled * normed, axis=-1, keepdims=True)
        final_back = s * (scaled - normed * mean)
        final_out[...] = final_back
        branch_out[...] = final_back.astype(bf16)

    return pl.pallas_call(
        kernel,
        out_shape=[
            jax.ShapeDtypeStruct((tokens, dim), f32),
            jax.ShapeDtypeStruct((tokens, dim), bf16),
            jax.ShapeDtypeStruct((act + 3, dim), f32),
        ],
        compiler_params=pltpu.CompilerParams(vmem_limit_bytes=20 * MIB),
        cost_estimate=cost("readout_loss"),
        name="readout_loss",
    )(residual, branch_own, branch_oth, gain_row, readout, target, valid)


def on_device(
    ring,
    prefix_in,
    action_in,
    target,
    valid_mask,
    prefix_ids,
    action_ids,
    action_blocks,
    learning_rate,
    prefix_weight,
    attention_weight,
    feedforward_weight,
    prefix_gains,
    action_gains,
    readout_weight,
    prefix_weight_moment,
    attention_weight_moment,
    feedforward_weight_moment,
    prefix_gains_moment,
    action_gains_moment,
    readout_weight_moment,
    prefix_weight_average,
    attention_weight_average,
    feedforward_weight_average,
    prefix_gains_average,
    action_gains_average,
    readout_weight_average,
):
    core = lax.axis_index("wide") % 2
    rows_a, width_a = attention_weight.shape
    width_p = 2 * prefix_weight.shape[1]
    rows_p = prefix_weight.shape[0]
    n_right, n_left = ring.n_right, ring.n_left
    order, swap = Order(), ring.to_core

    def by_core(v, size):
        cut = v.reshape(v.shape[0], ring.chips, 2, size)
        cut = [cut[:, :, c].reshape(v.shape[0], ring.chips * size) for c in (0, 1)]
        return jnp.where(core == 0, cut[0], cut[1]), jnp.where(core == 0, cut[1], cut[0])

    def in_order(v, size):
        cut = v.reshape(2, ring.chips, size)
        return jnp.where(core == 0, cut, cut[::-1]).transpose(1, 0, 2).reshape(-1)

    def halves_of(v, axis):
        half = v.shape[axis] // 2
        if half % 16:
            return jnp.split(v, 2, axis)
        me = lax.axis_index("batch")
        return [lax.dynamic_slice_in_dim(v, at * half, half, axis) for at in (me, 1 - me)]

    prefix_bf = prefix_weight.astype(bf16)
    packed = jnp.concatenate(
        [attention_weight.astype(bf16), prefix_bf[:rows_a], prefix_bf[rows_a:]], axis=1
    )
    sides = [("right", d) for d in range(n_right)] + [("left", d) for d in range(n_left)]
    packed_halves = order(*halves_of(packed, 0))
    att = Gathering(ring, order, packed_halves, 0, True)
    att.start("right")
    att.start("left")
    ff_halves = order(*halves_of(jnp.transpose(feedforward_weight, (1, 0, 2)).astype(bf16), 1))
    ff = Gathering(ring, order, ff_halves, 1, False)
    side_of = {"R": "right", "L": "left"}

    def serve(step):
        for word in PLAN[step]:
            chain, what = {"a": att, "f": ff}[word[0]], word[1]
            if what == ">":
                chain.start(side_of[word[2]])
            elif what in side_of:
                chain.land(side_of[what])
            else:
                key = (side_of[word[2]], int(word[3]))
                (chain.cross if what == "X" else chain.settle)(key)

    ff.whole = order(ff.whole)
    own_parts = packed_halves if att.can else (packed,)
    prefix_rows = order(prefix_in[0])
    if rows_p % 128 == 0:
        pre_rel = order(norm_by_core(ring, prefix_rows, prefix_gains, rows_p))
    else:
        normed = rms_norm(prefix_rows.astype(f32), prefix_gains[0]).astype(bf16)
        pre_rel = order(jnp.concatenate(by_core(normed, rows_p), 1))
    serve("norm")
    action_rows = order(action_in[0]).astype(f32)
    action_norm = rms_norm(action_rows, action_gains[0]).astype(bf16)
    norm_mine, norm_other = order(*by_core(action_norm, rows_a))
    serve("action")
    norm_oth = order(swap(order(norm_other)))
    norm_rel = order(jnp.concatenate([norm_mine, norm_other], 1))
    serve("swapped")
    allowed = order(visible(prefix_ids[0], *order(action_ids[0], action_blocks[0])))
    serve("seen")
    while any(att.d[x] < att.count[x] for x in att.d):
        att.land("right", "left")
    att.settle(*[k for k in sides if len(att.blocks[k]) == 1])
    blocks = [own_parts] + [att.blocks[k] for k in sides]
    qkv_own, out_own, pre_own = order(*assemble(ring, blocks, rows_a, width_a))
    pre_oth, qkv_oth = swap(pre_own), swap(qkv_own)
    serve("assembled")

    prefix_kv = order(half_product(pre_rel, 0, order(pre_own), None))
    action_qkv = order(half_product(norm_rel, 0, order(qkv_own), None))
    serve("half")
    pre_oth, qkv_oth, out_own = order(pre_oth, qkv_oth, out_own)
    out_oth = swap(out_own)
    prefix_kv = order(half_product(pre_rel, 1, order(pre_oth), prefix_kv))
    action_qkv = order(half_product(norm_rel, 1, order(qkv_oth), action_qkv))
    serve("half2")
    out_own, out_oth = order(out_own, out_oth)
    out_weight = order(interleave(ring, out_own, out_oth, rows_a))
    serve("woven")
    action_qkv = order(action_qkv)
    part = order(attention(action_qkv, prefix_kv, allowed, 0, HEADS // 2, ()))
    serve("attended")
    part = order(part)
    mixed_heads = order(
        attention(action_qkv, prefix_kv, allowed, HEADS // 2, HEADS // 2, (part,))
    )
    mixed_oth = swap(mixed_heads)
    serve("attended2")
    mixed_heads = order(mixed_heads)
    residual = action_rows + mm(mixed_heads, out_weight, (1, 1))
    tokens = residual.shape[0]
    hidden_norm = rms_norm(residual, action_gains[1]).astype(bf16)
    residual, hidden_norm, mixed_oth = order(residual, hidden_norm, mixed_oth)
    norm_two = order(jnp.concatenate([hidden_norm, order(swap(hidden_norm))], 0))
    serve("normed")

    def weights(key):
        return (ff.whole,) if key[0] == "own" else ff.blocks[key]

    early = [("own", 0)] + [x for d in range(n_left - 1) for x in (("left", d), ("right", d))]
    late = [("right", n_left - 1), ("left", n_left - 1)]
    late += [("right", d) for d in range(n_left, n_right)]
    groups = [early, late]
    kept, branch = [], None
    for group in groups:
        for side, d in group:
            while side != "own" and ff.d[side] <= d:
                ff.land(side)
        ff.cross(*[k for k in group if k[0] != "own"])
        ff.settle(*[k for k in group if len(ff.blocks.get(k, ())) == 2])
        norm_two = order(norm_two)
        *values, own_rows, other_rows = ff_forward(norm_two, [weights(k) for k in group], branch)
        branch = order(own_rows, other_rows)
        kept.append(values)
        if group is early:
            serve("early")
    dim = action_rows.shape[1]
    branch_own, branch_oth = order(branch[0], swap(branch[1]))
    back_final, back_branch, small_rows = order(
        *readout_loss(
            residual,
            branch_own,
            branch_oth,
            action_gains[2:3],
            readout_weight.T,
            target[0].T,
            valid_mask[0].T,
        )
    )
    branch_two = order(jnp.concatenate([back_branch, swap(back_branch)], 0))
    act = readout_weight.shape[1]
    n_back = n_right + (n_left > 1)
    ff_sum = Summing(ring, order, 1, n_back)

    def way_back(key):
        side, d = key
        return ("right", ring.chips - 2 - d) if side == "left" and ring.chips - 2 - d < n_back else key

    own_key, back = ("own", 0), None
    att_sum = Summing(ring, order, 0, n_right)
    small_sum, swapped = None, {}

    def serve_back(step):
        nonlocal small_sum
        for word in PLAN[step]:
            chain, rest = (att_sum, word[1:]) if word[0] == "A" else (ff_sum, word)
            if word in ("q", "o"):
                if word in swapped:
                    swapped[word] = order(swapped[word])
            elif word == "Aown":
                while att_sum.d["left"] >= 0:
                    att_sum.step("left")
                att_sum.own(jnp.split(cut[0], 2, 0))
            elif rest in side_of:
                side = side_of[rest]
                if (side, chain.d[side]) in chain.parts:
                    chain.step(side)
            elif rest == "own":
                while ff_sum.d["left"] >= 0:
                    ff_sum.step("left")
                own_grads = [ff_sum.parts[own_key]]
                if ff.can:
                    own_grads.append(ff_sum.sends["own"].reshape(own_grads[0].shape))
                else:
                    own_grads = jnp.split(own_grads[0], 2, 1)
                ff_sum.own(own_grads)
            elif rest == "close":
                while ff_sum.d["right"] >= 0:
                    ff_sum.step("right")
                ff_sum.close()
            elif rest == "s":
                if small_sum is None:
                    small_sum = SmallSum(ring, order, small_rows)
                else:
                    small_sum.step()
            else:
                chain = att_sum if rest[1:] == "A" else ff_sum
                name = "all" if rest[1:] == "A" else rest[1:]
                (chain.cross if rest[0] == "x" else chain.ready)(name)

    for name, group, values in (("late", late, kept[1]), ("early", early, kept[0])):
        turned = [way_back(k) for k in group[::-1]]
        rights = sorted((k for k in turned if k[0] == "right"), key=lambda k: -k[1])
        if not ff.can:
            lists = {}
        elif name == "late":
            lists = {"first": rights[:1], "second": rights[1:2], "third": rights[2:]}
        else:
            lists = {"early": rights, "own": [own_key]}
        lists = {k: v for k, v in lists.items() if v}
        branch_two = order(branch_two)
        made, sent, back = ff_backward(
            norm_two,
            branch_two,
            [weights(k) for k in group[::-1]],
            [[turned.index(k) for k in keys] for keys in lists.values()],
            values,
            (len(group) - 1, -1),
            back,
        )
        flat = list(order(*back, *made, *sent))
        back, made, sent = flat[:2], flat[2 : 2 + len(turned)], flat[2 + len(turned) :]
        ff_sum.put(
            dict(zip(turned, made)),
            dict(zip(lists, sent)),
            {k: (n, i) for n, keys in lists.items() for i, k in enumerate(keys)},
        )
        if name == "late":
            serve_back("back_late")
    back_oth = swap(back[1])
    serve_back("back_early")
    back_own, back_oth = order(back[0], back_oth)
    back_attention, back_mixed, grad_gain_hidden = order(
        *mid_back(residual, back_final, back_own, back_oth, action_gains[1:2], out_weight)
    )
    serve_back("mid")
    back_mixed = order(back_mixed)
    part = order(
        *attention_back(action_qkv, prefix_kv, allowed, back_mixed, 0, HEADS // 2, ())
    )
    serve_back("back_a")
    attn_mine, attn_other = order(*by_core(order(back_attention), rows_a))
    attn_oth = swap(attn_other)
    serve_back("core")
    back_mixed, attn_oth, *part = order(back_mixed, attn_oth, *part)
    back_qkv, back_prefix_kv = order(
        *attention_back(action_qkv, prefix_kv, allowed, back_mixed, HEADS // 2, HEADS // 2, part)
    )
    swapped["q"] = swap(back_qkv)
    serve_back("back_b")

    swapped["o"] = swap(order(side_gradient(pre_rel, order(back_prefix_kv), 1)))
    serve_back("side")
    grad_output = order(pair_gradient((attn_mine, attn_oth), order(mixed_heads, mixed_oth)))
    serve_back("pair")
    cut = order(
        *disassemble(
            ring,
            att.can,
            (norm_mine, norm_oth),
            (back_qkv, order(swapped["q"])),
            pre_rel,
            back_prefix_kv,
            order(swapped["o"]),
            order(grad_output),
            rows_a,
        )
    )
    att_sum.put(
        dict(zip(sides, cut[1:])),
        {"all": cut[ring.chips]} if att.can else {},
        {("right", d): ("all", d) for d in range(n_right)} if att.can else {},
    )
    serve_back("cut")
    back_qkv, back_prefix_kv = order(back_qkv, back_prefix_kv)
    sums = order(
        gain_sums(back_qkv, norm_rel, qkv_own, qkv_oth),
        gain_sums(back_prefix_kv, pre_rel, pre_own, pre_oth),
    )
    grad_gain_action = in_order(sums[0][0], rows_a) / (1.0 + action_gains[0])
    grad_gain_prefix = in_order(sums[1][0], rows_p) / (1.0 + prefix_gains[0])
    late_rows = order(grad_gain_prefix.reshape(-1, dim), grad_gain_action[None], grad_gain_hidden)
    small_rows = [small_rows, *late_rows]
    serve_back("gains")
    serve_back("tail")
    while att_sum.d["right"] >= 0:
        att_sum.step("right")
    if small_sum is None:
        small_sum = SmallSum(ring, order, small_rows)
    while small_sum.step():
        pass
    ff_total = ff_sum.result()
    small = small_sum.total
    n_pre = grad_gain_prefix.shape[0] // dim
    count = small[act + 2, 0]
    loss_value = small[act + 1, 0] / count
    scale = 1.0 / count
    step_rate = learning_rate[0]
    third = order(
        *advance(
            feedforward_weight,
            feedforward_weight_moment,
            feedforward_weight_average,
            jnp.transpose(ff_total, (1, 0, 2)) * scale,
            step_rate,
        )
    )
    att_sum.close()
    packed_total = att_sum.result()
    first = advance(
        prefix_weight,
        prefix_weight_moment,
        prefix_weight_average,
        jnp.concatenate(
            [
                packed_total[:, width_a : width_a + width_p // 2],
                packed_total[:, width_a + width_p // 2 :],
            ],
            0,
        )
        * scale,
        step_rate,
    )
    second = advance(
        attention_weight,
        attention_weight_moment,
        attention_weight_average,
        packed_total[:, :width_a] * scale,
        step_rate,
    )
    fourth = advance(
        prefix_gains,
        prefix_gains_moment,
        prefix_gains_average,
        small[act + 3 : act + 3 + n_pre].reshape(1, -1) * scale,
        step_rate,
    )
    fifth = advance(
        action_gains,
        action_gains_moment,
        action_gains_average,
        jnp.concatenate([small[act + 3 + n_pre :], small[act : act + 1]], 0) * scale,
        step_rate,
    )
    sixth = advance(
        readout_weight,
        readout_weight_moment,
        readout_weight_average,
        small[:act].T * scale,
        step_rate,
    )
    loss_value = loss_value + order.token.astype(f32)
    return (loss_value,) + tuple(
        group[i]
        for i in range(3)
        for group in (first, second, third, fourth, fifth, sixth)
    )


def solution(mesh):
    rows = P(("batch", "wide"))
    wide = P("wide")
    whole = P()
    weights = (wide, wide, wide, whole, whole, whole)
    return jax.shard_map(
        functools.partial(on_device, Ring(mesh.shape["wide"])),
        mesh=mesh,
        in_specs=(rows,) * 7 + (whole,) + weights * 3,
        out_specs=(whole,) + weights * 3,
        check_vma=False,
    )
```

```python
import functools
import math

import jax
import jax.numpy as jnp
import numpy as np
from jax import lax
from jax.experimental import pallas as pl
from jax.experimental.pallas import tpu as pltpu
from jax.sharding import PartitionSpec as P

HEADS = 8
HEAD_DIM = 256
QUERY_WIDTH = HEADS * HEAD_DIM
QKV_WIDTH = QUERY_WIDTH + 2 * HEAD_DIM
SCORE_SCALE = HEAD_DIM ** (-0.5)

NORM_EPSILON = 1e-06
MOMENTUM = 0.9
AVERAGE_DECAY = 0.8
NEGATIVE = -1e30

bf16 = jnp.bfloat16
f32 = jnp.float32
HIGHEST = lax.Precision.HIGHEST
MIB = 2**20
CUT = 512
PLAN = dict(
    norm=("aR", "aL", "aXR0", "aXL0", "aR"),
    action=("aL", "aSL0", "aXL1", "aR", "aXR1", "aSR0", "aL", "f>L", "aSL1", "aR", "aXR2", "f>R", "aXR3"),
    swapped=("aSR1", "aXL2", "aSR2", "aSL2"),
    seen=("fR", "fXR0", "fL", "aSR3"),
    assembled=(),
    half=(),
    half2=("fSR0", "fR", "fXR1"),
    woven=(),
    attended=(),
    attended2=("fR", "fSR1", "fXR2", "fL"),
    normed=(),
    early=("fR", "fSR2", "fXR3"),
    back_late=("xfirst", "xsecond"),
    back_early=("R", "L"),
    mid=(),
    back_a=(),
    core=("R", "xearly", "xthird"),
    back_b=("rthird", "L"),
    side=("q", "R", "o"),
    pair=(),
    cut=("xA", "AL"),
    gains=("R",),
    tail=(
        "s", "own", "R", "rA", "AR", "s", "AL", "s", "AR",
        "AL", "close", "s", "AR", "s", "AR", "AL", "AR", "Aown",
    ),
)
COST = dict(
    add=11, assemble=11, half_product=11, gain_sums=11, pair_gradient=11, side_gradient=11,
    disassemble=11, norm_by_core=11, ff_forward=9, ff_backward=0, attention=11, attention_back=8,
    mid_back=8, interleave=11, readout_loss=11,
)


def cost(name):
    return pl.CostEstimate(flops=10 ** COST[name], transcendentals=0, bytes_accessed=1)


def rms_norm(stream, gain_row):
    return (
        stream
        * lax.rsqrt(jnp.mean(stream * stream, axis=-1, keepdims=True) + NORM_EPSILON)
        * (1.0 + gain_row)
    )


def norm_back(stream, gain_row, cotangent):
    _, pull = jax.vjp(rms_norm, stream, gain_row)
    return pull(cotangent)


def gated_unit(gate_value, linear_value):
    return jax.nn.gelu(gate_value, approximate=True) * linear_value


def visible(prefix_ids, action_ids, block_flags):
    length = block_flags.shape[0]
    place = jnp.arange(length)
    upto = place[None, :] <= place[:, None]
    levels = jnp.sum(jnp.where(upto, block_flags[None, :], 0), axis=1)
    from_prefix = prefix_ids[:, None] == action_ids[None, :]
    from_action = (action_ids[:, None] == action_ids[None, :]) & (
        levels[:, None] <= levels[None, :]
    )
    return jnp.concatenate([from_prefix, from_action], axis=0).astype(jnp.int32)


def advance(weight, moment, average, gradient, step_rate):
    moment_next = MOMENTUM * moment + gradient
    weight_next = weight - step_rate * (gradient + MOMENTUM * moment_next)
    average_next = AVERAGE_DECAY * average + (1.0 - AVERAGE_DECAY) * weight_next
    return (weight_next, moment_next, average_next)


def mm(a, b, contract, out=f32):
    return lax.dot_general(
        a, b, (((contract[0],), (contract[1],)), ((), ())), preferred_element_type=f32
    ).astype(out)


class Order:
    def __init__(self):
        self.token = jnp.zeros((), jnp.int32)

    def __call__(self, *values):
        *values, self.token = lax.optimization_barrier((*values, self.token))
        return values[0] if len(values) == 1 else values


class Ring:
    def __init__(self, wide):
        chips = wide // 2
        self.wide, self.chips = wide, chips
        self.cycle = list(range(0, chips, 2)) + list(range(1, chips, 2))[::-1]
        ahead = [(self.cycle[i], self.cycle[(i + 1) % chips]) for i in range(chips)]
        self.right = [(2 * s + c, 2 * t + c) for s, t in ahead for c in (0, 1)]
        self.left = [(t, s) for s, t in self.right]
        self.core = [(w, w ^ 1) for w in range(wide)]
        self.n_right = chips // 2
        self.n_left = chips - 1 - self.n_right

    def to_right(self, v):
        return lax.ppermute(v, "wide", self.right)

    def to_left(self, v):
        return lax.ppermute(v, "wide", self.left)

    def to_core(self, v):
        return lax.ppermute(v, "wide", self.core)

    def to_peer(self, v):
        return lax.ppermute(v, "batch", [(0, 1), (1, 0)])

    def owners(self, w):
        here = self.cycle.index(w // 2)
        rights = [self.cycle[(here - d) % self.chips] for d in range(1, self.n_right + 1)]
        lefts = [self.cycle[(here + d) % self.chips] for d in range(1, self.n_left + 1)]
        return [w // 2] + rights + lefts

    def bits(self):
        k, steps = 1, [self.to_peer]
        while k < self.wide:
            pairs = [(w, w ^ k) for w in range(self.wide)]
            steps.append(functools.partial(lax.ppermute, axis_name="wide", perm=pairs))
            k *= 2
        return steps


def add(*terms, step=None):
    terms = [t if isinstance(t, tuple) else (t, 0, 1) for t in terms]
    shape = terms[0][0].shape
    cols = shape[-1]
    rows = math.prod(shape[:-1])
    if step is None:
        step = 128 if rows % 128 == 0 and rows > 128 else rows

    def kernel(*refs):
        refs[-1][...] = sum(r[...].astype(f32) for r in refs[:-1]).astype(bf16)

    def block(k, stride):
        return pl.BlockSpec((step, cols), lambda i: (stride * i + k, 0))

    return pl.pallas_call(
        kernel,
        out_shape=jax.ShapeDtypeStruct((rows, cols), bf16),
        grid=(rows // step,),
        in_specs=[block(k, stride) for _, k, stride in terms],
        out_specs=block(0, 1),
        compiler_params=pltpu.CompilerParams(vmem_limit_bytes=8 * MIB),
        cost_estimate=cost("add"),
        name="add",
    )(*[t.reshape(-1, cols) for t, _, _ in terms]).reshape(shape)


class SmallSum:
    def __init__(self, ring, order, rows):
        self.order, self.steps = order, ring.bits()
        self.total = order(jnp.concatenate(rows, 0))
        self.moved = self.steps.pop(0)(self.total)

    def step(self):
        if self.moved is None:
            return False
        total, moved = self.order(self.total, self.moved)
        self.total = self.order(total + moved)
        self.moved = self.steps.pop(0)(self.total) if self.steps else None
        return True


class Gathering:
    def __init__(self, ring, order, halves, axis, split_left):
        self.ring, self.order = ring, order
        self.halves, self.split_left = halves, split_left
        self.whole = jnp.concatenate(halves, axis)
        self.can = halves[0].shape[axis] % 16 == 0
        self.blocks, self.flying = {}, {}
        self.count = {"right": ring.n_right, "left": ring.n_left}
        self.d = {"right": 0, "left": 0}

    def cut(self, side):
        return self.can and (side == "right" or self.split_left)

    def start(self, side):
        self.send(side, self.order(self.halves[0] if self.cut(side) else self.whole))

    def send(self, side, v):
        self.flying[side] = self.ring.to_right(v) if side == "right" else self.ring.to_left(v)

    def land(self, *sides):
        sides = [x for x in sides if self.d[x] < self.count[x] and x in self.flying]
        if not sides:
            return
        came = self.order(*[self.flying[x] for x in sides])
        for side, v in zip(sides, came if len(sides) > 1 else [came]):
            self.blocks[side, self.d[side]] = (v,)
            self.d[side] += 1
            if self.d[side] < self.count[side]:
                self.send(side, v)

    def cross(self, *keys):
        for key in keys:
            if self.cut(key[0]) and len(self.blocks.get(key, (0, 0))) == 1:
                (v,) = self.blocks[key]
                v = self.order(v)
                self.blocks[key] = (v, self.ring.to_peer(v))

    def settle(self, *keys):
        for key in keys:
            if key in self.blocks:
                self.cross(key)
                self.blocks[key] = tuple(self.order(p) for p in self.blocks[key])


class Summing:
    def __init__(self, ring, order, axis, n_right):
        self.ring, self.order, self.axis = ring, order, axis
        self.parts, self.sends, self.spots, self.crossed = {}, {}, {}, {}
        self.came = {"right": None, "left": None}
        self.d = {"right": n_right - 1, "left": ring.chips - 2 - n_right}

    def put(self, parts, sends, spots):
        self.parts.update(parts)
        self.sends.update(sends)
        self.spots.update(spots)

    def cross(self, *names):
        for name in names:
            if name in self.sends and name not in self.crossed:
                self.crossed[name] = self.ring.to_peer(self.order(self.sends[name]))

    def ready(self, *names):
        for name in names:
            if name in self.crossed:
                self.crossed[name] = self.order(self.crossed[name])

    def step(self, *sides):
        for side in sides:
            d = self.d[side]
            if d < 0:
                continue
            terms = [self.parts[side, d]]
            terms += [self.came[side]] if self.came[side] is not None else []
            if (side, d) in self.spots:
                name, spot = self.spots[side, d]
                self.cross(name)
                *terms, self.crossed[name] = self.order(*terms, self.crossed[name])
                rows = math.prod(self.parts[side, d].shape[:-1])
                step = 128 if rows % 128 == 0 and rows > 128 else rows
                terms.append((self.crossed[name], spot * (rows // step), 1))
            else:
                terms = self.order(*terms)
                terms = list(terms) if isinstance(terms, (list, tuple)) else [terms]
            total = self.order(add(*terms)) if len(terms) > 1 else terms[0]
            self.came[side] = self.ring.to_left(total) if side == "right" else self.ring.to_right(total)
            self.d[side] = d - 1

    def land(self, side):
        self.came[side] = self.order(self.came[side])

    def left(self):
        return max(self.d.values()) + 1

    def own(self, halves):
        left = self.order(self.came["left"])
        half = halves[0].shape[self.axis]
        self.split = bool(self.spots)
        if self.split:
            stride = 2 if self.axis else 1
            self.rows = half
            self.mine = [halves[0], (left, 0, stride)]
            other = self.order(add(halves[1], (left, 1, stride), step=half))
            self.across = self.ring.to_peer(other)
        else:
            self.mine = [self.order(add(jnp.concatenate(halves, self.axis), left))]
            self.rows = None

    def close(self):
        self.came["right"] = self.order(self.came["right"])
        terms = self.mine + [self.came["right"]]
        if self.split:
            self.across = self.order(self.across)
            terms.append(self.across)
        self.total = self.order(add(*terms, step=self.rows))
        self.across = self.ring.to_peer(self.total)

    def result(self):
        me = lax.axis_index("batch")
        total, across = [v.astype(f32) for v in self.order(self.total, self.across)]
        if not self.split:
            return total + across
        return jnp.where(
            me == 0,
            jnp.concatenate([total, across], self.axis),
            jnp.concatenate([across, total], self.axis),
        )


def places(ring, counts, rows):
    table = np.zeros((2, ring.wide, 2, sum(counts)), np.int32)
    for me in (0, 1):
        for w in range(ring.wide):
            where, first = [], []
            for owner, n in zip(ring.owners(w), counts):
                where += [owner] * n
                first += [me * rows // 2, (1 - me) * rows // 2] if n == 2 else [0]
            table[me, w] = where, first
    return jnp.array(table)[lax.axis_index("batch"), lax.axis_index("wide")]


def assemble(ring, blocks, rows, width_a):
    counts = [len(b) for b in blocks]
    parts = [p for b in blocks for p in b]
    n = len(parts)
    table = places(ring, counts, rows)
    side_rows = rows * ring.chips
    pw = (parts[0].shape[1] - width_a) // 2
    shapes = ((side_rows, QKV_WIDTH), (side_rows, width_a - QKV_WIDTH), (2 * side_rows, pw))

    def kernel(table_ref, *refs):
        ins, (qkv, out, pre, sems) = refs[:n], refs[n:]
        copies = []

        def copy(i, start, width, to, row):
            size = parts[i].shape[0]
            target = to.at[pl.ds(pl.multiple_of(row, size), size), :]
            copies.append(
                pltpu.make_async_copy(ins[i].at[:, pl.ds(start, width)], target, sems.at[len(copies)])
            )

        for i in range(n):
            chip, first = table_ref[0, i], table_ref[1, i]
            copy(i, 0, QKV_WIDTH, qkv, chip * rows + first)
            copy(i, QKV_WIDTH, width_a - QKV_WIDTH, out, chip * rows + first)
            for j in (0, 1):
                copy(i, width_a + j * pw, pw, pre, (2 * chip + j) * rows + first)
        for c in copies:
            c.start()
        for c in copies:
            c.wait()

    return pl.pallas_call(
        kernel,
        out_shape=[jax.ShapeDtypeStruct(sh, bf16) for sh in shapes],
        grid_spec=pltpu.PrefetchScalarGridSpec(
            num_scalar_prefetch=1,
            grid=(1,),
            in_specs=[pl.BlockSpec(memory_space=pl.ANY)] * n,
            out_specs=[pl.BlockSpec(sh, lambda i, t: (0, 0)) for sh in shapes],
            scratch_shapes=[pltpu.SemaphoreType.DMA((4 * n,))],
        ),
        compiler_params=pltpu.CompilerParams(vmem_limit_bytes=14 * MIB),
        cost_estimate=cost("assemble"),
        name="assemble",
    )(table, *parts)


def interleave(ring, own, other, rows):
    core = (lax.axis_index("wide") % 2).reshape(1)

    def kernel(core_ref, own_ref, other_ref, out_ref, sems):
        copies = []
        for chip in range(ring.chips):
            for j, ref in enumerate((own_ref, other_ref)):
                side = core_ref[0] if j == 0 else 1 - core_ref[0]
                to = pl.ds(pl.multiple_of((2 * chip + side) * rows, rows), rows)
                copies.append(
                    pltpu.make_async_copy(
                        ref.at[pl.ds(chip * rows, rows), :], out_ref.at[to, :], sems.at[chip, j]
                    )
                )
        for c in copies:
            c.start()
        for c in copies:
            c.wait()

    shape = (2 * own.shape[0], own.shape[1])
    return pl.pallas_call(
        kernel,
        out_shape=jax.ShapeDtypeStruct(shape, bf16),
        grid_spec=pltpu.PrefetchScalarGridSpec(
            num_scalar_prefetch=1,
            grid=(1,),
            in_specs=[pl.BlockSpec(memory_space=pl.ANY)] * 2,
            out_specs=pl.BlockSpec(shape, lambda i, t: (0, 0)),
            scratch_shapes=[pltpu.SemaphoreType.DMA((ring.chips, 2))],
        ),
        compiler_params=pltpu.CompilerParams(vmem_limit_bytes=12 * MIB),
        cost_estimate=cost("interleave"),
        name="interleave",
    )(core, own, other)


def side_gradient(rows, cols, which=0):
    tokens, width = rows.shape[0], rows.shape[1] // 2

    def kernel(rows_ref, cols_ref, out_ref):
        out_ref[...] = mm(rows_ref[...], cols_ref[...], (0, 0), bf16)

    return pl.pallas_call(
        kernel,
        out_shape=jax.ShapeDtypeStruct((width, cols.shape[1]), bf16),
        grid=(1,),
        in_specs=[
            pl.BlockSpec((tokens, width), lambda i: (0, which)),
            pl.BlockSpec(cols.shape, lambda i: (0, 0)),
        ],
        out_specs=pl.BlockSpec((width, cols.shape[1]), lambda i: (0, 0)),
        compiler_params=pltpu.CompilerParams(vmem_limit_bytes=14 * MIB),
        cost_estimate=cost("side_gradient"),
        name="side_gradient",
    )(rows, cols)


def half_product(rows, side, weight, before):
    tokens, width = rows.shape[0], rows.shape[1] // 2
    cols = weight.shape[1]
    kind = f32 if before is None else bf16

    def kernel(rows_ref, weight_ref, *refs):
        out_ref = refs[-1]
        for c in range(cols // CUT):
            at = slice(c * CUT, (c + 1) * CUT)
            total = mm(rows_ref[...], weight_ref[:, at], (1, 0))
            out_ref[:, at] = (total if before is None else total + refs[0][:, at]).astype(kind)

    extra = [] if before is None else [before]
    return pl.pallas_call(
        kernel,
        out_shape=jax.ShapeDtypeStruct((tokens, cols), kind),
        grid=(1,),
        in_specs=[
            pl.BlockSpec((tokens, width), lambda i: (0, side)),
            pl.BlockSpec(weight.shape, lambda i: (0, 0)),
        ]
        + [pl.BlockSpec((tokens, cols), lambda i: (0, 0)) for _ in extra],
        out_specs=pl.BlockSpec((tokens, cols), lambda i: (0, 0)),
        compiler_params=pltpu.CompilerParams(vmem_limit_bytes=22 * MIB),
        cost_estimate=cost("half_product"),
        name="half_product",
    )(rows, weight, *extra)


def gain_sums(back, rows, own, other):
    tokens, width = rows.shape[0], rows.shape[1] // 2
    cols = own.shape[1]
    step = 256

    def kernel(back_ref, rows_ref, own_ref, other_ref, out_ref):
        @pl.when(pl.program_id(0) == 0)
        def _():
            out_ref[...] = jnp.zeros_like(out_ref)

        for side, ref in enumerate((own_ref, other_ref)):
            at = slice(side * width, (side + 1) * width)
            total = mm(back_ref[...], ref[...], (1, 1)) * rows_ref[:, at].astype(f32)
            out_ref[:, at] += jnp.sum(total, axis=0, keepdims=True)

    return pl.pallas_call(
        kernel,
        out_shape=jax.ShapeDtypeStruct((1, 2 * width), f32),
        grid=(tokens // step,),
        in_specs=[
            pl.BlockSpec((step, cols), lambda i: (i, 0)),
            pl.BlockSpec((step, 2 * width), lambda i: (i, 0)),
        ]
        + [pl.BlockSpec(w.shape, lambda i: (0, 0)) for w in (own, other)],
        out_specs=pl.BlockSpec((1, 2 * width), lambda i: (0, 0)),
        compiler_params=pltpu.CompilerParams(vmem_limit_bytes=20 * MIB),
        cost_estimate=cost("gain_sums"),
        name="gain_sums",
    )(back, rows, own, other)


def pair_gradient(rows, cols):
    width, step = rows[0].shape[1], 512

    def kernel(r0, r1, c0, c1, out_ref):
        out_ref[...] = (mm(r0[...], c0[...], (0, 0)) + mm(r1[...], c1[...], (0, 0))).astype(bf16)

    once = [pl.BlockSpec(r.shape, lambda i: (0, 0)) for r in rows]
    return pl.pallas_call(
        kernel,
        out_shape=jax.ShapeDtypeStruct((width, cols[0].shape[1]), bf16),
        grid=(cols[0].shape[1] // step,),
        in_specs=once + [pl.BlockSpec((c.shape[0], step), lambda i: (0, i)) for c in cols],
        out_specs=pl.BlockSpec((width, step), lambda i: (0, i)),
        compiler_params=pltpu.CompilerParams(vmem_limit_bytes=14 * MIB),
        cost_estimate=cost("pair_gradient"),
        name="pair_gradient",
    )(*rows, *cols)


def disassemble(ring, halved, norm_rows, qkv_back, pre_rel, back_prefix_kv, other_side, grad_output, rows):
    cuts = 2 if halved else 1
    size = rows // cuts
    table = places(ring, [cuts] * ring.chips, rows)
    spots, sizes = [], []
    for j in range(ring.chips):
        right = 1 <= j <= ring.n_right
        sizes.append(size if right else rows)
        if right and halved:
            spots += [(j, 0), (ring.chips, (j - 1) * size)]
        else:
            spots += [(j, k * size) for k in range(cuts)]
    if halved:
        sizes.append(ring.n_right * size)
    n = len(sizes)
    side_rows = rows * ring.chips
    pre_cols = back_prefix_kv.shape[1]
    out_cols = grad_output.shape[1]
    width = QKV_WIDTH + out_cols + 2 * pre_cols
    step = 512

    def kernel(table_ref, n0, n1, q0, q1, pre_ref, back_ref, side_ref, out_ref, *refs):
        parts, (qkv_sum, pre_sum, sems) = refs[:n], refs[n:]

        def copies(i, k):
            chip, first = table_ref[0, i], table_ref[1, i]
            part, top = spots[i]

            def piece(ref, row, at, w, j):
                source = ref.at[pl.ds(pl.multiple_of(row, size), size), :]
                target = parts[part].at[pl.ds(top, size), pl.ds(at, w)]
                return pltpu.make_async_copy(source, target, sems.at[i, j])

            if k == 0:
                return [piece(out_ref, chip * rows + first, QKV_WIDTH, out_cols, 0)]
            if k == 1:
                at = QKV_WIDTH + out_cols
                return [
                    piece(pre_sum, (2 * chip + j) * rows + first, at + j * pre_cols, pre_cols, 1 + j)
                    for j in (0, 1)
                ]
            return [piece(qkv_sum, chip * rows + first, 0, QKV_WIDTH, 3)]

        def start(k):
            for i in range(len(spots)):
                for c in copies(i, k):
                    c.start()

        start(0)
        total = mm(pre_ref[...], back_ref[...], (0, 0)) + side_ref[...].astype(f32)
        pre_sum[...] = total.astype(bf16)
        start(1)
        for c in range(QKV_WIDTH // step):
            at = slice(c * step, (c + 1) * step)
            total = mm(n0[...], q0[:, at], (0, 0)) + mm(n1[...], q1[:, at], (0, 0))
            qkv_sum[:, at] = total.astype(bf16)
        start(2)
        for i in range(len(spots)):
            for k in (0, 1, 2):
                for c in copies(i, k):
                    c.wait()

    def once(v):
        return pl.BlockSpec(v.shape, lambda i, t: (0, 0))

    tokens = pre_rel.shape[0]
    out = pl.pallas_call(
        kernel,
        out_shape=[jax.ShapeDtypeStruct((size, width), bf16) for size in sizes],
        grid_spec=pltpu.PrefetchScalarGridSpec(
            num_scalar_prefetch=1,
            grid=(1,),
            in_specs=[once(v) for v in (*norm_rows, *qkv_back)]
            + [pl.BlockSpec((tokens, 2 * side_rows), lambda i, t: (0, 0))]
            + [once(v) for v in (back_prefix_kv, other_side, grad_output)],
            out_specs=[pl.BlockSpec(memory_space=pltpu.HBM)] * n,
            scratch_shapes=[
                pltpu.VMEM((side_rows, QKV_WIDTH), bf16),
                pltpu.VMEM((2 * side_rows, pre_cols), bf16),
                pltpu.SemaphoreType.DMA((len(spots), 4)),
            ],
        ),
        compiler_params=pltpu.CompilerParams(vmem_limit_bytes=22 * MIB),
        cost_estimate=cost("disassemble"),
        name="disassemble",
    )(table, *norm_rows, *qkv_back, pre_rel, back_prefix_kv, other_side, grad_output)
    return out


def norm_by_core(ring, rows, gains, size):
    core = (lax.axis_index("wide") % 2).reshape(1)
    tokens, dim = rows.shape
    step = 128

    def kernel(core_ref, rows_ref, gains_ref, out_ref):
        v = rows_ref[...].astype(f32)
        normed = rms_norm(v, gains_ref[0]).astype(bf16)
        for swapped in (0, 1):

            @pl.when(core_ref[0] == swapped)
            def _(swapped=swapped):
                for chip in range(ring.chips):
                    for side in (0, 1):
                        at = (2 * chip + (side ^ swapped)) * size
                        to = side * (dim // 2) + chip * size
                        out_ref[:, to : to + size] = normed[:, at : at + size]

    return pl.pallas_call(
        kernel,
        out_shape=jax.ShapeDtypeStruct((tokens, dim), bf16),
        grid_spec=pltpu.PrefetchScalarGridSpec(
            num_scalar_prefetch=1,
            grid=(tokens // step,),
            in_specs=[
                pl.BlockSpec((step, dim), lambda i, t: (i, 0)),
                pl.BlockSpec((1, dim), lambda i, t: (0, 0)),
            ],
            out_specs=pl.BlockSpec((step, dim), lambda i, t: (i, 0)),
        ),
        compiler_params=pltpu.CompilerParams(vmem_limit_bytes=12 * MIB),
        cost_estimate=cost("norm_by_core"),
        name="norm_by_core",
    )(core, rows, gains)


def gelu_parts(v):
    c = math.sqrt(2.0 / math.pi)
    square = v * v
    t = jnp.tanh(c * v * (1.0 + 0.044715 * square))
    half = 0.5 * (1.0 + t)
    slope = half + 0.5 * v * (1.0 - t * t) * c * (1.0 + 3.0 * 0.044715 * square)
    return v * half, slope


def load_block(refs, buf, sems, k):
    at, made = 0, []
    for j, r in enumerate(refs):
        size = r.shape[1]
        made.append(pltpu.make_async_copy(r, buf.at[:, pl.ds(at, size), :], sems.at[k, j]))
        at += size
    return made


def ff_forward(norm_two, blocks, before):
    nb = len(blocks)
    flat = [a for blk in blocks for a in blk]
    tokens, dim = norm_two.shape
    units = sum(a.shape[1] for a in blocks[0])
    half = tokens // 2
    has_before = before is not None

    def kernel(norm_ref, *refs):
        refs = list(refs)
        ins = [[refs.pop(0) for _ in blk] for blk in blocks]
        if has_before:
            own_in, oth_in = refs.pop(0), refs.pop(0)
        gate_out, lin_out, hid_out, own_out, oth_out, buf, total, sems = refs
        i = pl.program_id(0)

        @pl.when(i == 0)
        def _():
            for k in range(nb):
                for c in load_block(ins[k], buf.at[k], sems, k):
                    c.start()
            if has_before:
                total[:half] = own_in[...]
                total[half:] = oth_in[...]
            else:
                total[...] = jnp.zeros_like(total)

        for k in range(nb):

            @pl.when(i == k)
            def _(k=k):
                for c in load_block(ins[k], buf.at[k], sems, k):
                    c.wait()

        w = buf.at[i]
        if units % 128 == 0:
            both = mm(norm_ref[...], w[:2].reshape(2 * units, dim), (1, 1))
            gate, linear = both[:, :units], both[:, units:]
        else:
            gate, linear = (mm(norm_ref[...], w[j], (1, 1)) for j in (0, 1))
        gate_out[0] = gate
        lin_out[0] = linear
        hidden = (gelu_parts(gate)[0] * linear).astype(bf16)
        hid_out[0] = hidden
        total[...] += mm(hidden, w[2], (1, 0))

        @pl.when(i == nb - 1)
        def _():
            own_out[...] = total[:half]
            oth_out[...] = total[half:]

    once = pl.BlockSpec((tokens, dim), lambda i: (0, 0))
    row = pl.BlockSpec((half, dim), lambda i: (0, 0))
    step = pl.BlockSpec((1, tokens, units), lambda i: (i, 0, 0))
    any_space = pl.BlockSpec(memory_space=pl.ANY)
    return pl.pallas_call(
        kernel,
        out_shape=[
            jax.ShapeDtypeStruct((nb, tokens, units), f32),
            jax.ShapeDtypeStruct((nb, tokens, units), f32),
            jax.ShapeDtypeStruct((nb, tokens, units), bf16),
            jax.ShapeDtypeStruct((half, dim), f32),
            jax.ShapeDtypeStruct((half, dim), f32),
        ],
        grid=(nb,),
        in_specs=[once] + [any_space] * len(flat) + [row, row] * has_before,
        out_specs=[step, step, step, row, row],
        scratch_shapes=[
            pltpu.VMEM((nb, 3, units, dim), bf16),
            pltpu.VMEM((tokens, dim), f32),
            pltpu.SemaphoreType.DMA((nb, 2)),
        ],
        compiler_params=pltpu.CompilerParams(vmem_limit_bytes=22 * MIB),
        cost_estimate=cost("ff_forward"),
        name="ff_forward",
    )(norm_two, *flat, *(before or ()))


def ff_backward(norm_two, branch_two, blocks, sends, kept, picks, before):
    nb = len(blocks)
    flat = [a for blk in blocks for a in blk]
    gate_all, lin_all, hid_all = kept
    tokens, dim = norm_two.shape
    units = sum(a.shape[1] for a in blocks[0])
    half = tokens // 2
    has_before = before is not None
    first, stride = picks

    def kernel(norm_ref, branch_ref, gate_ref, lin_ref, hid_ref, *refs):
        refs = list(refs)
        ins = [[refs.pop(0) for _ in blk] for blk in blocks]
        if has_before:
            own_in, oth_in = refs.pop(0), refs.pop(0)
        outs = [[refs.pop(0)] for _ in blocks]
        for keys in sends:
            ref = refs.pop(0)
            for spot, k in enumerate(keys):
                outs[k].append(ref.at[spot])
        own_out, oth_out, buf, grads, total, sems, out_sems = refs
        i = pl.program_id(0)

        def stores(k):
            at, made = 0, []
            for j, r in enumerate(outs[k]):
                size = r.shape[1]
                made.append(pltpu.make_async_copy(grads.at[k, :, pl.ds(at, size), :], r, out_sems.at[k, j]))
                at += size
            return made

        @pl.when(i == 0)
        def _():
            for k in range(nb):
                for c in load_block(ins[k], buf.at[k], sems, k):
                    c.start()
            if has_before:
                total[:half] = own_in[...]
                total[half:] = oth_in[...]
            else:
                total[...] = jnp.zeros_like(total)

        for k in range(nb):

            @pl.when(i == k)
            def _(k=k):
                for c in load_block(ins[k], buf.at[k], sems, k):
                    c.wait()

        w, g = buf.at[i], grads.at[i]
        back_hidden = mm(branch_ref[...], w[2], (1, 1))
        value, slope = gelu_parts(gate_ref[0])
        back_gate = (back_hidden * lin_ref[0] * slope).astype(bf16)
        back_linear = (back_hidden * value).astype(bf16)
        if units % 128 == 0:
            both = jnp.concatenate([back_gate, back_linear], 1)
            g[:2] = mm(both, norm_ref[...], (0, 0), bf16).reshape(2, units, dim)
            total[...] += mm(both, w[:2].reshape(2 * units, dim), (1, 0))
        else:
            for j, back in enumerate((back_gate, back_linear)):
                g[j] = mm(back, norm_ref[...], (0, 0), bf16)
                total[...] += mm(back, w[j], (1, 0))
        g[2] = mm(hid_ref[0], branch_ref[...], (0, 0), bf16)

        for k in range(nb):

            @pl.when(i == k)
            def _(k=k):
                for c in stores(k):
                    c.start()

        @pl.when(i == nb - 1)
        def _():
            own_out[...] = total[:half]
            oth_out[...] = total[half:]
            for k in range(nb):
                for c in stores(k):
                    c.wait()

    once = pl.BlockSpec((tokens, dim), lambda i: (0, 0))
    row = pl.BlockSpec((half, dim), lambda i: (0, 0))
    step = pl.BlockSpec((1, tokens, units), lambda i: (first + stride * i, 0, 0))
    any_space = pl.BlockSpec(memory_space=pl.ANY)
    hbm = pl.BlockSpec(memory_space=pltpu.HBM)
    made = pl.pallas_call(
        kernel,
        out_shape=[
            jax.ShapeDtypeStruct((3, units // (2 if any(k in x for x in sends) else 1), dim), bf16)
            for k in range(nb)
        ]
        + [jax.ShapeDtypeStruct((len(x), 3, units // 2, dim), bf16) for x in sends]
        + [jax.ShapeDtypeStruct((half, dim), f32)] * 2,
        grid=(nb,),
        in_specs=[once, once, step, step, step] + [any_space] * len(flat) + [row, row] * has_before,
        out_specs=[hbm] * (nb + len(sends)) + [row, row],
        scratch_shapes=[
            pltpu.VMEM((nb, 3, units, dim), bf16),
            pltpu.VMEM((nb, 3, units, dim), bf16),
            pltpu.VMEM((tokens, dim), f32),
            pltpu.SemaphoreType.DMA((nb, 2)),
            pltpu.SemaphoreType.DMA((nb, 2)),
        ],
        compiler_params=pltpu.CompilerParams(vmem_limit_bytes=36 * MIB),
        cost_estimate=cost("ff_backward"),
        name="ff_backward",
    )(norm_two, branch_two, gate_all, lin_all, hid_all, *flat, *(before or ()))
    made = list(made)
    return made[:nb], made[nb:-2], made[-2:]


def attention(action_qkv, prefix_kv, allowed, first, heads, before):
    tokens, keys = action_qkv.shape[0], allowed.shape[0]
    n_pre = prefix_kv.shape[0]

    def kernel(q_ref, kv_ref, pre_ref, allowed_ref, *refs):
        out_ref, k_all, v_turned = refs[-3:]
        h = pl.program_id(0)

        @pl.when(h == 0)
        def _():
            k_all[:n_pre] = pre_ref[:, :HEAD_DIM]
            k_all[n_pre:] = kv_ref[:, :HEAD_DIM]
            v_turned[:, :n_pre] = pre_ref[:, HEAD_DIM:].T
            v_turned[:, n_pre:] = kv_ref[:, HEAD_DIM:].T
            if before:
                out_ref[:, : first * HEAD_DIM] = refs[0][...]

        scores = mm(k_all[...], q_ref[...], (1, 1)) * SCORE_SCALE
        scores = jnp.where(allowed_ref[...] != 0, scores, NEGATIVE)
        exp_scores = jnp.exp(scores - jnp.max(scores, axis=0, keepdims=True))
        soft = exp_scores / jnp.sum(exp_scores, axis=0, keepdims=True)
        at = pl.ds(pl.multiple_of((first + h) * HEAD_DIM, HEAD_DIM), HEAD_DIM)
        out_ref[:, at] = mm(v_turned[...], soft.astype(bf16), (1, 0)).T.astype(bf16)

    width = (first + heads) * HEAD_DIM
    return pl.pallas_call(
        kernel,
        out_shape=jax.ShapeDtypeStruct((tokens, width), bf16),
        grid=(heads,),
        in_specs=[
            pl.BlockSpec((tokens, HEAD_DIM), lambda h: (0, first + h)),
            pl.BlockSpec((tokens, 2 * HEAD_DIM), lambda h: (0, HEADS // 2)),
            pl.BlockSpec((n_pre, 2 * HEAD_DIM), lambda h: (0, 0)),
            pl.BlockSpec((keys, tokens), lambda h: (0, 0)),
        ]
        + [pl.BlockSpec(v.shape, lambda h: (0, 0)) for v in before],
        out_specs=pl.BlockSpec((tokens, width), lambda h: (0, 0)),
        scratch_shapes=[pltpu.VMEM((keys, HEAD_DIM), bf16), pltpu.VMEM((HEAD_DIM, keys), bf16)],
        compiler_params=pltpu.CompilerParams(vmem_limit_bytes=20 * MIB),
        cost_estimate=cost("attention"),
        name="attention",
    )(action_qkv, action_qkv, prefix_kv, allowed, *before)


def attention_back(action_qkv, prefix_kv, allowed, back_mixed, first, heads, before):
    tokens, keys = action_qkv.shape[0], allowed.shape[0]
    n_pre = prefix_kv.shape[0]
    last = first + heads == HEADS
    n_before = len(before)

    def kernel(q_ref, kv_ref, pre_ref, allowed_ref, back_ref, *refs):
        before_refs, refs = refs[:n_before], refs[n_before:]
        if last:
            qkv_out, pre_out, k_sum, v_sum, k_all, v_all, k_turned = refs
        else:
            qkv_out, k_sum, v_sum, k_all, v_all, k_turned = refs
        h = pl.program_id(0)

        @pl.when(h == 0)
        def _():
            k_all[:n_pre] = pre_ref[:, :HEAD_DIM]
            k_all[n_pre:] = kv_ref[:, :HEAD_DIM]
            v_all[:n_pre] = pre_ref[:, HEAD_DIM:]
            v_all[n_pre:] = kv_ref[:, HEAD_DIM:]
            k_turned[...] = k_all[...].T
            if n_before:
                qkv_out[:, : first * HEAD_DIM] = before_refs[0][...]
                k_sum[...] = before_refs[1][...]
                v_sum[...] = before_refs[2][...]
            else:
                k_sum[...] = jnp.zeros_like(k_sum)
                v_sum[...] = jnp.zeros_like(v_sum)

        query, back = q_ref[...], back_ref[...]
        scores = mm(k_all[...], query, (1, 1)) * SCORE_SCALE
        scores = jnp.where(allowed_ref[...] != 0, scores, NEGATIVE)
        exp_scores = jnp.exp(scores - jnp.max(scores, axis=0, keepdims=True))
        soft = exp_scores / jnp.sum(exp_scores, axis=0, keepdims=True)
        v_sum[...] += mm(soft.astype(bf16), back, (1, 0))
        back_soft = mm(v_all[...], back, (1, 1))
        mean = jnp.sum(soft * back_soft, axis=0, keepdims=True)
        back_scores = (soft * (back_soft - mean)).astype(bf16)
        k_sum[...] += mm(back_scores, query, (1, 0))
        turned = mm(k_turned[...], back_scores, (1, 0)) * SCORE_SCALE
        at = pl.ds(pl.multiple_of((first + h) * HEAD_DIM, HEAD_DIM), HEAD_DIM)
        qkv_out[:, at] = turned.T.astype(bf16)

        if last:

            @pl.when(h == heads - 1)
            def _():
                pre_out[:, :HEAD_DIM] = (k_sum[:n_pre] * SCORE_SCALE).astype(bf16)
                pre_out[:, HEAD_DIM:] = v_sum[:n_pre].astype(bf16)
                keys_out = (k_sum[n_pre:] * SCORE_SCALE).astype(bf16)
                qkv_out[:, QUERY_WIDTH : QUERY_WIDTH + HEAD_DIM] = keys_out
                qkv_out[:, QUERY_WIDTH + HEAD_DIM :] = v_sum[n_pre:].astype(bf16)

    def once(shape):
        return pl.BlockSpec(shape, lambda h: (0, 0))

    sums = jax.ShapeDtypeStruct((keys, HEAD_DIM), f32)
    if last:
        out_shapes = [
            jax.ShapeDtypeStruct((tokens, QKV_WIDTH), bf16),
            jax.ShapeDtypeStruct((n_pre, 2 * HEAD_DIM), bf16),
        ]
        kept = [pltpu.VMEM(sums.shape, f32)] * 2
    else:
        out_shapes = [jax.ShapeDtypeStruct((tokens, heads * HEAD_DIM), bf16), sums, sums]
        kept = []
    return pl.pallas_call(
        kernel,
        out_shape=out_shapes,
        grid=(heads,),
        in_specs=[
            pl.BlockSpec((tokens, HEAD_DIM), lambda h: (0, first + h)),
            pl.BlockSpec((tokens, 2 * HEAD_DIM), lambda h: (0, HEADS // 2)),
            once((n_pre, 2 * HEAD_DIM)),
            once((keys, tokens)),
            pl.BlockSpec((tokens, HEAD_DIM), lambda h: (0, first + h)),
        ]
        + [once(v.shape) for v in before],
        out_specs=[once(o.shape) for o in out_shapes],
        scratch_shapes=kept
        + [
            pltpu.VMEM((keys, HEAD_DIM), bf16),
            pltpu.VMEM((keys, HEAD_DIM), bf16),
            pltpu.VMEM((HEAD_DIM, keys), bf16),
        ],
        compiler_params=pltpu.CompilerParams(vmem_limit_bytes=22 * MIB),
        cost_estimate=cost("attention_back"),
        name="attention_back",
    )(action_qkv, action_qkv, prefix_kv, allowed, back_mixed, *before)


def mid_back(residual, back_final, back_own, back_oth, gain_row, out_weight):
    tokens, dim = residual.shape

    def kernel(res_ref, fin_ref, own_ref, oth_ref, gain_ref, weight_ref, attn_out, mixed_out, gain_out):
        v = res_ref[...]
        s = lax.rsqrt(jnp.mean(v * v, axis=-1, keepdims=True) + NORM_EPSILON)
        normed = v * s
        back = own_ref[...] + oth_ref[...]
        gain_out[...] = jnp.sum(back * normed, axis=0, keepdims=True)
        scaled = back * (1.0 + gain_ref[...])
        mean = jnp.mean(scaled * normed, axis=-1, keepdims=True)
        attn = (fin_ref[...] + s * (scaled - normed * mean)).astype(bf16)
        attn_out[...] = attn
        mixed_out[...] = mm(attn, weight_ref[...], (1, 0), bf16)

    return pl.pallas_call(
        kernel,
        out_shape=[
            jax.ShapeDtypeStruct((tokens, dim), bf16),
            jax.ShapeDtypeStruct((tokens, QUERY_WIDTH), bf16),
            jax.ShapeDtypeStruct((1, dim), f32),
        ],
        compiler_params=pltpu.CompilerParams(vmem_limit_bytes=18 * MIB),
        cost_estimate=cost("mid_back"),
        name="mid_back",
    )(residual, back_final, back_own, back_oth, gain_row, out_weight)


def readout_loss(residual, branch_own, branch_oth, gain_row, readout, target, valid):
    tokens, dim = residual.shape
    act = readout.shape[0]

    def full(a, b, contract):
        return lax.dot_general(
            a, b, (((contract[0],), (contract[1],)), ((), ())),
            precision=HIGHEST, preferred_element_type=f32,
        )

    def kernel(res_ref, own_ref, oth_ref, gain_ref, read_ref, target_ref, valid_ref, final_out, branch_out, rows_out):
        v = res_ref[...] + own_ref[...] + oth_ref[...]
        s = lax.rsqrt(jnp.mean(v * v, axis=-1, keepdims=True) + NORM_EPSILON)
        normed = v * s
        scale = 1.0 + gain_ref[...]
        final = normed * scale
        valid_rows = valid_ref[...].astype(f32)
        error = full(read_ref[...], final, (1, 1)) - target_ref[...]
        counted = valid_rows * error
        back = 2.0 * counted
        rows_out[:act] = full(back, final, (1, 0))
        back_norm = full(back.T, read_ref[...], (1, 0))
        rows_out[act : act + 1] = jnp.sum(back_norm * normed, axis=0, keepdims=True)
        loss = jnp.sum(jnp.sum(counted * error, axis=0, keepdims=True), axis=1, keepdims=True)
        count = jnp.sum(jnp.sum(valid_rows, axis=0, keepdims=True), axis=1, keepdims=True)
        rows_out[act + 1 : act + 2] = jnp.broadcast_to(loss, (1, dim))
        rows_out[act + 2 : act + 3] = jnp.broadcast_to(count, (1, dim))
        scaled = back_norm * scale
        mean = jnp.mean(scaled * normed, axis=-1, keepdims=True)
        final_back = s * (scaled - normed * mean)
        final_out[...] = final_back
        branch_out[...] = final_back.astype(bf16)

    return pl.pallas_call(
        kernel,
        out_shape=[
            jax.ShapeDtypeStruct((tokens, dim), f32),
            jax.ShapeDtypeStruct((tokens, dim), bf16),
            jax.ShapeDtypeStruct((act + 3, dim), f32),
        ],
        compiler_params=pltpu.CompilerParams(vmem_limit_bytes=20 * MIB),
        cost_estimate=cost("readout_loss"),
        name="readout_loss",
    )(residual, branch_own, branch_oth, gain_row, readout, target, valid)


def on_device(
    ring,
    prefix_in,
    action_in,
    target,
    valid_mask,
    prefix_ids,
    action_ids,
    action_blocks,
    learning_rate,
    prefix_weight,
    attention_weight,
    feedforward_weight,
    prefix_gains,
    action_gains,
    readout_weight,
    prefix_weight_moment,
    attention_weight_moment,
    feedforward_weight_moment,
    prefix_gains_moment,
    action_gains_moment,
    readout_weight_moment,
    prefix_weight_average,
    attention_weight_average,
    feedforward_weight_average,
    prefix_gains_average,
    action_gains_average,
    readout_weight_average,
):
    core = lax.axis_index("wide") % 2
    rows_a, width_a = attention_weight.shape
    width_p = 2 * prefix_weight.shape[1]
    rows_p = prefix_weight.shape[0]
    n_right, n_left = ring.n_right, ring.n_left
    order, swap = Order(), ring.to_core

    def by_core(v, size):
        cut = v.reshape(v.shape[0], ring.chips, 2, size)
        cut = [cut[:, :, c].reshape(v.shape[0], ring.chips * size) for c in (0, 1)]
        return jnp.where(core == 0, cut[0], cut[1]), jnp.where(core == 0, cut[1], cut[0])

    def in_order(v, size):
        cut = v.reshape(2, ring.chips, size)
        return jnp.where(core == 0, cut, cut[::-1]).transpose(1, 0, 2).reshape(-1)

    def halves_of(v, axis):
        half = v.shape[axis] // 2
        if half % 16:
            return jnp.split(v, 2, axis)
        me = lax.axis_index("batch")
        return [lax.dynamic_slice_in_dim(v, at * half, half, axis) for at in (me, 1 - me)]

    prefix_bf = prefix_weight.astype(bf16)
    packed = jnp.concatenate(
        [attention_weight.astype(bf16), prefix_bf[:rows_a], prefix_bf[rows_a:]], axis=1
    )
    sides = [("right", d) for d in range(n_right)] + [("left", d) for d in range(n_left)]
    packed_halves = order(*halves_of(packed, 0))
    att = Gathering(ring, order, packed_halves, 0, True)
    att.start("right")
    att.start("left")
    ff_halves = order(*halves_of(jnp.transpose(feedforward_weight, (1, 0, 2)).astype(bf16), 1))
    ff = Gathering(ring, order, ff_halves, 1, False)
    side_of = {"R": "right", "L": "left"}

    def serve(step):
        for word in PLAN[step]:
            chain, what = {"a": att, "f": ff}[word[0]], word[1]
            if what == ">":
                chain.start(side_of[word[2]])
            elif what in side_of:
                chain.land(side_of[what])
            else:
                key = (side_of[word[2]], int(word[3]))
                (chain.cross if what == "X" else chain.settle)(key)

    ff.whole = order(ff.whole)
    own_parts = packed_halves if att.can else (packed,)
    prefix_rows = order(prefix_in[0])
    if rows_p % 128 == 0:
        pre_rel = order(norm_by_core(ring, prefix_rows, prefix_gains, rows_p))
    else:
        normed = rms_norm(prefix_rows.astype(f32), prefix_gains[0]).astype(bf16)
        pre_rel = order(jnp.concatenate(by_core(normed, rows_p), 1))
    serve("norm")
    action_rows = order(action_in[0]).astype(f32)
    action_norm = rms_norm(action_rows, action_gains[0]).astype(bf16)
    norm_mine, norm_other = order(*by_core(action_norm, rows_a))
    serve("action")
    norm_oth = order(swap(order(norm_other)))
    norm_rel = order(jnp.concatenate([norm_mine, norm_other], 1))
    serve("swapped")
    allowed = order(visible(prefix_ids[0], *order(action_ids[0], action_blocks[0])))
    serve("seen")
    while any(att.d[x] < att.count[x] for x in att.d):
        att.land("right", "left")
    att.settle(*[k for k in sides if len(att.blocks[k]) == 1])
    blocks = [own_parts] + [att.blocks[k] for k in sides]
    qkv_own, out_own, pre_own = order(*assemble(ring, blocks, rows_a, width_a))
    pre_oth, qkv_oth = swap(pre_own), swap(qkv_own)
    serve("assembled")

    prefix_kv = order(half_product(pre_rel, 0, order(pre_own), None))
    action_qkv = order(half_product(norm_rel, 0, order(qkv_own), None))
    serve("half")
    pre_oth, qkv_oth, out_own = order(pre_oth, qkv_oth, out_own)
    out_oth = swap(out_own)
    prefix_kv = order(half_product(pre_rel, 1, order(pre_oth), prefix_kv))
    action_qkv = order(half_product(norm_rel, 1, order(qkv_oth), action_qkv))
    serve("half2")
    out_own, out_oth = order(out_own, out_oth)
    out_weight = order(interleave(ring, out_own, out_oth, rows_a))
    serve("woven")
    action_qkv = order(action_qkv)
    part = order(attention(action_qkv, prefix_kv, allowed, 0, HEADS // 2, ()))
    serve("attended")
    part = order(part)
    mixed_heads = order(
        attention(action_qkv, prefix_kv, allowed, HEADS // 2, HEADS // 2, (part,))
    )
    mixed_oth = swap(mixed_heads)
    serve("attended2")
    mixed_heads = order(mixed_heads)
    residual = action_rows + mm(mixed_heads, out_weight, (1, 1))
    tokens = residual.shape[0]
    hidden_norm = rms_norm(residual, action_gains[1]).astype(bf16)
    residual, hidden_norm, mixed_oth = order(residual, hidden_norm, mixed_oth)
    norm_two = order(jnp.concatenate([hidden_norm, order(swap(hidden_norm))], 0))
    serve("normed")

    def weights(key):
        return (ff.whole,) if key[0] == "own" else ff.blocks[key]

    early = [("own", 0)] + [x for d in range(n_left - 1) for x in (("left", d), ("right", d))]
    late = [("right", n_left - 1), ("left", n_left - 1)]
    late += [("right", d) for d in range(n_left, n_right)]
    groups = [early, late]
    kept, branch = [], None
    for group in groups:
        for side, d in group:
            while side != "own" and ff.d[side] <= d:
                ff.land(side)
        ff.cross(*[k for k in group if k[0] != "own"])
        ff.settle(*[k for k in group if len(ff.blocks.get(k, ())) == 2])
        norm_two = order(norm_two)
        *values, own_rows, other_rows = ff_forward(norm_two, [weights(k) for k in group], branch)
        branch = order(own_rows, other_rows)
        kept.append(values)
        if group is early:
            serve("early")
    dim = action_rows.shape[1]
    branch_own, branch_oth = order(branch[0], swap(branch[1]))
    back_final, back_branch, small_rows = order(
        *readout_loss(
            residual,
            branch_own,
            branch_oth,
            action_gains[2:3],
            readout_weight.T,
            target[0].T,
            valid_mask[0].T,
        )
    )
    branch_two = order(jnp.concatenate([back_branch, swap(back_branch)], 0))
    act = readout_weight.shape[1]
    n_back = n_right + (n_left > 1)
    ff_sum = Summing(ring, order, 1, n_back)

    def way_back(key):
        side, d = key
        return ("right", ring.chips - 2 - d) if side == "left" and ring.chips - 2 - d < n_back else key

    own_key, back = ("own", 0), None
    att_sum = Summing(ring, order, 0, n_right)
    small_sum, swapped = None, {}

    def serve_back(step):
        nonlocal small_sum
        for word in PLAN[step]:
            chain, rest = (att_sum, word[1:]) if word[0] == "A" else (ff_sum, word)
            if word in ("q", "o"):
                if word in swapped:
                    swapped[word] = order(swapped[word])
            elif word == "Aown":
                while att_sum.d["left"] >= 0:
                    att_sum.step("left")
                att_sum.own(jnp.split(cut[0], 2, 0))
            elif rest in side_of:
                side = side_of[rest]
                if (side, chain.d[side]) in chain.parts:
                    chain.step(side)
            elif rest == "own":
                while ff_sum.d["left"] >= 0:
                    ff_sum.step("left")
                own_grads = [ff_sum.parts[own_key]]
                if ff.can:
                    own_grads.append(ff_sum.sends["own"].reshape(own_grads[0].shape))
                else:
                    own_grads = jnp.split(own_grads[0], 2, 1)
                ff_sum.own(own_grads)
            elif rest == "close":
                while ff_sum.d["right"] >= 0:
                    ff_sum.step("right")
                ff_sum.close()
            elif rest == "s":
                if small_sum is None:
                    small_sum = SmallSum(ring, order, small_rows)
                else:
                    small_sum.step()
            else:
                chain = att_sum if rest[1:] == "A" else ff_sum
                name = "all" if rest[1:] == "A" else rest[1:]
                (chain.cross if rest[0] == "x" else chain.ready)(name)

    for name, group, values in (("late", late, kept[1]), ("early", early, kept[0])):
        turned = [way_back(k) for k in group[::-1]]
        rights = sorted((k for k in turned if k[0] == "right"), key=lambda k: -k[1])
        if not ff.can:
            lists = {}
        elif name == "late":
            lists = {"first": rights[:1], "second": rights[1:2], "third": rights[2:]}
        else:
            lists = {"early": rights, "own": [own_key]}
        lists = {k: v for k, v in lists.items() if v}
        branch_two = order(branch_two)
        made, sent, back = ff_backward(
            norm_two,
            branch_two,
            [weights(k) for k in group[::-1]],
            [[turned.index(k) for k in keys] for keys in lists.values()],
            values,
            (len(group) - 1, -1),
            back,
        )
        flat = list(order(*back, *made, *sent))
        back, made, sent = flat[:2], flat[2 : 2 + len(turned)], flat[2 + len(turned) :]
        ff_sum.put(
            dict(zip(turned, made)),
            dict(zip(lists, sent)),
            {k: (n, i) for n, keys in lists.items() for i, k in enumerate(keys)},
        )
        if name == "late":
            serve_back("back_late")
    back_oth = swap(back[1])
    serve_back("back_early")
    back_own, back_oth = order(back[0], back_oth)
    back_attention, back_mixed, grad_gain_hidden = order(
        *mid_back(residual, back_final, back_own, back_oth, action_gains[1:2], out_weight)
    )
    serve_back("mid")
    back_mixed = order(back_mixed)
    part = order(
        *attention_back(action_qkv, prefix_kv, allowed, back_mixed, 0, HEADS // 2, ())
    )
    serve_back("back_a")
    attn_mine, attn_other = order(*by_core(order(back_attention), rows_a))
    attn_oth = swap(attn_other)
    serve_back("core")
    back_mixed, attn_oth, *part = order(back_mixed, attn_oth, *part)
    back_qkv, back_prefix_kv = order(
        *attention_back(action_qkv, prefix_kv, allowed, back_mixed, HEADS // 2, HEADS // 2, part)
    )
    swapped["q"] = swap(back_qkv)
    serve_back("back_b")

    swapped["o"] = swap(order(side_gradient(pre_rel, order(back_prefix_kv), 1)))
    serve_back("side")
    grad_output = order(pair_gradient((attn_mine, attn_oth), order(mixed_heads, mixed_oth)))
    serve_back("pair")
    cut = order(
        *disassemble(
            ring,
            att.can,
            (norm_mine, norm_oth),
            (back_qkv, order(swapped["q"])),
            pre_rel,
            back_prefix_kv,
            order(swapped["o"]),
            order(grad_output),
            rows_a,
        )
    )
    att_sum.put(
        dict(zip(sides, cut[1:])),
        {"all": cut[ring.chips]} if att.can else {},
        {("right", d): ("all", d) for d in range(n_right)} if att.can else {},
    )
    serve_back("cut")
    back_qkv, back_prefix_kv = order(back_qkv, back_prefix_kv)
    sums = order(
        gain_sums(back_qkv, norm_rel, qkv_own, qkv_oth),
        gain_sums(back_prefix_kv, pre_rel, pre_own, pre_oth),
    )
    grad_gain_action = in_order(sums[0][0], rows_a) / (1.0 + action_gains[0])
    grad_gain_prefix = in_order(sums[1][0], rows_p) / (1.0 + prefix_gains[0])
    late_rows = order(grad_gain_prefix.reshape(-1, dim), grad_gain_action[None], grad_gain_hidden)
    small_rows = [small_rows, *late_rows]
    serve_back("gains")
    serve_back("tail")
    while att_sum.d["right"] >= 0:
        att_sum.step("right")
    if small_sum is None:
        small_sum = SmallSum(ring, order, small_rows)
    while small_sum.step():
        pass
    ff_total = ff_sum.result()
    small = small_sum.total
    n_pre = grad_gain_prefix.shape[0] // dim
    count = small[act + 2, 0]
    loss_value = small[act + 1, 0] / count
    scale = 1.0 / count
    step_rate = learning_rate[0]
    third = order(
        *advance(
            feedforward_weight,
            feedforward_weight_moment,
            feedforward_weight_average,
            jnp.transpose(ff_total, (1, 0, 2)) * scale,
            step_rate,
        )
    )
    att_sum.close()
    packed_total = att_sum.result()
    first = advance(
        prefix_weight,
        prefix_weight_moment,
        prefix_weight_average,
        jnp.concatenate(
            [
                packed_total[:, width_a : width_a + width_p // 2],
                packed_total[:, width_a + width_p // 2 :],
            ],
            0,
        )
        * scale,
        step_rate,
    )
    second = advance(
        attention_weight,
        attention_weight_moment,
        attention_weight_average,
        packed_total[:, :width_a] * scale,
        step_rate,
    )
    fourth = advance(
        prefix_gains,
        prefix_gains_moment,
        prefix_gains_average,
        small[act + 3 : act + 3 + n_pre].reshape(1, -1) * scale,
        step_rate,
    )
    fifth = advance(
        action_gains,
        action_gains_moment,
        action_gains_average,
        jnp.concatenate([small[act + 3 + n_pre :], small[act : act + 1]], 0) * scale,
        step_rate,
    )
    sixth = advance(
        readout_weight,
        readout_weight_moment,
        readout_weight_average,
        small[:act].T * scale,
        step_rate,
    )
    loss_value = loss_value + order.token.astype(f32)
    return (loss_value,) + tuple(
        group[i]
        for i in range(3)
        for group in (first, second, third, fourth, fifth, sixth)
    )


def solution(mesh):
    rows = P(("batch", "wide"))
    wide = P("wide")
    whole = P()
    weights = (wide, wide, wide, whole, whole, whole)
    return jax.shard_map(
        functools.partial(on_device, Ring(mesh.shape["wide"])),
        mesh=mesh,
        in_specs=(rows,) * 7 + (whole,) + weights * 3,
        out_specs=(whole,) + weights * 3,
        check_vma=False,
    )
```
